128 devices in a mesh: dp: 16 (over y_lo, x, core), fsdp: 8 (over y_hi, z).
Axes of the slice: x: 4, y: 4 (y_hi: 2, y_lo: 2; y = y_hi * 2 + y_lo), z: 4, core: 2. Of those that a mesh axis runs over, the one named last changes fastest.
Arguments:
- layer_input: bfloat16 [64, 1024, 960], P('dp', 'fsdp'), may hold values from -6 to 6
- segments: int32 [64, 1024], P('dp'), may hold values from 0 to 6, as said below
- w_query: bfloat16 [960, 960], P('fsdp'), may hold values from -0.1875 to 0.1875
- w_key: bfloat16 [960, 320], P('fsdp'), may hold values from -0.1875 to 0.1875
- w_value: bfloat16 [960, 320], P('fsdp'), may hold values from -0.1875 to 0.1875
- w_output: bfloat16 [960, 960], P('fsdp'), may hold values from -0.75 to 0.75
- w_gate: bfloat16 [960, 2560], P('fsdp'), may hold values from -0.1875 to 0.1875
- w_up: bfloat16 [960, 2560], P('fsdp'), may hold values from -0.1875 to 0.1875
- w_down: bfloat16 [2560, 960], P('fsdp'), may hold values from -0.125 to 0.125
- gain_attn: bfloat16 [960], P('fsdp'), may hold values from 0.099609375 to 1.8984375
- gain_ffn: bfloat16 [960], P('fsdp'), may hold values from 0.099609375 to 1.8984375
- cotangent: bfloat16 [64, 1024, 960], P('dp', 'fsdp'), may hold values from -6 to 6
Outputs:
- out: bfloat16 [64, 1024, 960], P('dp', 'fsdp')
- grad_input: float32 [64, 1024, 960], P('dp', 'fsdp')
- grad_query: float32 [960, 960], P('fsdp')
- grad_key: float32 [960, 320], P('fsdp')
- grad_value: float32 [960, 320], P('fsdp')
- grad_output: float32 [960, 960], P('fsdp')
- grad_gate: float32 [960, 2560], P('fsdp')
- grad_up: float32 [960, 2560], P('fsdp')
- grad_down: float32 [2560, 960], P('fsdp')
- grad_gain_attn: float32 [960], P('fsdp')
- grad_gain_ffn: float32 [960], P('fsdp')
The draws below stay inside these ranges and needn't reach their ends.
Inputs may be any that keep to these rules, and one draw needn't show every extreme that they name: `segments`: segment numbers never fall along a sequence and start at 0; each run is one document or the cut-off part of one, whole documents being 200 to 2000 tokens long.
All inputs are finite; a program needn't handle non-finite values.
Results may differ from the reference program's by a relative error of at most 0.028.
Values may be sent and summed in bfloat16 or wider, within the bound.
No kernel may reach another device: no remote copies, remote signals or barrier semaphores. Data moves between devices by JAX's collectives and lax.ppermute only.
A program may use at most 320 MiB of HBM per device.

```python
import jax
import jax.numpy as jnp
from jax import lax

D = 960
H = 15
KVH = 5
HDIM = 64
FF = 2560
HD = 960
KVD = 320
LEN = 1024
BATCH = 64
DOC_MIN = 200
DOC_MAX = 2000


def draw_segments(key, part):
    key = jax.random.fold_in(key, 7)
    first_key, second_key, third_key = jax.random.split(key, 3)
    count = LEN // DOC_MIN + 2
    sizes = jax.random.randint(first_key, (BATCH, count), DOC_MIN, DOC_MAX + 1)
    offset = jax.random.randint(second_key, (BATCH, 1), 0, DOC_MIN)
    chosen = jax.random.randint(third_key, (), 0, BATCH)
    picked = (jnp.arange(BATCH, dtype=jnp.int32) == chosen)[:, None]
    sizes = jnp.where(picked, jnp.full_like(sizes, DOC_MIN), sizes)
    offset = jnp.where(picked, jnp.full_like(offset, DOC_MIN - 1), offset)
    ends = jnp.cumsum(sizes, axis=1) - offset
    index = jnp.arange(LEN, dtype=jnp.int32)
    return jnp.sum((ends[:, None, :] <= index[None, :, None]).astype(jnp.int32), axis=-1).astype(jnp.int32)


def block_levels(key, extent, cuts, least, top_value):
    loudness = 1.0
    for position, shards_of in cuts:
        draws = jax.random.uniform(jax.random.fold_in(jax.random.fold_in(key, 6), position), (shards_of,), jnp.float32, least / len(cuts), top_value / len(cuts))
        loudness = loudness * jnp.repeat(jnp.exp(draws), extent[position] // shards_of).reshape((-1,) + (1,) * (len(extent) - 1 - position))
    return loudness


def normal_values(own_key, dims, deviation, most, cuts=(), kind=jnp.bfloat16):
    values = deviation * jax.random.normal(own_key, dims, jnp.float32)
    if cuts:
        values = values * block_levels(own_key, dims, cuts, -0.22, 0.18)
    return jnp.clip(values, -most, most).astype(kind)


def setup_inputs(seed: int = 0) -> dict:
    key_of = jax.random.split(jax.random.key(seed), 13)
    return {
        "layer_input": normal_values(key_of[0], (BATCH, LEN, D), 1.0, 6.0, ((0, 16), (1, 8))),
        "segments": draw_segments(jax.random.fold_in(key_of[12], 71), 0),
        "w_query": normal_values(key_of[2], (D, HD), D ** -0.5, 0.1875, ((0, 8),)),
        "w_key": normal_values(key_of[3], (D, KVD), D ** -0.5, 0.1875, ((0, 8),)),
        "w_value": normal_values(key_of[4], (D, KVD), D ** -0.5, 0.1875, ((0, 8),)),
        "w_output": normal_values(key_of[5], (HD, D), (D // 16) ** -0.5, 0.75, ((0, 8),)),
        "w_gate": normal_values(key_of[6], (D, FF), D ** -0.5, 0.1875, ((0, 8),)),
        "w_up": normal_values(key_of[7], (D, FF), D ** -0.5, 0.1875, ((0, 8),)),
        "w_down": normal_values(key_of[8], (FF, D), FF ** -0.5, 0.125, ((0, 8),)),
        "gain_attn": jnp.clip(1.0 + 0.18 * jax.random.normal(key_of[9], (D,), jnp.float32), 0.099609375, 1.8984375).astype(jnp.bfloat16),
        "gain_ffn": jnp.clip(1.0 + 0.18 * jax.random.normal(key_of[10], (D,), jnp.float32), 0.099609375, 1.8984375).astype(jnp.bfloat16),
        "cotangent": normal_values(key_of[11], (BATCH, LEN, D), 1.0, 6.0, ((0, 16), (1, 8))),
    }


@jax.custom_vjp
def low(v):
    return lax.optimization_barrier(v.astype(jnp.bfloat16)).astype(jnp.float32)

@jax.custom_vjp
def low_back(v):
    return v

def low_keep(v):
    return (low(v), None)

def low_pass(kept, grad):
    return (grad,)

def back_keep(v):
    return (v, None)

def back_low(kept, grad):
    return (low(grad),)
low.defvjp(low_keep, low_pass)
low_back.defvjp(back_keep, back_low)
EPS = 1e-05
THETA = 100000.0

def doc_positions(seg):
    index = jnp.arange(seg.shape[0], dtype=jnp.int32)
    before = jnp.concatenate([seg[:1] - 1, seg[:-1]])
    starts = jnp.where(seg != before, index, jnp.zeros_like(index))
    return index - lax.cummax(starts, axis=0)

def rotate(values, pos):
    half = HDIM // 2
    freq = THETA ** (-(jnp.arange(half, dtype=jnp.float32) * 2.0) / HDIM)
    angle = pos.astype(jnp.float32)[:, None] * freq[None, :]
    cosine = jnp.cos(angle)[:, None, :]
    sine = jnp.sin(angle)[:, None, :]
    first = values[..., :half]
    second = values[..., half:]
    return jnp.concatenate([first * cosine - second * sine, second * cosine + first * sine], axis=-1)

def mult(a, b):
    return jnp.dot(a, b, precision=lax.Precision.HIGHEST)

def layer(xval, seg, w_query, w_key, w_value, w_output, w_gate, w_up, w_down, gain_attn, gain_ffn):
    length = xval.shape[0]
    group = H // KVH
    pos = doc_positions(seg)
    index = jnp.arange(length, dtype=jnp.int32)
    r1 = lax.rsqrt(lax.optimization_barrier(jnp.mean(xval * xval, axis=-1, keepdims=True)) + EPS)
    h1 = low(xval * r1 * gain_attn)
    query_pre = low_back(mult(h1, w_query)).reshape(length, H, HDIM)
    key_pre = low_back(mult(h1, w_key)).reshape(length, KVH, HDIM)
    values = low(low_back(mult(h1, w_value))).reshape(length, KVH, HDIM)
    query = low(rotate(query_pre, pos)).reshape(length, KVH, group, HDIM)
    keys = low(rotate(key_pre, pos))
    mask = (seg[:, None] == seg[None, :]) & (index[:, None] >= index[None, :])
    scores = low_back(jnp.einsum('rkgd,lkd->kgrl', query, keys, precision=lax.Precision.HIGHEST) * HDIM ** (-0.5))
    scores = jnp.where(mask[None, None], scores, -1e+30)
    top = lax.optimization_barrier(jnp.max(scores, axis=-1, keepdims=True))
    expo = jnp.exp(scores - top)
    probs = low(expo / lax.optimization_barrier(jnp.sum(expo, axis=-1, keepdims=True)))
    mixed = jnp.einsum('kgrl,lkd->rkgd', probs, values, precision=lax.Precision.HIGHEST).reshape(length, HD)
    mixed = low(low_back(mixed))
    x1 = xval + low_back(mult(mixed, w_output))
    r2 = lax.rsqrt(lax.optimization_barrier(jnp.mean(x1 * x1, axis=-1, keepdims=True)) + EPS)
    h2 = low(x1 * r2 * gain_ffn)
    gate = low_back(mult(h2, w_gate))
    upval = low_back(mult(h2, w_up))
    hidden = low(gate * jax.nn.sigmoid(gate) * upval)
    return x1 + low_back(mult(hidden, w_down))

def reference(layer_input, segments, w_query, w_key, w_value, w_output, w_gate, w_up, w_down, gain_attn, gain_ffn, cotangent):
    params = tuple((w.astype(jnp.float32) for w in (w_query, w_key, w_value, w_output, w_gate, w_up, w_down, gain_attn, gain_ffn)))

    def one(carry, item):
        xs, seg, grad_out = item

        def forward(xval, *weights):
            return layer(xval, seg, *weights)
        result, pull = jax.vjp(forward, xs.astype(jnp.float32), *params)
        grads = pull(grad_out.astype(jnp.float32))
        carry = tuple((c + g for c, g in zip(carry, grads[1:])))
        return (carry, (result.astype(jnp.bfloat16), grads[0]))
    init = tuple((jnp.zeros_like(p) for p in params))
    sums, (outs, grad_in) = lax.scan(one, init, (layer_input, segments, cotangent))
    return (outs, grad_in, sums[0], sums[1], sums[2], sums[3], sums[4], sums[5], sums[6], sums[7], sums[8])
```

```python
import functools

import jax
import jax.numpy as jnp
from jax import lax
from jax.experimental import pallas as pl
from jax.experimental.pallas import tpu as pltpu
from jax.sharding import PartitionSpec as P

D = 960
H = 15
KVH = 5
HDIM = 64
FF = 2560
KVD = 320
LEN = 1024
EPS = 1e-05
THETA = 100000.0
TOK = 512
ROWS = 120
NEG = -1e30
BF = jnp.bfloat16
F32 = jnp.float32
AXES = ("dp", "fsdp")


def coords(i):
    dp, fs = divmod(i, 8)
    ylo, rest = divmod(dp, 8)
    x, core = divmod(rest, 2)
    yhi, z = divmod(fs, 4)
    return ylo, x, core, yhi, z


def flat(ylo, x, core, yhi, z):
    return ((ylo * 4 + x) * 2 + core) * 8 + yhi * 4 + z


def perm(fn, keep=lambda *a: True):
    return [(i, flat(*fn(*coords(i)))) for i in range(128) if keep(*coords(i))]


Z1 = perm(lambda yl, x, c, yh, z: (yl, x, c, yh, z ^ 1))
Z2 = perm(lambda yl, x, c, yh, z: (yl, x, c, yh, 3 - z))
Y2 = perm(lambda yl, x, c, yh, z: (1 - yl, x, c, 1 - yh, z))
CC = perm(lambda yl, x, c, yh, z: (yl, x, 1 - c, yh, z))
Y2_OWN = perm(
    lambda yl, x, c, yh, z: (1 - yl, x, c, 1 - yh, z), lambda yl, x, c, yh, z: c == yh
)
Y2_BACK = perm(
    lambda yl, x, c, yh, z: (1 - yl, x, 1 - c, 1 - yh, z), lambda yl, x, c, yh, z: c != yh
)
BITS = {"z1": 1, "z2": 2, "y2": 4}
PERMS = {"z1": Z1, "z2": Z2, "y2": Y2}

CORE_OF = (0, 0, 1, 1, 1, 1, 0, 0)
RANK_OF = (0, 1, 0, 1, 2, 3, 2, 3)


def relay(r):
    pairs = []
    for i in range(128):
        yl, x, b, yh, z = coords(i)
        s = yh * 4 + z
        t = 4 * b + (RANK_OF[s] + r) % 4
        pairs.append((i, flat(yl, x, CORE_OF[s], t // 4, t % 4)))
    return pairs


def send(x, pairs):
    return lax.ppermute(x, AXES, pairs)


def gather_rows(part, order):
    cur, slots = part[None], [0]
    for name in order:
        got = send(cur, PERMS[name])
        cur = jnp.concatenate([cur, got], axis=0)
        slots = slots + [s | BITS[name] for s in slots]
    if slots != list(range(len(slots))):
        cur = jnp.concatenate([cur[slots.index(s)][None] for s in range(len(slots))], axis=0)
    return cur


def scatter_step(cur, slots, name):
    bit = BITS[name]
    out = [k for k, s in enumerate(slots) if s & bit]
    keep = [k for k, s in enumerate(slots) if not s & bit]
    got = send(pick(cur, out), PERMS[name])
    total = pick(cur, keep).astype(F32) + got.astype(F32)
    return total.astype(BF), [slots[k] for k in keep]


def pick(cur, index):
    first, count = index[0], len(index)
    if index == list(range(first, first + count)):
        return cur[first : first + count]
    return jnp.concatenate([cur[k][None] for k in index], axis=0)


def scatter_rows(cur, order):
    slots = list(range(cur.shape[0]))
    for name in order:
        cur, slots = scatter_step(cur, slots, name)
    return cur[0]


def nn(a, b):
    return lax.dot_general(a, b, (((1,), (0,)), ((), ())), preferred_element_type=F32)


def nt(a, b):
    return lax.dot_general(a, b, (((1,), (1,)), ((), ())), preferred_element_type=F32)


def tn(a, b):
    return lax.dot_general(a, b, (((0,), (0,)), ((), ())), preferred_element_type=F32)


def cost(flops, nbytes, trans=0):
    return pl.CostEstimate(flops=int(flops), bytes_accessed=int(nbytes), transcendentals=int(trans))


VMEM = pl.BlockSpec(memory_space=pltpu.VMEM)
SMEM = pl.BlockSpec(memory_space=pltpu.SMEM)


def call(kernel, outs, ins, flops, scratch=(), trans=0):
    nbytes = sum(a.size * a.dtype.itemsize for a in ins) + sum(
        a.size * a.dtype.itemsize for a in outs
    )
    return pl.pallas_call(
        kernel,
        out_shape=outs,
        in_specs=[SMEM] + [VMEM] * (len(ins) - 1),
        out_specs=[VMEM] * len(outs),
        scratch_shapes=list(scratch),
        cost_estimate=cost(flops, nbytes, trans),
        compiler_params=pltpu.CompilerParams(vmem_limit_bytes=48 * 1024 * 1024),
    )(*ins)


def sds(shape, dtype):
    return jax.ShapeDtypeStruct(shape, dtype)


def to_slots(scalars, scratch, value):
    for s in range(8):
        at = pl.multiple_of(scalars[s] * ROWS, 8)
        scratch[pl.ds(at, ROWS), :] = value[s * ROWS : (s + 1) * ROWS]
    return scratch[...]


def from_slots(scalars, scratch, value):
    scratch[...] = value
    return jnp.concatenate(
        [scratch[pl.ds(pl.multiple_of(scalars[s] * ROWS, 8), ROWS), :] for s in range(8)], axis=0
    )


def assemble_kernel(scalars, r0, r1, r2, r3, out):
    for r, ref in enumerate((r0, r1, r2, r3)):
        k = lax.rem(scalars[12] - r + 4, 4)
        out[:, pl.ds(pl.multiple_of(k * 128, 128), 128)] = ref[...]


def assemble(scalars, got):
    return call(assemble_kernel, [sds((D, TOK), BF)], [scalars, *got], 0)[0]


def store_chunks(scalars, out, value):
    for k in range(4):
        out[lax.rem(scalars[12] - k + 4, 4)] = value[:, k * 128 : (k + 1) * 128]


def finish_kernel(scalars, r0, r1, r2, r3, out):
    for r, ref in enumerate((r0, r1, r2, r3)):
        out[lax.rem(scalars[17] + r, 4)] = ref[...].astype(out.dtype)


def finish(scalars, got, dtype):
    return call(finish_kernel, [sds((4, D, 128), dtype)], [scalars, *got], 0)[0]


def rope(value, cosine, sine):
    parts = []
    for h in range(value.shape[0] // HDIM):
        first = value[h * HDIM : h * HDIM + 32]
        second = value[h * HDIM + 32 : (h + 1) * HDIM]
        parts += [first * cosine - second * sine, second * cosine + first * sine]
    return jnp.concatenate(parts, axis=0)


def pre_kernel(scalars, x, wq0, wq1, wk, wv, cos, sin, q_out, kv_out, h_out, scr):
    xv = x[...].astype(F32)
    r1 = lax.rsqrt(jnp.mean(xv * xv, axis=0, keepdims=True) + EPS)
    xn = to_slots(scalars, scr, xv * r1)
    h1 = (xn * wk[:, 320:321].astype(F32)).astype(BF)
    h_out[...] = h1
    cosine, sine = cos[...], sin[...]
    q0 = rope(tn(wq0[...], h1), cosine, sine)
    q_out[0:512, :] = (q0.astype(BF).astype(F32) * 0.125).astype(BF)
    q1 = rope(tn(wq1[...], h1)[:448], cosine, sine)
    q_out[512:960, :] = (q1.astype(BF).astype(F32) * 0.125).astype(BF)
    kv_out[0:320, :] = rope(tn(wk[...], h1)[:320], cosine, sine).astype(BF)
    kv_out[320:640, :] = tn(wv[...], h1)[:320].astype(BF)


def place_keys(scalars, out, own, other):
    for j in range(2):
        lo = j * 256
        out[:, pl.ds(pl.multiple_of(scalars[13 + j] * 256, 256), 256)] = own[:, lo : lo + 256]
        out[:, pl.ds(pl.multiple_of(scalars[15 + j] * 256, 256), 256)] = other[:, lo : lo + 256]


def allowed(first, index, lo, keys):
    key = lax.broadcasted_iota(jnp.int32, (keys, 256), 0)
    return (key >= first[:, lo : lo + 256]) & (key <= index[:, lo : lo + 256])


def attn_kernel(scalars, q, ko, kp, vo, vp, first, index, o_out, lse_out, kscr, vscr):
    place_keys(scalars, kscr, ko, kp)
    place_keys(scalars, vscr, vo, vp)
    for j, keys in enumerate((512, 1024)):
        lo = j * 256
        ok = allowed(first[...], index[...], lo, keys)
        for h in range(3):
            s = tn(kscr[:, :keys], q[h * HDIM : (h + 1) * HDIM, lo : lo + 256])
            s = jnp.where(ok, s, NEG)
            top = jnp.max(s, axis=0, keepdims=True)
            p = jnp.exp(s - top)
            total = jnp.sum(p, axis=0, keepdims=True)
            o = nn(vscr[:, :keys], p.astype(BF)) / total
            o_out[h * HDIM : (h + 1) * HDIM, lo : lo + 256] = o.astype(BF)
            lse_out[0, h : h + 1, lo : lo + 256] = top + jnp.log(total)


def group_spec(rows):
    return pl.BlockSpec((rows, TOK), lambda g, *_: (g, 0))


def value_spec():
    return pl.BlockSpec((HDIM, TOK), lambda g, *_: (KVH + g, 0))


def row_spec():
    return pl.BlockSpec((1, TOK), lambda g, *_: (0, 0))


def attention(scalars, q, kv_own, kv_other, first, index):
    return pl.pallas_call(
        attn_kernel,
        out_shape=[sds((D, TOK), BF), sds((KVH, 8, TOK), F32)],
        grid=(KVH,),
        in_specs=[
            SMEM,
            group_spec(192),
            group_spec(HDIM),
            group_spec(HDIM),
            value_spec(),
            value_spec(),
            row_spec(),
            row_spec(),
        ],
        out_specs=[group_spec(192), pl.BlockSpec((1, 8, TOK), lambda g: (g, 0, 0))],
        scratch_shapes=[pltpu.VMEM((HDIM, LEN), BF), pltpu.VMEM((HDIM, LEN), BF)],
        cost_estimate=cost(12e9, 6e6, 6e6),
        compiler_params=pltpu.CompilerParams(vmem_limit_bytes=48 * 1024 * 1024),
    )(scalars, q, kv_own, kv_other, kv_own, kv_other, first, index)


def attn_back_kernel(
    scalars, q, ko, kp, vo, vp, do, o, lse, first, index, dq_out, dko, dkp, dvo, dvp, kscr, vscr, dk, dv
):
    place_keys(scalars, kscr, ko, kp)
    place_keys(scalars, vscr, vo, vp)
    for j, keys in ((1, 1024), (0, 512)):
        lo = j * 256
        ok = allowed(first[...], index[...], lo, keys)
        dkt, dvt = None, None
        for h in range(3):
            rows = slice(h * HDIM, (h + 1) * HDIM)
            qh, doh = q[rows, lo : lo + 256], do[rows, lo : lo + 256]
            delta = jnp.sum(
                doh.astype(F32) * o[rows, lo : lo + 256].astype(F32), axis=0, keepdims=True
            )
            s = tn(kscr[:, :keys], qh)
            p = jnp.exp(jnp.where(ok, s - lse[0, h : h + 1, lo : lo + 256], NEG))
            dp = tn(vscr[:, :keys], doh)
            ds = (p * (dp - delta)).astype(BF)
            dq_out[rows, lo : lo + 256] = nn(kscr[:, :keys], ds) * 0.125
            a, b = nt(qh, ds), nt(doh, p.astype(BF))
            dkt = a if dkt is None else dkt + a
            dvt = b if dvt is None else dvt + b
        if j == 1:
            dk[...] = dkt
            dv[...] = dvt
        else:
            dk[:, :512] += dkt
            dv[:, :512] += dvt
    for j in range(2):
        lo = j * 256
        own = pl.ds(pl.multiple_of(scalars[13 + j] * 256, 256), 256)
        other = pl.ds(pl.multiple_of(scalars[15 + j] * 256, 256), 256)
        dko[:, lo : lo + 256] = dk[:, own].astype(BF)
        dkp[:, lo : lo + 256] = dk[:, other].astype(BF)
        dvo[:, lo : lo + 256] = dv[:, own].astype(BF)
        dvp[:, lo : lo + 256] = dv[:, other].astype(BF)


def attention_back(scalars, q, kv_own, kv_other, do, o, lse, first, index):
    return pl.pallas_call(
        attn_back_kernel,
        out_shape=[sds((D, TOK), F32)] + [sds((KVD, TOK), BF)] * 4,
        grid=(KVH,),
        in_specs=[
            SMEM,
            group_spec(192),
            group_spec(HDIM),
            group_spec(HDIM),
            value_spec(),
            value_spec(),
            group_spec(192),
            group_spec(192),
            pl.BlockSpec((1, 8, TOK), lambda g: (g, 0, 0)),
            row_spec(),
            row_spec(),
        ],
        out_specs=[group_spec(192)] + [group_spec(HDIM)] * 4,
        scratch_shapes=[
            pltpu.VMEM((HDIM, LEN), BF),
            pltpu.VMEM((HDIM, LEN), BF),
            pltpu.VMEM((HDIM, LEN), F32),
            pltpu.VMEM((HDIM, LEN), F32),
        ],
        cost_estimate=cost(30e9, 10e6, 6e6),
        compiler_params=pltpu.CompilerParams(vmem_limit_bytes=48 * 1024 * 1024),
    )(scalars, q, kv_own, kv_other, kv_own, kv_other, do, o, lse, first, index)


def post_kernel(scalars, o, wo0, wo1, x, wv, x1_out, o_rel_out, h2_out, scr):
    o_rel = to_slots(scalars, scr, o[...].astype(F32)).astype(BF)
    o_rel_out[...] = o_rel
    x1 = x[...].astype(F32) + jnp.concatenate(
        [tn(wo0[...], o_rel), tn(wo1[...], o_rel)[:448]], axis=0
    )
    x1_out[...] = x1
    r2 = lax.rsqrt(jnp.mean(x1 * x1, axis=0, keepdims=True) + EPS)
    xn = to_slots(scalars, scr, x1 * r2)
    h2_out[...] = (xn * wv[:, 320:321].astype(F32)).astype(BF)


FT = 256
FSTEPS = 1280 // FT


def ffn_kernel(
    scalars, h2o, h2p, go, gp, wg, wu, wd, out_o, out_p, dh_o, dh_p, gg, gu, gd, acc_o, acc_d
):
    step = pl.program_id(0)
    at = []
    for c in range(4):
        chunk = step * 4 + c
        at.append((scalars[8 + chunk // 5], pl.multiple_of(lax.rem(chunk, 5) * 64, 64)))
    wdt = jnp.concatenate([wd[a, pl.ds(b, 64), :] for a, b in at], axis=0)
    wgt, wut = wg[...], wu[...]
    grad_g, grad_u, grad_d = None, None, None
    for half, (h2, g) in enumerate(((h2o, go), (h2p, gp))):
        hv, gv = h2[...], g[...]
        gate = tn(wgt, hv)
        up = tn(wut, hv)
        sig = 1.0 / (1.0 + jnp.exp(-gate))
        silu = gate * sig
        hid = (silu * up).astype(BF)
        dhid = nn(wdt, gv)
        dgt = (dhid * up * (sig * (1.0 + gate * (1.0 - sig)))).astype(BF)
        dup = (dhid * silu).astype(BF)
        out = tn(wdt, hid)
        dh = nn(wgt, dgt) + nn(wut, dup)
        a, b, c = nt(hv, dgt), nt(hv, dup), nt(hid, gv)
        if half == 0:
            grad_g, grad_u, grad_d = a, b, c
        else:
            grad_g, grad_u, grad_d = grad_g + a, grad_u + b, grad_d + c
        acc_out, acc_dh = (out_o, dh_o) if half == 0 else (acc_o, acc_d)

        @pl.when(step == 0)
        def _():
            acc_out[...] = out
            acc_dh[...] = dh

        @pl.when(step > 0)
        def _():
            acc_out[...] += out
            acc_dh[...] += dh

    gg[...] = grad_g.astype(BF)
    gu[...] = grad_u.astype(BF)
    for c, (a, b) in enumerate(at):
        gd[a, pl.ds(b, 64), :] = grad_d[c * 64 : (c + 1) * 64].astype(BF)

    @pl.when(step == FSTEPS - 1)
    def _():
        out_p[...] = acc_o[...].astype(BF)
        dh_p[...] = acc_d[...].astype(BF)


def ffn(scalars, h2o, h2p, go, gp, wg, wu, wd):
    whole = pl.BlockSpec((D, TOK), lambda t: (0, 0))
    tile = pl.BlockSpec((D, FT), lambda t: (0, t))
    down = pl.BlockSpec((4, 320, D), lambda t: (0, 0, 0))
    return pl.pallas_call(
        ffn_kernel,
        out_shape=[
            sds((D, TOK), F32),
            sds((D, TOK), BF),
            sds((D, TOK), F32),
            sds((D, TOK), BF),
            sds((D, 1280), BF),
            sds((D, 1280), BF),
            sds((4, 320, D), BF),
        ],
        grid=(FSTEPS,),
        in_specs=[SMEM, whole, whole, whole, whole, tile, tile, down],
        out_specs=[whole, whole, whole, whole, tile, tile, down],
        scratch_shapes=[pltpu.VMEM((D, TOK), F32), pltpu.VMEM((D, TOK), F32)],
        cost_estimate=cost(2 * 9 * 1024 * D * 1280, 30e6, 2e6),
        compiler_params=pltpu.CompilerParams(vmem_limit_bytes=56 * 1024 * 1024),
    )(scalars, h2o, h2p, go, gp, wg, wu, wd)


def norm_back_rel(scalars, scr, dh, src_rel, inv, gain):
    scaled = dh * gain
    total = jnp.sum(scaled * src_rel, axis=0, keepdims=True)
    grad_gain = jnp.sum(dh * src_rel * inv, axis=1, keepdims=True)
    back = inv * scaled - src_rel * (inv * inv * inv * total * (1.0 / D))
    return from_slots(scalars, scr, back), grad_gain


def mid_kernel(
    scalars, dho, dhr, oo, orr, x1, g, wv, o_rel, wo0, wo1, dx_out, do_out, out_out, gw0, gw1, gg_out, scr, scr2
):
    x1v = x1[...]
    out = x1v + oo[...] + orr[...].astype(F32)
    store_chunks(scalars, out_out, out.astype(BF))
    r2 = lax.rsqrt(jnp.mean(x1v * x1v, axis=0, keepdims=True) + EPS)
    x1_rel = to_slots(scalars, scr, x1v)
    dh = dho[...] + dhr[...].astype(F32)
    back, grad_gain = norm_back_rel(
        scalars, scr2, dh, x1_rel, r2, wv[:, 320:321].astype(F32)
    )
    gg_out[...] = jnp.broadcast_to(grad_gain, (D, 128))
    dx = g[...].astype(F32) + back
    dx_out[...] = dx
    low = jnp.concatenate([dx.astype(BF), jnp.zeros((64, TOK), BF)], axis=0)
    o_r = o_rel[...]
    gw0[...] = nt(o_r, low[:512]).astype(BF)
    gw1[...] = nt(o_r, low[512:]).astype(BF)
    do = nn(wo0[...], low[:512]) + nn(wo1[...], low[512:])
    do_out[...] = from_slots(scalars, scr, do).astype(BF)


def last_kernel(
    scalars, dq, dko, dkr, dvo, dvr, cos, sin, h1, x, dx1, wq0, wq1, wk, wv, gg2,
    gq0, gq1, gk, gv, gin, scr, scr2,
):
    cosine, sine = cos[...], -sin[...]
    zero = jnp.zeros((64, TOK), BF)
    dqp = jnp.concatenate([rope(dq[...], cosine, sine).astype(BF), zero], axis=0)
    dk = dko[...].astype(F32) + dkr[...].astype(F32)
    dkp = jnp.concatenate([rope(dk, cosine, sine).astype(BF), zero], axis=0)
    dvb = jnp.concatenate(
        [(dvo[...].astype(F32) + dvr[...].astype(F32)).astype(BF), zero], axis=0
    )
    h = h1[...]
    gq0[...] = nt(h, dqp[:512]).astype(BF)
    gq1[...] = nt(h, dqp[512:]).astype(BF)
    dh = nn(wq0[...], dqp[:512]) + nn(wq1[...], dqp[512:]) + nn(wk[...], dkp) + nn(wv[...], dvb)
    xv = x[...].astype(F32)
    r1 = lax.rsqrt(jnp.mean(xv * xv, axis=0, keepdims=True) + EPS)
    x_rel = to_slots(scalars, scr, xv)
    back, gain1 = norm_back_rel(scalars, scr2, dh, x_rel, r1, wk[:, 320:321].astype(F32))
    store_chunks(scalars, gin, (dx1[...] + back).astype(BF))
    lane = lax.broadcasted_iota(jnp.int32, (D, 128), 1)
    for ref, grad, gain in ((gk, nt(h, dkp), gain1), (gv, nt(h, dvb), gg2[:, 0:1])):
        ref[:, :256] = grad[:, :256].astype(BF)
        ref[:, 256:] = jnp.where(lane == 64, gain, grad[:, 256:]).astype(BF)


def body(
    layer_input,
    segments,
    w_query,
    w_key,
    w_value,
    w_output,
    w_gate,
    w_up,
    w_down,
    gain_attn,
    gain_ffn,
    cotangent,
):
    dp, fs = lax.axis_index("dp"), lax.axis_index("fsdp")
    core, yhi, z = dp % 2, fs // 4, fs % 4
    first_core = core == 0
    code = jnp.array([0, 1, 3, 2], jnp.int32)
    zcode = code[z]
    mine = yhi * 4 + zcode
    block = jnp.arange(8, dtype=jnp.int32)
    slot = (block // 4 * 4 + code[block % 4]) ^ mine
    slot4 = code ^ zcode
    rank = jnp.array(RANK_OF, jnp.int32)[fs]
    own_blocks = jnp.where(first_core, jnp.array([0, 3]), jnp.array([1, 2])).astype(jnp.int32)
    other_blocks = jnp.where(first_core, jnp.array([1, 2]), jnp.array([0, 3])).astype(jnp.int32)
    scalars = jnp.concatenate(
        [slot, slot4, jnp.stack([z]), own_blocks, other_blocks, jnp.stack([rank])]
    ).astype(jnp.int32)

    def to_chip(value):
        turned = jnp.swapaxes(value, 1, 2)
        return [
            send(lax.dynamic_index_in_dim(turned, (rank + r) % 4, 0, False), relay(r))
            for r in range(4)
        ]

    def from_chip(chunks):
        return [send(chunks[r], [(b, a) for a, b in relay(r)]) for r in range(4)]

    x_got = to_chip(layer_input)

    def pad(value, width):
        return jnp.pad(value, ((0, 0), (0, width - value.shape[1])))

    wide = jnp.where(first_core, w_query, w_output)
    narrow = jnp.where(
        first_core,
        pad(jnp.concatenate([w_key, gain_attn[:, None]], axis=1), 384),
        pad(jnp.concatenate([w_value, gain_ffn[:, None]], axis=1), 384),
    )
    wide = pad(wide, 1024)
    held = (
        gather_rows(wide[:, :512], ("z1", "z2", "y2")),
        gather_rows(wide[:, 512:], ("z2", "y2", "z1")),
        gather_rows(narrow, ("y2", "z1", "z2")),
    )
    held = tuple(a.reshape(D, a.shape[2]) for a in held)
    others = tuple(send(a, CC) for a in held)
    wq0, wq1, wk = (jnp.where(first_core, a, b) for a, b in zip(held, others))
    wo0, wo1, wv = (jnp.where(first_core, b, a) for a, b in zip(held, others))

    seg_here = lax.dynamic_index_in_dim(segments, z, 0, False)
    seg = jnp.where(core == yhi, seg_here, send(seg_here, CC))
    index = (own_blocks[:, None] * 256 + jnp.arange(256, dtype=jnp.int32)[None, :]).reshape(TOK)
    seg_own = jnp.concatenate(
        [lax.dynamic_slice_in_dim(seg, own_blocks[j] * 256, 256) for j in range(2)]
    )
    first = jnp.sum((seg[:, None] < seg_own[None, :]).astype(jnp.int32), axis=0)
    pos = (index - first).astype(F32)
    freq = THETA ** (-(jnp.arange(32, dtype=F32) * 2.0) / HDIM)
    angle = freq[:, None] * pos[None, :]
    cosine, sine = jnp.cos(angle), jnp.sin(angle)
    first, index = first[None, :], index[None, :]

    x = assemble(scalars, x_got)
    q, kv, h1 = call(
        pre_kernel,
        [sds((D, TOK), BF), sds((2 * KVD, TOK), BF), sds((D, TOK), BF)],
        [scalars, x, wq0, wq1, wk, wv, cosine, sine],
        2 * TOK * D * 1792,
        [pltpu.VMEM((D, TOK), F32)],
    )
    kv_other = send(kv, CC)
    o, lse = attention(scalars, q, kv, kv_other, first, index)

    half = core * 1280
    wg = gather_rows(lax.dynamic_slice_in_dim(w_gate, half, 1280, 1), ("z1", "z2", "y2"))
    wu = gather_rows(lax.dynamic_slice_in_dim(w_up, half, 1280, 1), ("z2", "y2", "z1"))
    wd = jnp.where(core == yhi, w_down, send(w_down, Y2_OWN))
    wd = gather_rows(wd, ("z1", "z2"))
    wg, wu = wg.reshape(D, 1280), wu.reshape(D, 1280)

    g = assemble(scalars, to_chip(cotangent))
    g_other = send(g, CC)

    x1, o_rel, h2 = call(
        post_kernel,
        [sds((D, TOK), F32), sds((D, TOK), BF), sds((D, TOK), BF)],
        [scalars, o, wo0, wo1, x, wv],
        2 * TOK * D * 1024,
        [pltpu.VMEM((D, TOK), F32)],
    )
    h2_other = send(h2, CC)
    out_own, out_part, dh_own, dh_part, grad_g, grad_u, grad_d = ffn(
        scalars, h2, h2_other, g, g_other, wg, wu, wd
    )
    dh_got = send(dh_part, CC)
    out_got = send(out_part, CC)
    dx1, do, out, gwo0, gwo1, gg2 = call(
        mid_kernel,
        [
            sds((D, TOK), F32),
            sds((D, TOK), BF),
            sds((4, D, 128), BF),
            sds((D, 512), BF),
            sds((D, 512), BF),
            sds((D, 128), F32),
        ],
        [scalars, dh_own, dh_got, out_own, out_got, x1, g, wv, o_rel, wo0, wo1],
        4 * TOK * D * 1024,
        [pltpu.VMEM((D, TOK), F32), pltpu.VMEM((D, TOK), F32)],
    )
    out_back = from_chip(out)

    grad_g = scatter_rows(grad_g.reshape(8, ROWS, 1280), ("y2", "z2", "z1"))
    grad_u = scatter_rows(grad_u.reshape(8, ROWS, 1280), ("z1", "y2", "z2"))
    grad_d = scatter_rows(grad_d, ("z2", "z1"))
    got = send(grad_d, Y2_BACK)
    grad_d = jnp.where(core == yhi, grad_d, got)
    rows = lax.dynamic_slice_in_dim(grad_d, (1 - core) * 160, 160, 0)
    keep = lax.dynamic_slice_in_dim(grad_d, core * 160, 160, 0)
    grad_d = (keep.astype(F32) + send(rows, CC).astype(F32)).astype(BF)
    groups = [list(range(c, 16, 2)) for c in range(2)]

    def over_dp(value):
        parts = value.reshape(8, value.shape[0] // 8, value.shape[1])
        got = lax.all_to_all(parts, "dp", 0, 0, axis_index_groups=groups)
        total = jnp.sum(got.astype(F32), axis=0).astype(BF)
        every = lax.all_gather(total, "dp", axis=0)
        every = every.reshape(8, 2, *total.shape)
        return every[:, 0].reshape(value.shape), every[:, 1].reshape(value.shape)

    joined = jnp.concatenate(
        [grad_g, grad_u, grad_d.reshape(ROWS, 1280), jnp.zeros((24, 1280), BF)], axis=0
    )
    ffn0, ffn1 = over_dp(joined)

    dq, dko, dkp, dvo, dvp = attention_back(scalars, q, kv, kv_other, do, o, lse, first, index)
    dkr, dvr = send(dkp, CC), send(dvp, CC)
    gq0, gq1, gk, gv, gin = call(
        last_kernel,
        [
            sds((D, 512), BF),
            sds((D, 512), BF),
            sds((D, 384), BF),
            sds((D, 384), BF),
            sds((4, D, 128), BF),
        ],
        [scalars, dq, dko, dkr, dvo, dvr, cosine, sine, h1, x, dx1, wq0, wq1, wk, wv, gg2],
        4 * TOK * D * 1792,
        [pltpu.VMEM((D, TOK), F32), pltpu.VMEM((D, TOK), F32)],
    )
    gin_back = from_chip(gin)

    def over_core(for0, for1):
        got = send(jnp.where(first_core, for1, for0), CC)
        total = jnp.where(first_core, for0, for1).astype(F32) + got.astype(F32)
        return total.astype(BF).reshape(8, ROWS, for0.shape[1])

    attn = jnp.concatenate(
        [
            scatter_rows(over_core(gq0, gwo0), ("y2", "z2", "z1")),
            scatter_rows(over_core(gq1, gwo1), ("z1", "y2", "z2")),
            scatter_rows(over_core(gk, gv), ("z2", "z1", "y2")),
        ],
        axis=1,
    )
    attn0, attn1 = over_dp(jnp.pad(attn, ((0, 8), (0, 0))))

    out_final = jnp.swapaxes(finish(scalars, out_back, BF), 1, 2)
    gin_final = jnp.swapaxes(finish(scalars, gin_back, F32), 1, 2)
    attn0, attn1 = attn0[:ROWS].astype(F32), attn1[:ROWS].astype(F32)
    ffn0, ffn1 = ffn0.astype(F32), ffn1.astype(F32)
    return (
        out_final,
        gin_final,
        attn0[:, :960],
        attn0[:, 1024:1344],
        attn1[:, 1024:1344],
        attn1[:, :960],
        jnp.concatenate([ffn0[:120], ffn1[:120]], axis=1),
        jnp.concatenate([ffn0[120:240], ffn1[120:240]], axis=1),
        jnp.concatenate(
            [ffn0[240:360].reshape(160, 960), ffn1[240:360].reshape(160, 960)], axis=0
        ),
        attn0[:, 1344],
        attn1[:, 1344],
    )


def solution(mesh):
    rows = P("fsdp", None)
    in_specs = (
        (P("dp", "fsdp", None), P("dp", None))
        + (rows,) * 7
        + (P("fsdp"), P("fsdp"), P("dp", "fsdp", None))
    )
    out_specs = (P("dp", "fsdp", None),) * 2 + (rows,) * 7 + (P("fsdp"), P("fsdp"))
    return jax.shard_map(body, mesh=mesh, in_specs=in_specs, out_specs=out_specs, check_vma=False)
```

```python
import functools

import jax
import jax.numpy as jnp
import numpy as np
from jax import lax
from jax.experimental import pallas as pl
from jax.experimental.pallas import tpu as pltpu
from jax.sharding import PartitionSpec as P

D = 960
H = 15
KVH = 5
HDIM = 64
FF = 2560
KVD = 320
LEN = 1024
EPS = 1e-05
THETA = 100000.0
TOK = 512
ROWS = 120
NEG = -1e30
BF = jnp.bfloat16
F32 = jnp.float32
AXES = ("dp", "fsdp")


def coords(i):
    dp, fs = divmod(i, 8)
    ylo, rest = divmod(dp, 8)
    x, core = divmod(rest, 2)
    yhi, z = divmod(fs, 4)
    return ylo, x, core, yhi, z


def flat(ylo, x, core, yhi, z):
    return ((ylo * 4 + x) * 2 + core) * 8 + yhi * 4 + z


def perm(fn, keep=lambda *a: True):
    return [(i, flat(*fn(*coords(i)))) for i in range(128) if keep(*coords(i))]


Z1 = perm(lambda yl, x, c, yh, z: (yl, x, c, yh, z ^ 1))
Z2 = perm(lambda yl, x, c, yh, z: (yl, x, c, yh, 3 - z))
Y2 = perm(lambda yl, x, c, yh, z: (1 - yl, x, c, 1 - yh, z))
CC = perm(lambda yl, x, c, yh, z: (yl, x, 1 - c, yh, z))
DUP_X = perm(lambda yl, x, c, yh, z: (yl, 3 - x if c else x ^ 1, c, yh, z))
DUP_Y = perm(lambda yl, x, c, yh, z: (1 - yl, x, c, yh, z))


def dup_x(x, core):
    return x >> 1 if core else (x >> 1) ^ (x & 1)


DIMS = (("z1", "z2", "y2"), ("z2", "y2", "z1"))
FLIP = {
    "z1": lambda yl, x, c, yh, z: (yl, x, c, yh, z ^ 1),
    "z2": lambda yl, x, c, yh, z: (yl, x, c, yh, 3 - z),
    "y2": lambda yl, x, c, yh, z: (1 - yl, x, c, 1 - yh, z),
}
STEPS = [perm(lambda yl, x, c, yh, z, k=k: FLIP[DIMS[c][k]](yl, x, c, yh, z)) for k in range(3)]
D_STEPS = [Y2, Z1, Z2]
GRAY = (0, 1, 3, 2)

CORE_OF = (0, 0, 1, 1, 1, 1, 0, 0)
RANK_OF = (0, 1, 0, 1, 2, 3, 2, 3)


AT = (lambda z: z, lambda z: z ^ 1, lambda z: 3 - z, lambda z: (z + 2) % 4)
RELAY = [
    perm(lambda yl, x, c, yh, z, r=r: (1 - yl, x, CORE_OF[yh * 4 + z], c, AT[r](z)))
    for r in range(4)
]
RELAY_BACK = [[(b, a) for a, b in pairs] for pairs in RELAY]
SEGMENTS = perm(lambda yl, x, c, yh, z: (1 - yl, x, yh, c, z))


def send(x, pairs):
    return lax.ppermute(x, AXES, pairs)


def nn(a, b):
    return lax.dot_general(a, b, (((1,), (0,)), ((), ())), preferred_element_type=F32)


def nt(a, b):
    return lax.dot_general(a, b, (((1,), (1,)), ((), ())), preferred_element_type=F32)


def tn(a, b):
    return lax.dot_general(a, b, (((0,), (0,)), ((), ())), preferred_element_type=F32)


def cost(flops, nbytes, trans=0):
    return pl.CostEstimate(flops=int(flops), bytes_accessed=int(nbytes), transcendentals=int(trans))


VMEM = pl.BlockSpec(memory_space=pltpu.VMEM)
SMEM = pl.BlockSpec(memory_space=pltpu.SMEM)
ANY = pl.BlockSpec(memory_space=pl.ANY)


def call(kernel, outs, ins, flops, scratch=(), trans=0, deps=(), specs=None):
    nbytes = sum(a.size * a.dtype.itemsize for a in ins) + sum(
        a.size * a.dtype.itemsize for a in outs
    )
    n_in, n_dep = len(ins), len(deps)

    def run(*refs):
        kernel(*refs[:n_in], *refs[n_in + n_dep :])

    return pl.pallas_call(
        run,
        out_shape=outs,
        grid=(1,) if specs else (),
        in_specs=(specs or [SMEM] + [VMEM] * (n_in - 1))
        + [pl.BlockSpec(memory_space=pl.ANY)] * n_dep,
        out_specs=[VMEM] * len(outs),
        scratch_shapes=list(scratch),
        cost_estimate=cost(flops, nbytes, trans),
        compiler_params=pltpu.CompilerParams(vmem_limit_bytes=48 * 1024 * 1024),
    )(*ins, *deps)


def sds(shape, dtype):
    return jax.ShapeDtypeStruct(shape, dtype)


A, B, MINE, OTHER, D_OF, SEQ, POS, ROUND, OWN, PAIR, CORE, HALF, DOWN = (
    0, 8, 16, 24, 32, 40, 44, 48, 52, 54, 56, 57, 58
)


def scalar_table():
    table = np.zeros((128, 59), np.int32)
    for i in range(128):
        yl, x, c, yh, z = coords(i)
        apart = [(s // 4 * 4 + GRAY[s % 4]) ^ (yh * 4 + GRAY[z]) for s in range(8)]
        orders = (apart, [a // 2 + a % 2 * 4 for a in apart])
        slots = [a // 4 + a % 4 * 2 for a in apart]
        senders = [[h * 4 + AT[r](z) for h in range(2)] for r in range(4)]
        places = [RANK_OF[q] for pair in senders for q in pair if CORE_OF[q] == c]
        table[i] = (
            orders[0]
            + orders[1]
            + orders[c]
            + orders[1 - c]
            + [slots.index(k) for k in range(8)]
            + [AT[r](z) for r in range(4)]
            + places
            + [places.index(k) for k in range(4)]
            + ([1, 2, 0, 3] if c else [0, 3, 1, 2])
            + [c, dup_x(x, c), yl ^ yh]
        )
    return table


def to_slots(scalars, base, scratch, value):
    for s in range(8):
        at = pl.multiple_of(scalars[base + s] * ROWS, 8)
        scratch[pl.ds(at, ROWS), : value.shape[1]] = value[s * ROWS : (s + 1) * ROWS]
    return scratch[:, : value.shape[1]]


def from_slots(scalars, base, scratch, value):
    scratch[:, : value.shape[1]] = value
    return jnp.concatenate(
        [
            scratch[pl.ds(pl.multiple_of(scalars[base + s] * ROWS, 8), ROWS), : value.shape[1]]
            for s in range(8)
        ],
        axis=0,
    )


def join_kernel(scalars, a, b, out):
    n = a.shape[0]
    out[:n] = a[...]
    out[n:] = b[...]


def join(scalars, a, b, deps=()):
    shape = (2 * a.shape[0], *a.shape[1:])
    return call(join_kernel, [sds(shape, a.dtype)], [scalars, a, b], 0, deps=deps)[0]


def add_kernel(shape, scalars, *refs):
    outs = list(refs[sum(sum(group) for group in shape) :])
    at = 0
    for group in shape:
        totals = []
        for count in group:
            total = refs[at][...].astype(F32)
            for k in range(1, count):
                total = total + refs[at + k][...].astype(F32)
            at += count
            totals.append(total.astype(BF))
        total = totals[0] if len(totals) == 1 else jnp.concatenate(totals, axis=-1)
        half = total.shape[0] // 2
        if half:
            outs.pop(0)[...] = total[:half]
            outs.pop(0)[...] = total[half:]
        else:
            outs.pop(0)[...] = total


def add(scalars, groups, deps=()):
    outs = []
    for group in groups:
        n = group[0][0].shape[0]
        shape = (*group[0][0].shape[1:-1], sum(terms[0].shape[-1] for terms in group))
        outs += [sds((n // 2, *shape), BF)] * 2 if n > 1 else [sds((n, *shape), BF)]
    return call(
        functools.partial(add_kernel, [[len(terms) for terms in group] for group in groups]),
        outs,
        [scalars, *[a for group in groups for terms in group for a in terms]],
        0,
        deps=deps,
    )


def touch_kernel(value, *refs):
    pass


def touch(value, deps):
    return pl.pallas_call(
        touch_kernel,
        out_shape=sds(value.shape, value.dtype),
        in_specs=[ANY] * (1 + len(deps)),
        out_specs=ANY,
        input_output_aliases={0: 0},
    )(value, *deps)


def pick_kernel(scalars, value, *outs):
    for r, ref in enumerate(outs):
        ref[...] = value[scalars[SEQ + r]]


def pick(scalars, value, deps=()):
    value = jnp.swapaxes(value, 1, 2)
    return call(pick_kernel, [sds((D, 128), BF)] * 4, [scalars, value], 0, deps=deps)


def assemble_kernel(scalars, r0, r1, r2, r3, out):
    for r, ref in enumerate((r0, r1, r2, r3)):
        out[:, pl.ds(pl.multiple_of(scalars[POS + r] * 128, 128), 128)] = ref[...]


def assemble(scalars, got, deps=()):
    return call(assemble_kernel, [sds((D, TOK), BF)], [scalars, *got], 0, deps=deps)[0]


def store_chunks(scalars, out, value):
    for k in range(4):
        out[scalars[ROUND + k]] = value[:, k * 128 : (k + 1) * 128]


def finish_kernel(scalars, r0, r1, r2, r3, out):
    for r, ref in enumerate((r0, r1, r2, r3)):
        out[scalars[SEQ + r]] = ref[...].astype(out.dtype)


def finish(scalars, got, dtype, deps=()):
    return call(finish_kernel, [sds((4, D, 128), dtype)], [scalars, *got], 0, deps=deps)[0]


def rope(value, cosine, sine):
    parts = []
    for h in range(value.shape[0] // HDIM):
        first = value[h * HDIM : h * HDIM + 32]
        second = value[h * HDIM + 32 : (h + 1) * HDIM]
        parts += [first * cosine - second * sine, second * cosine + first * sine]
    return jnp.concatenate(parts, axis=0)


def by_core(scalars, held, other):
    zero = scalars[CORE] == 0
    return jnp.where(zero, held, other), jnp.where(zero, other, held)


def rows_of(first, second):
    return jnp.concatenate([first[...], second[...]], axis=0)


WIDTH = 896
GAIN_SPEC = pl.BlockSpec((D // 2, 128), lambda i: (0, 6))
UP, OUT = 1280, 512


def prep_kernel(scalars, wq, wk, wv, gains, out):
    zero = lax.broadcasted_iota(jnp.int32, (1, 1), 0) + scalars[CORE] == 0
    out[...] = jnp.where(
        zero,
        jnp.concatenate([wq[:, :768], gains[...]], axis=1),
        jnp.concatenate([wq[:, 768:], wk[...], wv[...], jnp.zeros((ROWS, 64), BF)], axis=1),
    )


def columns_of(w, core):
    return jnp.concatenate(
        [w[:, 320 * s + 160 * core : 320 * s + 160 * (core + 1)] for s in range(8)], axis=1
    )


def prep_ffn_kernel(scalars, two, got, wg, wu, wd, wo, held, gu, down):
    join_kernel(scalars, two, got, held)
    zero = lax.broadcasted_iota(jnp.int32, (1, 1), 0) + scalars[CORE] == 0
    first = lax.broadcasted_iota(jnp.int32, (1, 1), 0) + scalars[HALF] == 0
    w = jnp.where(first, wg[...], wu[...])
    gu[0, :, :UP] = jnp.where(zero, columns_of(w, 0), columns_of(w, 1))
    rest = jnp.concatenate([wo[:, OUT:], jnp.zeros((ROWS, 64), BF)], axis=1)
    gu[0, :, UP:] = jnp.where(zero, wo[:, :OUT], rest)
    at = pl.multiple_of(scalars[CORE] * 160 + scalars[DOWN] * 80, 16)
    down[0] = wd[pl.ds(at, 80), :]


def grow_kernel(scalars, gu, gu_got, down, down_got, gu_out, down_out, *only):
    n = gu.shape[0]
    gu_out[:n] = gu[...]
    gu_out[n:] = gu_got[...]
    down_out[:n] = down[...]
    down_out[n:] = down_got[...]
    for ref in only:
        ref[:n] = gu[:, :, :UP]
        ref[n:] = gu_got[:, :, :UP]


def grow(scalars, gu, gu_got, down, down_got, last, deps):
    outs = [sds((2 * a.shape[0], *a.shape[1:]), BF) for a in (gu, down)]
    if last:
        outs.append(sds((2 * gu.shape[0], ROWS, UP), BF))
    return call(grow_kernel, outs, [scalars, gu, gu_got, down, down_got], 0, deps=deps)


def part_kernel(scalars, gu0, gu1, up1, wo):
    up1[...] = gu1[:, :, :UP]
    wo[:4] = gu0[:, :, UP:]
    wo[4:] = gu1[:, :, UP:]


def pre_kernel(scalars, x, h0, h1, o0, o1, cos, sin, q_out, kv_out, ha_out, hb_out, scr):
    wa, wb = by_core(scalars, rows_of(h0, h1), rows_of(o0, o1))
    xv = x[...].astype(F32)
    r1 = lax.rsqrt(jnp.mean(xv * xv, axis=0, keepdims=True) + EPS)
    ha = (to_slots(scalars, A, scr, xv * r1) * wa[:, 768:769].astype(F32)).astype(BF)
    hb = to_slots(scalars, B, scr, from_slots(scalars, A, scr, ha.astype(F32))).astype(BF)
    ha_out[...] = ha
    hb_out[...] = hb
    cosine, sine = cos[...], sin[...]
    q0 = rope(tn(wa[:, :768], ha), cosine, sine)
    q_out[0:768, :] = (q0.astype(BF).astype(F32) * 0.125).astype(BF)
    rest = tn(wb, hb)
    q1 = rope(rest[:192], cosine, sine)
    q_out[768:960, :] = (q1.astype(BF).astype(F32) * 0.125).astype(BF)
    kv_out[0:320, :] = rope(rest[192:512], cosine, sine).astype(BF)
    kv_out[320:640, :] = rest[512:832].astype(BF)


def place_keys(scalars, out, own, other):
    for j in range(2):
        lo = j * 256
        out[:, pl.ds(pl.multiple_of(scalars[OWN + j] * 256, 256), 256)] = own[:, lo : lo + 256]
        out[:, pl.ds(pl.multiple_of(scalars[PAIR + j] * 256, 256), 256)] = other[:, lo : lo + 256]


def allowed(first, index, lo, keys):
    key = lax.broadcasted_iota(jnp.int32, (keys, 256), 0)
    return (key >= first[:, lo : lo + 256]) & (key <= index[:, lo : lo + 256])


def attn_kernel(scalars, q, ko, kp, vo, vp, first, index, o_out, lse_out, kscr, vscr):
    place_keys(scalars, kscr, ko, kp)
    place_keys(scalars, vscr, vo, vp)
    for j, keys in enumerate((512, 1024)):
        lo = j * 256
        ok = allowed(first[...], index[...], lo, keys)
        for h in range(3):
            s = tn(kscr[:, :keys], q[h * HDIM : (h + 1) * HDIM, lo : lo + 256])
            s = jnp.where(ok, s, NEG)
            top = jnp.max(s, axis=0, keepdims=True)
            p = jnp.exp(s - top)
            total = jnp.sum(p, axis=0, keepdims=True)
            o = nn(vscr[:, :keys], p.astype(BF)) / total
            o_out[h * HDIM : (h + 1) * HDIM, lo : lo + 256] = o.astype(BF)
            lse_out[0, h : h + 1, lo : lo + 256] = top + jnp.log(total)


def group_spec(rows):
    return pl.BlockSpec((rows, TOK), lambda g, *_: (g, 0))


def value_spec():
    return pl.BlockSpec((HDIM, TOK), lambda g, *_: (KVH + g, 0))


def row_spec():
    return pl.BlockSpec((1, TOK), lambda g, *_: (0, 0))


def skip(kernel, first, count):
    def run(*refs):
        kernel(*refs[:first], *refs[first + count :])

    return run


def attention(scalars, q, kv_own, kv_other, first, index, deps):
    return pl.pallas_call(
        skip(attn_kernel, 8, len(deps)),
        out_shape=[sds((D, TOK), BF), sds((KVH, 8, TOK), F32)],
        grid=(KVH,),
        in_specs=[
            SMEM,
            group_spec(192),
            group_spec(HDIM),
            group_spec(HDIM),
            value_spec(),
            value_spec(),
            row_spec(),
            row_spec(),
        ]
        + [ANY] * len(deps),
        out_specs=[group_spec(192), pl.BlockSpec((1, 8, TOK), lambda g: (g, 0, 0))],
        scratch_shapes=[pltpu.VMEM((HDIM, LEN), BF), pltpu.VMEM((HDIM, LEN), BF)],
        cost_estimate=cost(12e9, 6e6, 6e6),
        compiler_params=pltpu.CompilerParams(vmem_limit_bytes=48 * 1024 * 1024),
    )(scalars, q, kv_own, kv_other, kv_own, kv_other, first, index, *deps)


def attn_back_kernel(
    scalars, q, ko, kp, vo, vp, do, o, lse, first, index, dq_out, dko, dkp, dvo, dvp, kscr, vscr, dk, dv
):
    place_keys(scalars, kscr, ko, kp)
    place_keys(scalars, vscr, vo, vp)
    for j, keys in ((1, 1024), (0, 512)):
        lo = j * 256
        ok = allowed(first[...], index[...], lo, keys)
        dkt, dvt = None, None
        for h in range(3):
            rows = slice(h * HDIM, (h + 1) * HDIM)
            qh, doh = q[rows, lo : lo + 256], do[rows, lo : lo + 256]
            delta = jnp.sum(
                doh.astype(F32) * o[rows, lo : lo + 256].astype(F32), axis=0, keepdims=True
            )
            s = tn(kscr[:, :keys], qh)
            p = jnp.exp(jnp.where(ok, s - lse[0, h : h + 1, lo : lo + 256], NEG))
            dp = tn(vscr[:, :keys], doh)
            ds = (p * (dp - delta)).astype(BF)
            dq_out[rows, lo : lo + 256] = nn(kscr[:, :keys], ds) * 0.125
            a, b = nt(qh, ds), nt(doh, p.astype(BF))
            dkt = a if dkt is None else dkt + a
            dvt = b if dvt is None else dvt + b
        if j == 1:
            dk[...] = dkt
            dv[...] = dvt
        else:
            dk[:, :512] += dkt
            dv[:, :512] += dvt
    for j in range(2):
        lo = j * 256
        own = pl.ds(pl.multiple_of(scalars[OWN + j] * 256, 256), 256)
        other = pl.ds(pl.multiple_of(scalars[PAIR + j] * 256, 256), 256)
        dko[:, lo : lo + 256] = dk[:, own].astype(BF)
        dkp[:, lo : lo + 256] = dk[:, other].astype(BF)
        dvo[:, lo : lo + 256] = dv[:, own].astype(BF)
        dvp[:, lo : lo + 256] = dv[:, other].astype(BF)


def attention_back(scalars, q, kv_own, kv_other, do, o, lse, first, index, deps):
    return pl.pallas_call(
        skip(attn_back_kernel, 11, len(deps)),
        out_shape=[sds((D, TOK), F32)] + [sds((KVD, TOK), BF)] * 4,
        grid=(KVH,),
        in_specs=[
            SMEM,
            group_spec(192),
            group_spec(HDIM),
            group_spec(HDIM),
            value_spec(),
            value_spec(),
            group_spec(192),
            group_spec(192),
            pl.BlockSpec((1, 8, TOK), lambda g: (g, 0, 0)),
            row_spec(),
            row_spec(),
        ]
        + [ANY] * len(deps),
        out_specs=[group_spec(192)] + [group_spec(HDIM)] * 4,
        scratch_shapes=[
            pltpu.VMEM((HDIM, LEN), BF),
            pltpu.VMEM((HDIM, LEN), BF),
            pltpu.VMEM((HDIM, LEN), F32),
            pltpu.VMEM((HDIM, LEN), F32),
        ],
        cost_estimate=cost(30e9, 10e6, 6e6),
        compiler_params=pltpu.CompilerParams(vmem_limit_bytes=48 * 1024 * 1024),
    )(scalars, q, kv_own, kv_other, kv_own, kv_other, do, o, lse, first, index, *deps)


def gain_of(scalars, scr, gains, column):
    gains = by_core(scalars, rows_of(*gains[:2]), rows_of(*gains[2:]))[0]
    return from_slots(scalars, A, scr, gains.astype(F32))[:, column : column + 1]


def post_kernel(
    scalars, o, ho, oo, x, g0, g1, g2, g3, x1_out, oa_out, ob_out, h2_out, h2_send, scr
):
    of = o[...].astype(F32)
    wo0, wo1 = by_core(scalars, ho[...], oo[...])
    oa = to_slots(scalars, A, scr, of).astype(BF)
    ob = to_slots(scalars, B, scr, of).astype(BF)
    oa_out[...] = oa
    ob_out[...] = ob
    x1 = x[...].astype(F32) + jnp.concatenate([tn(wo0, oa), tn(wo1, ob)[:448]], axis=0)
    x1_out[...] = x1
    r2 = lax.rsqrt(jnp.mean(x1 * x1, axis=0, keepdims=True) + EPS)
    h2 = x1 * r2 * gain_of(scalars, scr, (g0, g1, g2, g3), 1)
    h2_out[...] = to_slots(scalars, MINE, scr, h2).astype(BF)
    h2_send[...] = to_slots(scalars, OTHER, scr, h2).astype(BF)


FT = 256
FSTEPS = 1280 // FT


def ffn_kernel(
    scalars, h2o, h2p, go, gp, a0, a1, b0, b1, d0, d1, e0, e1,
    out_o, out_p, dh_o, dh_p, keep, give, dkeep, dgive, acc_o, acc_d, wd, gd,
):
    step = pl.program_id(0)

    def rows_at(k, half):
        return pl.ds(pl.multiple_of(scalars[D_OF + k] * 160 + half * 80, 16), 80)

    @pl.when(step == 0)
    def _():
        for half, pair in ((scalars[DOWN], (d0, d1)), (1 - scalars[DOWN], (e0, e1))):
            for k in range(8):
                wd[rows_at(k, half), :] = pair[k // 4][k % 4]

    first = scalars[HALF] == 0
    mine, theirs = rows_of(a0, a1), rows_of(b0, b1)
    wgt, wut = jnp.where(first, mine, theirs), jnp.where(first, theirs, mine)
    wdt = wd[pl.ds(pl.multiple_of(step * FT, FT), FT), :]
    grad_g, grad_u, grad_d = None, None, None
    for half, (h2, g) in enumerate(((h2o, go), (h2p, gp))):
        hv, gv = h2[...], g[...]
        gate = tn(wgt, hv)
        up = tn(wut, hv)
        sig = 1.0 / (1.0 + jnp.exp(-gate))
        silu = gate * sig
        hid = (silu * up).astype(BF)
        dhid = nn(wdt, gv)
        dgt = (dhid * up * (sig * (1.0 + gate * (1.0 - sig)))).astype(BF)
        dup = (dhid * silu).astype(BF)
        out = tn(wdt, hid)
        dh = nn(wgt, dgt) + nn(wut, dup)
        a, b, c = nt(hv, dgt), nt(hv, dup), nt(hid, gv)
        if half == 0:
            grad_g, grad_u, grad_d = a, b, c
        else:
            grad_g, grad_u, grad_d = grad_g + a, grad_u + b, grad_d + c
        acc_out, acc_dh = (out_o, dh_o) if half == 0 else (acc_o, acc_d)

        @pl.when(step == 0)
        def _():
            acc_out[...] = out
            acc_dh[...] = dh

        @pl.when(step > 0)
        def _():
            acc_out[...] += out
            acc_dh[...] += dh

    grad_g, grad_u = grad_g.astype(BF), grad_u.astype(BF)
    keep[...], give[...] = jnp.where(first, grad_g, grad_u), jnp.where(first, grad_u, grad_g)
    gd[pl.ds(pl.multiple_of(step * FT, FT), FT), :] = grad_d.astype(BF)

    @pl.when(step == FSTEPS - 1)
    def _():
        out_p[...] = acc_o[...].astype(BF)
        dh_p[...] = acc_d[...].astype(BF)
        for k in range(8):
            dkeep[k] = gd[rows_at(k, scalars[HALF]), :]
            dgive[k] = gd[rows_at(k, 1 - scalars[HALF]), :]


def ffn(scalars, h2o, h2p, go, gp, up_weights, down_weights):
    whole = pl.BlockSpec((D, TOK), lambda t: (0, 0))
    part = pl.BlockSpec((D // 2, FT), lambda t: (0, t))
    full = pl.BlockSpec((D, FT), lambda t: (0, t))
    four = pl.BlockSpec((4, 80, D), lambda t: (0, 0, 0))
    eight = pl.BlockSpec((8, 80, D), lambda t: (0, 0, 0))
    return pl.pallas_call(
        ffn_kernel,
        out_shape=[
            sds((D, TOK), F32),
            sds((D, TOK), BF),
            sds((D, TOK), F32),
            sds((D, TOK), BF),
        ]
        + [sds((D, 1280), BF)] * 2
        + [sds((8, 80, D), BF)] * 2,
        grid=(FSTEPS,),
        in_specs=[SMEM] + [whole] * 4 + [part] * 4 + [four] * 4,
        out_specs=[whole] * 4 + [full] * 2 + [eight] * 2,
        scratch_shapes=[
            pltpu.VMEM((D, TOK), F32),
            pltpu.VMEM((D, TOK), F32),
            pltpu.VMEM((1280, D), BF),
            pltpu.VMEM((1280, D), BF),
        ],
        cost_estimate=cost(2 * 9 * 1024 * D * 1280, 30e6, 2e6),
        compiler_params=pltpu.CompilerParams(vmem_limit_bytes=56 * 1024 * 1024),
    )(scalars, h2o, h2p, go, gp, *up_weights, *down_weights)


def norm_back(dh, source, inv, gain):
    scaled = dh * gain
    total = jnp.sum(scaled * source, axis=0, keepdims=True)
    grad_gain = jnp.sum(dh * source * inv, axis=1, keepdims=True)
    return inv * scaled - source * (inv * inv * inv * total * (1.0 / D)), grad_gain


def mid_kernel(
    scalars, dho, dhr, x1, g, g0, g1, g2, g3, oa, ob, ho, oo,
    dx_out, do_out, keep, give, gg_out, scr,
):
    wo0, wo1 = by_core(scalars, ho[...], oo[...])
    x1v = x1[...]
    r2 = lax.rsqrt(jnp.mean(x1v * x1v, axis=0, keepdims=True) + EPS)
    dh = from_slots(scalars, MINE, scr, dho[...])
    dh = dh + from_slots(scalars, OTHER, scr, dhr[...].astype(F32))
    back, grad_gain = norm_back(dh, x1v, r2, gain_of(scalars, scr, (g0, g1, g2, g3), 1))
    gg_out[...] = jnp.broadcast_to(grad_gain, (D, 128))
    dx = g[...].astype(F32) + back
    dx_out[...] = dx
    low = jnp.concatenate([dx.astype(BF), jnp.zeros((64, TOK), BF)], axis=0)
    gw0 = nt(oa[...], low[:512]).astype(BF)
    gw1 = nt(ob[...], low[512:]).astype(BF)
    keep[...], give[...] = by_core(scalars, gw0, gw1)
    do = from_slots(scalars, A, scr, nn(wo0, low[:512]))
    do_out[...] = (do + from_slots(scalars, B, scr, nn(wo1, low[512:]))).astype(BF)


def out_kernel(scalars, x1, own, got, out):
    store_chunks(scalars, out, (x1[...] + own[...] + got[...].astype(F32)).astype(BF))


def gain1_of(scalars, scr, wa):
    return from_slots(scalars, A, scr, wa[:, 768:896].astype(F32))[:, 0:1]


def last_kernel(scalars, dq, dko, dvo, dkv, cos, sin, ha, hb, qkv, keep, give):
    cosine, sine = cos[...], -sin[...]
    dqp = rope(dq[...], cosine, sine).astype(BF)
    dkp = rope(dko[...].astype(F32) + dkv[:KVD].astype(F32), cosine, sine).astype(BF)
    dvb = (dvo[...].astype(F32) + dkv[KVD:].astype(F32)).astype(BF)
    rest = jnp.concatenate([dqp[768:], dkp, dvb, jnp.zeros((64, TOK), BF)], axis=0)
    qkv[:768] = dqp[:768]
    qkv[768:] = rest
    gwb = nt(hb[...], rest).astype(BF)
    gwa = jnp.concatenate([nt(ha[...], dqp[:768]), jnp.zeros((D, 128), F32)], axis=1).astype(BF)
    keep[...], give[...] = by_core(scalars, gwa, gwb)


def input_kernel(scalars, qkv, x, dx1, h0, h1, o0, o1, gain2, chunks, gains, scr):
    wa, wb = by_core(scalars, rows_of(h0, h1), rows_of(o0, o1))
    dh = from_slots(scalars, A, scr, nn(wa[:, :768], qkv[:768]))
    dh = dh + from_slots(scalars, B, scr, nn(wb, qkv[768:]))
    xv = x[...].astype(F32)
    r1 = lax.rsqrt(jnp.mean(xv * xv, axis=0, keepdims=True) + EPS)
    back, gain1 = norm_back(dh, xv, r1, gain1_of(scalars, scr, wa))
    store_chunks(scalars, chunks, (dx1[...] + back).astype(BF))
    lane = lax.broadcasted_iota(jnp.int32, (D, 128), 1) - scalars[CORE] * 64
    value = jnp.where(lane == 0, gain1, jnp.where(lane == 1, gain2[...], 0.0))
    gains[...] = to_slots(scalars, MINE, scr, value).astype(BF)


def sum_kernel(scalars, keep, got, gains, gu, gu_got, d, d_got, *outs):
    total = keep[...].astype(F32) + got[...].astype(F32)
    last = total[:, :, 768:] + gains[...].astype(F32)
    outs[0][:, :, :768] = total[:4, :, :768].astype(BF)
    outs[0][:, :, 768:] = last[:4].astype(BF)
    outs[1][:, :, :768] = total[4:, :, :768].astype(BF)
    outs[1][:, :, 768:] = last[4:].astype(BF)
    for k, (a, b) in enumerate(((gu, gu_got), (d, d_got))):
        value = (a[...].astype(F32) + b[...].astype(F32)).astype(BF)
        outs[2 + 2 * k][...] = value[:1]
        outs[3 + 2 * k][...] = value[1:]


def grads_kernel(groups, scalars, mine, other, gate, up, down):
    parts = by_core(scalars, mine[...], other[...])
    for which, ref in enumerate((gate, up)):
        halves = []
        for c in range(2):
            rows = [parts[c][d // 2, :32] for d in groups[2 * c + which]]
            halves.append(jnp.concatenate(rows, axis=0)[:ROWS])
        blocks = [h[:, 160 * s : 160 * (s + 1)] for s in range(8) for h in halves]
        ref[...] = jnp.concatenate(blocks, axis=1).astype(F32)
    for c in range(2):
        for half in range(2):
            rows = [parts[c][d // 2, 32:, :D].astype(F32) for d in groups[2 * c + half]]
            at = 160 * c + 80 * half
            down[at : at + 80, :] = jnp.concatenate(rows, axis=0)[:80]


def attn_grads_kernel(scalars, mine, other, query, key, value, output, gains):
    a, b = by_core(scalars, mine[...].astype(F32), other[...].astype(F32))
    a = a.reshape(128, a.shape[2])[:ROWS]
    b = b.reshape(128, b.shape[2])[:ROWS]
    query[:, :768] = a[:, :768]
    query[:, 768:] = b[:, :192]
    key[...] = b[:, 192:512].T
    value[...] = b[:, 512:832].T
    output[:, :OUT] = a[:, WIDTH:]
    output[:, OUT:] = b[:, WIDTH:1344]
    gains[...] = a[:, 768:896] + jnp.concatenate([b[:, 832:896], b[:, 832:896]], axis=1)


def body(
    layer_input,
    segments,
    w_query,
    w_key,
    w_value,
    w_output,
    w_gate,
    w_up,
    w_down,
    gain_attn,
    gain_ffn,
    cotangent,
):
    dp, fs = lax.axis_index("dp"), lax.axis_index("fsdp")
    core, yhi, z = dp % 2, fs // 4, fs % 4
    first_core = core == 0
    scalars = lax.dynamic_index_in_dim(jnp.asarray(scalar_table()), dp * 8 + fs, 0, False)
    own_blocks = scalars[OWN : OWN + 2]

    gains = jnp.pad(jnp.stack([gain_attn, gain_ffn], axis=1), ((0, 0), (0, 126)))
    part = call(
        prep_kernel, [sds((ROWS, WIDTH), BF)], [scalars, w_query, w_key, w_value, gains], 0
    )[0][None]
    chunks = pick(scalars, layer_input, (part,))
    x_got = [send(chunks[r], RELAY[r]) for r in range(4)]
    two = join(scalars, part, send(part, STEPS[0]), x_got[:2])
    held0, gu, down = call(
        prep_ffn_kernel,
        [sds((4, ROWS, WIDTH), BF), sds((1, ROWS, UP + OUT), BF), sds((1, 80, D), BF)],
        [scalars, two, send(two, STEPS[1]), w_gate, w_up, w_down, w_output],
        0,
        deps=x_got[2:],
    )
    x = assemble(scalars, x_got, (held0,))
    held1 = send(held0, STEPS[2])
    gu_got, down_got = send(gu, STEPS[0]), send(down, D_STEPS[0])
    other0 = send(held0, CC)
    other1 = send(held1, CC)
    gu, down = grow(scalars, gu, gu_got, down, down_got, False, (held1,))
    gu_got, down_got = send(gu, STEPS[1]), send(down, D_STEPS[1])
    chunks = pick(scalars, cotangent, (held0,))
    g_got = [send(chunks[r], RELAY[r]) for r in range(4)]
    weights = [a.reshape(D // 2, WIDTH) for a in (held0, held1, other0, other1)]

    seg = send(lax.dynamic_index_in_dim(segments, z, 0, False), SEGMENTS)
    index = (own_blocks[:, None] * 256 + jnp.arange(256, dtype=jnp.int32)[None, :]).reshape(TOK)
    seg_own = jnp.concatenate(
        [lax.dynamic_slice_in_dim(seg, own_blocks[j] * 256, 256) for j in range(2)]
    )
    first = jnp.sum((seg[:, None] < seg_own[None, :]).astype(jnp.int32), axis=0)
    pos = (index - first).astype(F32)
    freq = THETA ** (-(jnp.arange(32, dtype=F32) * 2.0) / HDIM)
    angle = freq[:, None] * pos[None, :]
    cosine, sine = jnp.cos(angle), jnp.sin(angle)
    first, index = first[None, :], index[None, :]

    q, kv, ha, hb = call(
        pre_kernel,
        [sds((D, TOK), BF), sds((2 * KVD, TOK), BF), sds((D, TOK), BF), sds((D, TOK), BF)],
        [scalars, x, *weights, cosine, sine],
        2 * TOK * D * 1664,
        [pltpu.VMEM((D, TOK), F32)],
        deps=(gu,),
    )
    kv_other = send(kv, CC)
    gu0, down0, up0 = grow(
        scalars, gu, gu_got, down, down_got, True, (kv, *g_got[:2])
    )
    gu1, down1 = send(gu0, STEPS[2]), send(down0, D_STEPS[2])
    up0_other, down0_other = send(up0, DUP_X), send(down0, DUP_Y)
    o, lse = attention(scalars, q, kv, kv_other, first, index, (gu0,))
    up1, wo_held = call(
        part_kernel,
        [sds((4, ROWS, UP), BF), sds((8, ROWS, OUT), BF)],
        [scalars, gu0, gu1],
        0,
        deps=(o, down1, up0_other, down0_other),
    )
    wo_held = wo_held.reshape(D, OUT)
    wo_other = send(wo_held, CC)
    up1_other, down1_other = send(up1, DUP_X), send(down1, DUP_Y)

    x1, oa, ob, h2, h2_send = call(
        post_kernel,
        [sds((D, TOK), F32)] + [sds((D, TOK), BF)] * 4,
        [scalars, o, wo_held, wo_other, x, *weights],
        2 * TOK * D * 1024,
        [pltpu.VMEM((D, TOK), F32)],
        deps=(*g_got[2:], up1_other, down1_other),
        specs=[SMEM] + [VMEM] * 4 + [GAIN_SPEC] * 4,
    )
    h2_other = send(h2_send, CC)
    g = assemble(scalars, g_got, (h2,))
    g_other = send(g, CC)
    up_weights = [a.reshape(D // 2, UP) for a in (up0, up1, up0_other, up1_other)]
    out_own, out_part, dh_own, dh_part, gu_keep, gu_give, d_keep, d_give = ffn(
        scalars, h2, h2_other, g, g_other, up_weights, [down0, down1, down0_other, down1_other]
    )
    gu_keep = gu_keep.reshape(8, ROWS, 1280)
    gu_got = send(gu_give.reshape(8, ROWS, 1280), DUP_X)
    d_got = send(d_give, DUP_X)
    dh_got = send(dh_part, CC)
    out_got = send(out_part, CC)
    dx1, do, wo_keep, wo_give, gg2 = call(
        mid_kernel,
        [
            sds((D, TOK), F32),
            sds((D, TOK), BF),
            sds((D, 512), BF),
            sds((D, 512), BF),
            sds((D, 128), F32),
        ],
        [scalars, dh_own, dh_got, x1, g, *weights, oa, ob, wo_held, wo_other],
        4 * TOK * D * 1024,
        [pltpu.VMEM((D, TOK), F32)],
        specs=[SMEM] + [VMEM] * 4 + [GAIN_SPEC] * 4 + [VMEM] * 4,
    )
    wo_got = send(wo_give, CC)
    out = call(
        out_kernel, [sds((4, D, 128), BF)], [scalars, x1, out_own, out_got], 0, deps=(do,)
    )[0]

    def from_chip(chunks):
        return [send(chunks[r], RELAY_BACK[r]) for r in range(4)]

    out_got = from_chip(out)
    dq, dko, dkp, dvo, dvp = attention_back(
        scalars, q, kv, kv_other, do, o, lse, first, index, (out,)
    )
    dkv = send(jnp.concatenate([dkp, dvp], axis=0), CC)
    wo_keep, wo_got = (a.reshape(8, ROWS, OUT) for a in (wo_keep, wo_got))
    gu_keep, gu_give, d_keep, d_give = add(
        scalars,
        [[(gu_keep, gu_got), (wo_keep, wo_got)], [(d_keep, d_got)]],
        (dq, *out_got[:2]),
    )
    gu_got, d_got = send(gu_give, STEPS[2]), send(d_give, D_STEPS[2])
    qkv, at_keep, at_give = call(
        last_kernel,
        [sds((1664, TOK), BF), sds((D, WIDTH), BF), sds((D, WIDTH), BF)],
        [scalars, dq, dko, dvo, dkv, cosine, sine, ha, hb],
        2 * TOK * D * 1664,
        deps=(gu_keep,),
    )
    gu_keep, gu_give, d_keep, d_give = add(
        scalars, [[(gu_keep, gu_got)], [(d_keep, d_got)]], (at_keep, *out_got[2:])
    )
    gu_got, d_got = send(gu_give, STEPS[1]), send(d_give, D_STEPS[1])
    at_keep, at_give = (a.reshape(8, ROWS, WIDTH) for a in (at_keep, at_give))
    at_got = send(touch(at_give, (gu_keep,)), CC)
    gin, gains = call(
        input_kernel,
        [sds((4, D, 128), BF), sds((D, 128), BF)],
        [scalars, qkv, x, dx1, *weights, gg2],
        2 * TOK * D * 1664,
        [pltpu.VMEM((D, TOK), F32)],
        deps=(gu_keep,),
    )
    at_keep, at_give, gu_keep, gu_give, d_keep, d_give = call(
        sum_kernel,
        [sds((4, ROWS, WIDTH), BF)] * 2 + [sds((1, ROWS, UP + OUT), BF)] * 2 + [sds((1, 80, D), BF)] * 2,
        [scalars, at_keep, at_got, gains.reshape(8, ROWS, 128), gu_keep, gu_got, d_keep, d_got],
        0,
    )
    at_got, gu_got, d_got = (
        send(at_give, STEPS[2]), send(gu_give, STEPS[0]), send(d_give, D_STEPS[0])
    )
    gin_got = from_chip(gin)
    at_keep, at_give, grad_gu, grad_d = add(
        scalars,
        [[(at_keep, at_got)], [(gu_keep, gu_got)], [(d_keep, d_got)]],
        gin_got[:2],
    )
    at_got = send(at_give, STEPS[1])
    grad_gu, grad_d = grad_gu[0], grad_d[0]

    def sum_over(value, groups):
        n = len(groups[0])
        parts = value.reshape(n, value.shape[0] // n, value.shape[1])
        got = lax.all_to_all(parts, "dp", 0, 0, axis_index_groups=groups)
        return jnp.sum(got.astype(F32), axis=0).astype(BF)

    at = lambda yl, x, c: (yl * 4 + x) * 2 + c
    x_pairs = (((0, 3), (1, 2)), ((0, 1), (2, 3)))
    gu_groups = [
        [at(yl, x, c) for yl in range(2) for x in pair] for c in range(2) for pair in x_pairs[c]
    ]
    all_groups = [list(range(c, 16, 2)) for c in range(2)]
    joined = jnp.concatenate(
        [
            jnp.pad(grad_gu[:, :UP], ((0, 8), (0, 0))).reshape(4, 32, UP),
            jnp.pad(grad_d, ((0, 16), (0, 320))).reshape(4, 24, UP),
        ],
        axis=1,
    )
    pieces = sum_over(joined.reshape(224, UP), gu_groups)

    def share(value):
        mine = lax.all_to_all(
            jnp.broadcast_to(value[None], (8, *value.shape)), "dp", 0, 0, axis_index_groups=all_groups
        )
        other = send(mine, CC)
        return mine, other

    at_keep, at_give = add(scalars, [[(at_keep, at_got)]], (pieces, *gin_got[2:]))
    at_got = send(at_give, STEPS[0])
    mine, other = share(pieces)
    gate, up, down = call(
        functools.partial(grads_kernel, gu_groups),
        [sds((ROWS, 2560), F32), sds((ROWS, 2560), F32), sds((320, D), F32)],
        [scalars, mine, other],
        0,
    )
    (attn,) = add(scalars, [[(at_keep, at_got)]], (mine,))
    attn = jnp.concatenate([attn[0], grad_gu[:, UP:]], axis=1)
    attn = sum_over(jnp.pad(attn, ((0, 8), (0, 0))), all_groups)
    mine, other = share(attn)
    query, key, value, output, gains = call(
        attn_grads_kernel,
        [
            sds((ROWS, D), F32),
            sds((KVD, ROWS), F32),
            sds((KVD, ROWS), F32),
            sds((ROWS, D), F32),
            sds((ROWS, 128), F32),
        ],
        [scalars, mine, other],
        0,
    )
    out_final = finish(scalars, out_got, BF, (pieces,))
    gin_final = finish(scalars, gin_got, F32, (pieces,))

    out_final = jnp.swapaxes(out_final, 1, 2)
    gin_final = jnp.swapaxes(gin_final, 1, 2)

    return (
        out_final,
        gin_final,
        query,
        key.T,
        value.T,
        output,
        gate,
        up,
        down,
        gains[:, 0],
        gains[:, 1],
    )


def solution(mesh):
    rows = P("fsdp", None)
    in_specs = (
        (P("dp", "fsdp", None), P("dp", None))
        + (rows,) * 7
        + (P("fsdp"), P("fsdp"), P("dp", "fsdp", None))
    )
    out_specs = (P("dp", "fsdp", None),) * 2 + (rows,) * 7 + (P("fsdp"), P("fsdp"))
    return jax.shard_map(body, mesh=mesh, in_specs=in_specs, out_specs=out_specs, check_vma=False)
```

```python
import functools

import jax
import jax.numpy as jnp
import numpy as np
from jax import lax
from jax.experimental import pallas as pl
from jax.experimental.pallas import tpu as pltpu
from jax.sharding import PartitionSpec as P

D = 960
H = 15
KVH = 5
HDIM = 64
FF = 2560
KVD = 320
LEN = 1024
EPS = 1e-05
THETA = 100000.0
TOK = 512
ROWS = 120
NEG = -1e30
BF = jnp.bfloat16
F32 = jnp.float32
AXES = ("dp", "fsdp")


def coords(i):
    dp, fs = divmod(i, 8)
    ylo, rest = divmod(dp, 8)
    x, core = divmod(rest, 2)
    yhi, z = divmod(fs, 4)
    return ylo, x, core, yhi, z


def flat(ylo, x, core, yhi, z):
    return ((ylo * 4 + x) * 2 + core) * 8 + yhi * 4 + z


def perm(fn, keep=lambda *a: True):
    return [(i, flat(*fn(*coords(i)))) for i in range(128) if keep(*coords(i))]


Z1 = perm(lambda yl, x, c, yh, z: (yl, x, c, yh, z ^ 1))
Z2 = perm(lambda yl, x, c, yh, z: (yl, x, c, yh, 3 - z))
Y2 = perm(lambda yl, x, c, yh, z: (1 - yl, x, c, 1 - yh, z))
CC = perm(lambda yl, x, c, yh, z: (yl, x, 1 - c, yh, z))
DUP_X = perm(lambda yl, x, c, yh, z: (yl, 3 - x if c else x ^ 1, c, yh, z))


def dup_x(x, core):
    return x >> 1 if core else (x >> 1) ^ (x & 1)


DIMS = (("z1", "z2", "y2"), ("z2", "y2", "z1"))
FLIP = {
    "z1": lambda yl, x, c, yh, z: (yl, x, c, yh, z ^ 1),
    "z2": lambda yl, x, c, yh, z: (yl, x, c, yh, 3 - z),
    "y2": lambda yl, x, c, yh, z: (1 - yl, x, c, 1 - yh, z),
}
STEPS = [perm(lambda yl, x, c, yh, z, k=k: FLIP[DIMS[c][k]](yl, x, c, yh, z)) for k in range(3)]
D_STEPS = [Y2, Z1, Z2]
D_BACK = [Z2, Y2, Z1]
GRAY = (0, 1, 3, 2)

CORE_OF = (0, 0, 1, 1, 1, 1, 0, 0)
RANK_OF = (0, 1, 0, 1, 2, 3, 2, 3)


AT = (lambda z: z, lambda z: z ^ 1, lambda z: 3 - z, lambda z: (z + 2) % 4)
RELAY = [
    perm(lambda yl, x, c, yh, z, r=r: (1 - yl, x, CORE_OF[yh * 4 + z], c, AT[r](z)))
    for r in range(4)
]
RELAY_BACK = [[(b, a) for a, b in pairs] for pairs in RELAY]
SEGMENTS = perm(lambda yl, x, c, yh, z: (1 - yl, x, yh, c, z))


def send(x, pairs):
    return lax.ppermute(x, AXES, pairs)


def nn(a, b):
    return lax.dot_general(a, b, (((1,), (0,)), ((), ())), preferred_element_type=F32)


def nt(a, b):
    return lax.dot_general(a, b, (((1,), (1,)), ((), ())), preferred_element_type=F32)


def tn(a, b):
    return lax.dot_general(a, b, (((0,), (0,)), ((), ())), preferred_element_type=F32)


def cost(flops, nbytes, trans=0):
    return pl.CostEstimate(flops=int(flops), bytes_accessed=int(nbytes), transcendentals=int(trans))


VMEM = pl.BlockSpec(memory_space=pltpu.VMEM)
SMEM = pl.BlockSpec(memory_space=pltpu.SMEM)
ANY = pl.BlockSpec(memory_space=pl.ANY)


def call(kernel, outs, ins, flops, scratch=(), trans=0, deps=(), specs=None, room=6):
    nbytes = sum(a.size * a.dtype.itemsize for a in ins) + sum(
        a.size * a.dtype.itemsize for a in outs
    )
    limit = int(1.15 * nbytes / 2**20 + room) + 2
    n_in, n_dep = len(ins), len(deps)

    def run(*refs):
        kernel(*refs[:n_in], *refs[n_in + n_dep :])

    return pl.pallas_call(
        run,
        out_shape=outs,
        grid=(1,) if specs else (),
        in_specs=(specs or [SMEM] + [VMEM] * (n_in - 1))
        + [pl.BlockSpec(memory_space=pl.ANY)] * n_dep,
        out_specs=[VMEM] * len(outs),
        scratch_shapes=list(scratch),
        cost_estimate=cost(flops, nbytes, trans),
        compiler_params=pltpu.CompilerParams(vmem_limit_bytes=limit * 1024 * 1024),
    )(*ins, *deps)


def sds(shape, dtype):
    return jax.ShapeDtypeStruct(shape, dtype)


A, B, MINE, OTHER, D_OF, G_OF, SEQ, POS, ROUND, OWN, PAIR, CORE, HALF = (
    0, 8, 16, 24, 32, 40, 48, 52, 56, 60, 62, 64, 65
)


def scalar_table():
    table = np.zeros((128, 66), np.int32)
    for i in range(128):
        yl, x, c, yh, z = coords(i)
        apart = [(s // 4 * 4 + GRAY[s % 4]) ^ (yh * 4 + GRAY[z]) for s in range(8)]
        orders = (apart, [a // 2 + a % 2 * 4 for a in apart])
        slots = [a // 4 + a % 4 * 2 for a in apart]
        back = [a % 2 * 4 + a // 4 * 2 + a // 2 % 2 for a in apart]
        senders = [[h * 4 + AT[r](z) for h in range(2)] for r in range(4)]
        places = [RANK_OF[q] for pair in senders for q in pair if CORE_OF[q] == c]
        table[i] = (
            orders[0]
            + orders[1]
            + orders[c]
            + orders[1 - c]
            + [slots.index(k) for k in range(8)]
            + [back.index(k) for k in range(8)]
            + [AT[r](z) for r in range(4)]
            + places
            + [places.index(k) for k in range(4)]
            + ([1, 2, 0, 3] if c else [0, 3, 1, 2])
            + [c, dup_x(x, c)]
        )
    return table


def to_slots(scalars, base, scratch, value):
    for s in range(8):
        at = pl.multiple_of(scalars[base + s] * ROWS, 8)
        scratch[pl.ds(at, ROWS), : value.shape[1]] = value[s * ROWS : (s + 1) * ROWS]
    return scratch[:, : value.shape[1]]


def from_slots(scalars, base, scratch, value):
    scratch[:, : value.shape[1]] = value
    return jnp.concatenate(
        [
            scratch[pl.ds(pl.multiple_of(scalars[base + s] * ROWS, 8), ROWS), : value.shape[1]]
            for s in range(8)
        ],
        axis=0,
    )


def join_kernel(scalars, a, b, out):
    n = a.shape[0]
    out[:n] = a[...]
    out[n:] = b[...]


def join(scalars, a, b, deps=()):
    shape = (2 * a.shape[0], *a.shape[1:])
    return call(join_kernel, [sds(shape, a.dtype)], [scalars, a, b], 0, deps=deps)[0]


def add_kernel(shape, scalars, *refs):
    outs = list(refs[sum(sum(group) for group in shape) :])
    at = 0
    for group in shape:
        totals = []
        for count in group:
            total = refs[at][...].astype(F32)
            for k in range(1, count):
                total = total + refs[at + k][...].astype(F32)
            at += count
            totals.append(total.astype(BF))
        total = totals[0] if len(totals) == 1 else jnp.concatenate(totals, axis=-1)
        half = total.shape[0] // 2
        if half:
            outs.pop(0)[...] = total[:half]
            outs.pop(0)[...] = total[half:]
        else:
            outs.pop(0)[...] = total


def add(scalars, groups, deps=()):
    outs = []
    for group in groups:
        n = group[0][0].shape[0]
        shape = (*group[0][0].shape[1:-1], sum(terms[0].shape[-1] for terms in group))
        outs += [sds((n // 2, *shape), BF)] * 2 if n > 1 else [sds((n, *shape), BF)]
    return call(
        functools.partial(add_kernel, [[len(terms) for terms in group] for group in groups]),
        outs,
        [scalars, *[a for group in groups for terms in group for a in terms]],
        0,
        deps=deps,
    )


def touch_kernel(value, *refs):
    pass


def touch(value, deps):
    return pl.pallas_call(
        touch_kernel,
        out_shape=sds(value.shape, value.dtype),
        in_specs=[ANY] * (1 + len(deps)),
        out_specs=ANY,
        input_output_aliases={0: 0},
    )(value, *deps)


def pick_kernel(scalars, value, *outs):
    for r, ref in enumerate(outs):
        ref[...] = value[scalars[SEQ + r]]


def pick(scalars, value, deps=()):
    value = jnp.swapaxes(value, 1, 2)
    return call(pick_kernel, [sds((D, 128), BF)] * 4, [scalars, value], 0, deps=deps)


def assemble_kernel(scalars, r0, r1, r2, r3, out):
    for r, ref in enumerate((r0, r1, r2, r3)):
        out[:, pl.ds(pl.multiple_of(scalars[POS + r] * 128, 128), 128)] = ref[...]


def assemble(scalars, got, deps=()):
    return call(assemble_kernel, [sds((D, TOK), BF)], [scalars, *got], 0, deps=deps)[0]


def store_chunks(scalars, out, value):
    for k in range(4):
        out[scalars[ROUND + k]] = value[:, k * 128 : (k + 1) * 128]


def finish_kernel(scalars, r0, r1, r2, r3, out):
    for r, ref in enumerate((r0, r1, r2, r3)):
        out[scalars[SEQ + r]] = ref[...].astype(out.dtype)


def finish(scalars, got, dtype, deps=()):
    return call(finish_kernel, [sds((4, D, 128), dtype)], [scalars, *got], 0, deps=deps)[0]


def rope(value, cosine, sine):
    parts = []
    for h in range(value.shape[0] // HDIM):
        first = value[h * HDIM : h * HDIM + 32]
        second = value[h * HDIM + 32 : (h + 1) * HDIM]
        parts += [first * cosine - second * sine, second * cosine + first * sine]
    return jnp.concatenate(parts, axis=0)


def by_core(scalars, held, other):
    zero = scalars[CORE] == 0
    return jnp.where(zero, held, other), jnp.where(zero, other, held)


def rows_of(first, second):
    return jnp.concatenate([first[...], second[...]], axis=0)


WIDTH = 896
GAIN_SPEC = pl.BlockSpec((D // 2, 128), lambda i: (0, 6))
UP, OUT = 1280, 512


def prep_kernel(scalars, wq, wk, wv, gains, out):
    zero = lax.broadcasted_iota(jnp.int32, (1, 1), 0) + scalars[CORE] == 0
    out[...] = jnp.where(
        zero,
        jnp.concatenate([wq[:, :768], gains[...]], axis=1),
        jnp.concatenate([wq[:, 768:], wk[...].T, wv[...].T, jnp.zeros((ROWS, 64), BF)], axis=1),
    )


def columns_of(w, core, half):
    at = [320 * s + 160 * core + 80 * half for s in range(8)]
    return [w[:, a : a + 80] for a in at]


def prep_ffn_kernel(scalars, two, got, wg, wu, wd, wo, held, gu, down):
    join_kernel(scalars, two, got, held)
    one = lax.broadcasted_iota(jnp.int32, (1, 1), 0)
    zero, first = one + scalars[CORE] == 0, one + scalars[HALF] == 0
    gate, up = wg[...], wu[...]
    options = [
        [
            jnp.concatenate(columns_of(gate, c, h) + columns_of(up, c, h), axis=1)
            for h in range(2)
        ]
        for c in range(2)
    ]
    gu[0, :, :UP] = jnp.where(
        zero,
        jnp.where(first, options[0][0], options[0][1]),
        jnp.where(first, options[1][0], options[1][1]),
    )
    rest = jnp.concatenate([wo[:, OUT:], jnp.zeros((ROWS, 64), BF)], axis=1)
    gu[0, :, UP:] = jnp.where(zero, wo[:, :OUT], rest)
    at = pl.multiple_of(scalars[CORE] * 160 + scalars[HALF] * 80, 16)
    down[0] = wd[pl.ds(at, 80), :]


def grow_kernel(scalars, gu, gu_got, down, down_got, gu_out, down_out, *only):
    n = gu.shape[0]
    gu_out[:n] = gu[...]
    gu_out[n:] = gu_got[...]
    down_out[:n] = down[...]
    down_out[n:] = down_got[...]
    for ref in only:
        ref[:n] = gu[:, :, :UP]
        ref[n:] = gu_got[:, :, :UP]


def grow(scalars, gu, gu_got, down, down_got, last, deps):
    outs = [sds((2 * a.shape[0], *a.shape[1:]), BF) for a in (gu, down)]
    if last:
        outs.append(sds((2 * gu.shape[0], ROWS, UP), BF))
    return call(grow_kernel, outs, [scalars, gu, gu_got, down, down_got], 0, deps=deps)


def part_kernel(scalars, gu0, gu1, up1, wo):
    up1[...] = gu1[:, :, :UP]
    wo[:4] = gu0[:, :, UP:]
    wo[4:] = gu1[:, :, UP:]


def pre_kernel(scalars, x, h0, h1, o0, o1, cos, sin, q_out, kv_out, ha_out, hb_out, scr):
    wa, wb = by_core(scalars, rows_of(h0, h1), rows_of(o0, o1))
    xv = x[...].astype(F32)
    r1 = lax.rsqrt(jnp.mean(xv * xv, axis=0, keepdims=True) + EPS)
    ha = (to_slots(scalars, A, scr, xv * r1) * wa[:, 768:769].astype(F32)).astype(BF)
    hb = to_slots(scalars, B, scr, from_slots(scalars, A, scr, ha.astype(F32))).astype(BF)
    ha_out[...] = ha
    hb_out[...] = hb
    cosine, sine = cos[...], sin[...]
    q0 = rope(tn(wa[:, :768], ha), cosine, sine)
    q_out[0:768, :] = (q0.astype(BF).astype(F32) * 0.125).astype(BF)
    rest = tn(wb, hb)
    q1 = rope(rest[:192], cosine, sine)
    q_out[768:960, :] = (q1.astype(BF).astype(F32) * 0.125).astype(BF)
    kv_out[0:320, :] = rope(rest[192:512], cosine, sine).astype(BF)
    kv_out[320:640, :] = rest[512:832].astype(BF)


def place_keys(scalars, out, own, other):
    for j in range(2):
        lo = j * 256
        out[:, pl.ds(pl.multiple_of(scalars[OWN + j] * 256, 256), 256)] = own[:, lo : lo + 256]
        out[:, pl.ds(pl.multiple_of(scalars[PAIR + j] * 256, 256), 256)] = other[:, lo : lo + 256]


def allowed(first, index, lo, keys):
    key = lax.broadcasted_iota(jnp.int32, (keys, 256), 0)
    return (key >= first[:, lo : lo + 256]) & (key <= index[:, lo : lo + 256])


def attn_kernel(scalars, q, ko, kp, vo, vp, first, index, o_out, lse_out, kscr, vscr):
    place_keys(scalars, kscr, ko, kp)
    place_keys(scalars, vscr, vo, vp)
    for j, keys in enumerate((512, 1024)):
        lo = j * 256
        ok = allowed(first[...], index[...], lo, keys)
        for h in range(3):
            s = tn(kscr[:, :keys], q[h * HDIM : (h + 1) * HDIM, lo : lo + 256])
            s = jnp.where(ok, s, NEG)
            top = jnp.max(s, axis=0, keepdims=True)
            p = jnp.exp(s - top)
            total = jnp.sum(p, axis=0, keepdims=True)
            o = nn(vscr[:, :keys], p.astype(BF)) / total
            o_out[h * HDIM : (h + 1) * HDIM, lo : lo + 256] = o.astype(BF)
            lse_out[0, h : h + 1, lo : lo + 256] = top + jnp.log(total)


def group_spec(rows):
    return pl.BlockSpec((rows, TOK), lambda g, *_: (g, 0))


def value_spec():
    return pl.BlockSpec((HDIM, TOK), lambda g, *_: (KVH + g, 0))


def row_spec():
    return pl.BlockSpec((1, TOK), lambda g, *_: (0, 0))


def skip(kernel, first, count):
    def run(*refs):
        kernel(*refs[:first], *refs[first + count :])

    return run


def attention(scalars, q, kv_own, kv_other, first, index, deps):
    return pl.pallas_call(
        skip(attn_kernel, 8, len(deps)),
        out_shape=[sds((D, TOK), BF), sds((KVH, 8, TOK), F32)],
        grid=(KVH,),
        in_specs=[
            SMEM,
            group_spec(192),
            group_spec(HDIM),
            group_spec(HDIM),
            value_spec(),
            value_spec(),
            row_spec(),
            row_spec(),
        ]
        + [ANY] * len(deps),
        out_specs=[group_spec(192), pl.BlockSpec((1, 8, TOK), lambda g: (g, 0, 0))],
        scratch_shapes=[pltpu.VMEM((HDIM, LEN), BF), pltpu.VMEM((HDIM, LEN), BF)],
        cost_estimate=cost(12e9, 6e6, 6e6),
        compiler_params=pltpu.CompilerParams(vmem_limit_bytes=12 * 1024 * 1024),
    )(scalars, q, kv_own, kv_other, kv_own, kv_other, first, index, *deps)


def attn_back_kernel(
    scalars, q, ko, kp, vo, vp, do, o, lse, first, index, dq_out, dko, dkp, dvo, dvp, kscr, vscr, dk, dv
):
    place_keys(scalars, kscr, ko, kp)
    place_keys(scalars, vscr, vo, vp)
    for j, keys in ((1, 1024), (0, 512)):
        lo = j * 256
        ok = allowed(first[...], index[...], lo, keys)
        dkt, dvt = None, None
        for h in range(3):
            rows = slice(h * HDIM, (h + 1) * HDIM)
            qh, doh = q[rows, lo : lo + 256], do[rows, lo : lo + 256]
            delta = jnp.sum(
                doh.astype(F32) * o[rows, lo : lo + 256].astype(F32), axis=0, keepdims=True
            )
            s = tn(kscr[:, :keys], qh)
            p = jnp.exp(jnp.where(ok, s - lse[0, h : h + 1, lo : lo + 256], NEG))
            dp = tn(vscr[:, :keys], doh)
            ds = (p * (dp - delta)).astype(BF)
            dq_out[rows, lo : lo + 256] = nn(kscr[:, :keys], ds) * 0.125
            a, b = nt(qh, ds), nt(doh, p.astype(BF))
            dkt = a if dkt is None else dkt + a
            dvt = b if dvt is None else dvt + b
        if j == 1:
            dk[...] = dkt
            dv[...] = dvt
        else:
            dk[:, :512] += dkt
            dv[:, :512] += dvt
    for j in range(2):
        lo = j * 256
        own = pl.ds(pl.multiple_of(scalars[OWN + j] * 256, 256), 256)
        other = pl.ds(pl.multiple_of(scalars[PAIR + j] * 256, 256), 256)
        dko[:, lo : lo + 256] = dk[:, own].astype(BF)
        dkp[:, lo : lo + 256] = dk[:, other].astype(BF)
        dvo[:, lo : lo + 256] = dv[:, own].astype(BF)
        dvp[:, lo : lo + 256] = dv[:, other].astype(BF)


def attention_back(scalars, q, kv_own, kv_other, do, o, lse, first, index, deps):
    return pl.pallas_call(
        skip(attn_back_kernel, 11, len(deps)),
        out_shape=[sds((D, TOK), F32)] + [sds((KVD, TOK), BF)] * 4,
        grid=(KVH,),
        in_specs=[
            SMEM,
            group_spec(192),
            group_spec(HDIM),
            group_spec(HDIM),
            value_spec(),
            value_spec(),
            group_spec(192),
            group_spec(192),
            pl.BlockSpec((1, 8, TOK), lambda g: (g, 0, 0)),
            row_spec(),
            row_spec(),
        ]
        + [ANY] * len(deps),
        out_specs=[group_spec(192)] + [group_spec(HDIM)] * 4,
        scratch_shapes=[
            pltpu.VMEM((HDIM, LEN), BF),
            pltpu.VMEM((HDIM, LEN), BF),
            pltpu.VMEM((HDIM, LEN), F32),
            pltpu.VMEM((HDIM, LEN), F32),
        ],
        cost_estimate=cost(30e9, 10e6, 6e6),
        compiler_params=pltpu.CompilerParams(vmem_limit_bytes=16 * 1024 * 1024),
    )(scalars, q, kv_own, kv_other, kv_own, kv_other, do, o, lse, first, index, *deps)


def gain_of(scalars, scr, gains, column):
    gains = by_core(scalars, rows_of(*gains[:2]), rows_of(*gains[2:]))[0]
    return from_slots(scalars, A, scr, gains.astype(F32))[:, column : column + 1]


def post_kernel(
    scalars, o, ho, oo, x, g0, g1, g2, g3, x1_out, oa_out, ob_out, h2_out, h2_send, scr
):
    of = o[...].astype(F32)
    wo0, wo1 = by_core(scalars, ho[...], oo[...])
    oa = to_slots(scalars, A, scr, of).astype(BF)
    ob = to_slots(scalars, B, scr, of).astype(BF)
    oa_out[...] = oa
    ob_out[...] = ob
    x1 = x[...].astype(F32) + jnp.concatenate([tn(wo0, oa), tn(wo1, ob)[:448]], axis=0)
    x1_out[...] = x1
    r2 = lax.rsqrt(jnp.mean(x1 * x1, axis=0, keepdims=True) + EPS)
    h2 = x1 * r2 * gain_of(scalars, scr, (g0, g1, g2, g3), 1)
    h2_out[...] = to_slots(scalars, MINE, scr, h2).astype(BF)
    h2_send[...] = to_slots(scalars, OTHER, scr, h2).astype(BF)


HID = 640


def ffn_kernel(more, scalars, h2o, h2p, go, gp, w0, w1, d0, d1, *refs):
    before, refs = refs[: 4 * more], refs[4 * more :]
    out_o, out_p, dh_o, dh_p, grad_w, grad_d, wd, gd = refs

    def rows_at(table, k):
        return pl.ds(pl.multiple_of(scalars[table + k] * 80, 16), 80)

    for k in range(8):
        wd[rows_at(D_OF, k), :] = (d0, d1)[k // 4][k % 4]
    w, wdv = rows_of(w0, w1), wd[...]
    h2 = jnp.concatenate([h2o[...], h2p[...]], axis=1)
    g = jnp.concatenate([go[...], gp[...]], axis=1)
    both = tn(w, h2)
    gate, up = both[:HID], both[HID:]
    dhid = nn(wdv, g)
    sig = 1.0 / (1.0 + jnp.exp(-gate))
    silu = gate * sig
    hid = (silu * up).astype(BF)
    dgt = (dhid * up * (sig * (1.0 + gate * (1.0 - sig)))).astype(BF)
    dboth = jnp.concatenate([dgt, (dhid * silu).astype(BF)], axis=0)
    out, dh = tn(wdv, hid), nn(w, dboth)
    if more:
        out = out + jnp.concatenate([before[0][...], before[1][...]], axis=1)
        dh = dh + jnp.concatenate([before[2][...], before[3][...]], axis=1)
    for value, own, other in ((out, out_o, out_p), (dh, dh_o, dh_p)):
        own[...] = value[:, :TOK]
        other[...] = value[:, TOK:].astype(other.dtype)
    grad_w[...] = nt(h2, dboth).astype(BF)
    gd[...] = nt(hid, g).astype(BF)
    for k in range(8):
        grad_d[k] = gd[rows_at(G_OF, k), :]


def ffn(scalars, h2, g, weights, before=(), deps=()):
    part = BF if before else F32
    return call(
        functools.partial(ffn_kernel, bool(before)),
        [sds((D, TOK), F32), sds((D, TOK), part), sds((D, TOK), F32), sds((D, TOK), part)]
        + [sds((D, UP), BF), sds((8, 80, D), BF)],
        [scalars, *h2, *g, *weights, *before],
        2 * 9 * 1024 * D * HID,
        [pltpu.VMEM((HID, D), BF), pltpu.VMEM((HID, D), BF)],
        deps=deps,
        room=18,
    )


def norm_back(dh, source, inv, gain):
    scaled = dh * gain
    total = jnp.sum(scaled * source, axis=0, keepdims=True)
    grad_gain = jnp.sum(dh * source * inv, axis=1, keepdims=True)
    return inv * scaled - source * (inv * inv * inv * total * (1.0 / D)), grad_gain


def mid_kernel(
    scalars, dho, dhr, x1, g, g0, g1, g2, g3, oa, ob, ho, oo,
    dx_out, do_out, keep, give, gg_out, scr,
):
    wo0, wo1 = by_core(scalars, ho[...], oo[...])
    x1v = x1[...]
    r2 = lax.rsqrt(jnp.mean(x1v * x1v, axis=0, keepdims=True) + EPS)
    dh = from_slots(scalars, MINE, scr, dho[...])
    dh = dh + from_slots(scalars, OTHER, scr, dhr[...].astype(F32))
    back, grad_gain = norm_back(dh, x1v, r2, gain_of(scalars, scr, (g0, g1, g2, g3), 1))
    gg_out[...] = jnp.broadcast_to(grad_gain, (D, 128))
    dx = g[...].astype(F32) + back
    dx_out[...] = dx
    low = jnp.concatenate([dx.astype(BF), jnp.zeros((64, TOK), BF)], axis=0)
    gw0 = nt(oa[...], low[:512]).astype(BF)
    gw1 = nt(ob[...], low[512:]).astype(BF)
    keep[...], give[...] = by_core(scalars, gw0, gw1)
    do = from_slots(scalars, A, scr, nn(wo0, low[:512]))
    do_out[...] = (do + from_slots(scalars, B, scr, nn(wo1, low[512:]))).astype(BF)


def out_kernel(scalars, x1, own, got, wo, wo_got, out, wo_keep, wo_give):
    store_chunks(scalars, out, (x1[...] + own[...] + got[...].astype(F32)).astype(BF))
    total = (wo[...].astype(F32) + wo_got[...].astype(F32)).astype(BF)
    wo_keep[...], wo_give[...] = total[:4], total[4:]


def gain1_of(scalars, scr, wa):
    return from_slots(scalars, A, scr, wa[:, 768:896].astype(F32))[:, 0:1]


def last_kernel(scalars, dq, dko, dvo, dkv, cos, sin, ha, hb, qkv, keep, give):
    cosine, sine = cos[...], -sin[...]
    dqp = rope(dq[...], cosine, sine).astype(BF)
    dkp = rope(dko[...].astype(F32) + dkv[:KVD].astype(F32), cosine, sine).astype(BF)
    dvb = (dvo[...].astype(F32) + dkv[KVD:].astype(F32)).astype(BF)
    rest = jnp.concatenate([dqp[768:], dkp, dvb, jnp.zeros((64, TOK), BF)], axis=0)
    qkv[:768] = dqp[:768]
    qkv[768:] = rest
    gwb = nt(hb[...], rest).astype(BF)
    gwa = jnp.concatenate([nt(ha[...], dqp[:768]), jnp.zeros((D, 128), F32)], axis=1).astype(BF)
    keep[...], give[...] = by_core(scalars, gwa, gwb)


def input_kernel(scalars, qkv, x, dx1, h0, h1, o0, o1, gain2, chunks, gains, scr):
    wa, wb = by_core(scalars, rows_of(h0, h1), rows_of(o0, o1))
    dh = from_slots(scalars, A, scr, nn(wa[:, :768], qkv[:768]))
    dh = dh + from_slots(scalars, B, scr, nn(wb, qkv[768:]))
    xv = x[...].astype(F32)
    r1 = lax.rsqrt(jnp.mean(xv * xv, axis=0, keepdims=True) + EPS)
    back, gain1 = norm_back(dh, xv, r1, gain1_of(scalars, scr, wa))
    store_chunks(scalars, chunks, (dx1[...] + back).astype(BF))
    lane = lax.broadcasted_iota(jnp.int32, (D, 128), 1) - scalars[CORE] * 64
    value = jnp.where(lane == 0, gain1, jnp.where(lane == 1, gain2[...], 0.0))
    gains[...] = to_slots(scalars, MINE, scr, value).astype(BF)


def sum_kernel(scalars, keep, got, gains, gu, gu_got, d, d_got, *outs):
    total = keep[...].astype(F32) + got[...].astype(F32)
    last = total[:, :, 768:] + gains[...].astype(F32)
    outs[0][:, :, :768] = total[:4, :, :768].astype(BF)
    outs[0][:, :, 768:] = last[:4].astype(BF)
    outs[1][:, :, :768] = total[4:, :, :768].astype(BF)
    outs[1][:, :, 768:] = last[4:].astype(BF)
    outs[2][...] = (gu[...].astype(F32) + gu_got[...].astype(F32)).astype(BF)
    value = (d[...].astype(F32) + d_got[...].astype(F32)).astype(BF)
    outs[3][...], outs[4][...] = value[:1], value[1:]


def grads_kernel(groups, scalars, mine, other, gate, up, down):
    pieces = by_core(scalars, mine[...], other[...])
    parts = []
    for c in range(2):
        for half in range(2):
            group = groups[2 * c + 1 - half]
            rows = [pieces[c][d // 2, :32] for d in group]
            parts.append(jnp.concatenate(rows, axis=0)[:ROWS])
            rows = [pieces[c][d // 2, 32:, :D].astype(F32) for d in group]
            at = 160 * c + 80 * half
            down[at : at + 80, :] = jnp.concatenate(rows, axis=0)[:80]
    for lo, ref in ((0, gate), (HID, up)):
        blocks = [p[:, lo + 80 * s : lo + 80 * (s + 1)] for s in range(8) for p in parts]
        ref[...] = jnp.concatenate(blocks, axis=1).astype(F32)


def attn_grads_kernel(scalars, mine, other, query, key, value, output, gains):
    a, b = by_core(scalars, mine[...].astype(F32), other[...].astype(F32))
    a = a.reshape(128, a.shape[2])[:ROWS]
    b = b.reshape(128, b.shape[2])[:ROWS]
    query[:, :768] = a[:, :768]
    query[:, 768:] = b[:, :192]
    key[...] = b[:, 192:512].T
    value[...] = b[:, 512:832].T
    output[:, :OUT] = a[:, WIDTH:]
    output[:, OUT:] = b[:, WIDTH:1344]
    gains[...] = a[:, 768:896] + jnp.concatenate([b[:, 832:896], b[:, 832:896]], axis=1)


def body(
    layer_input,
    segments,
    w_query,
    w_key,
    w_value,
    w_output,
    w_gate,
    w_up,
    w_down,
    gain_attn,
    gain_ffn,
    cotangent,
):
    dp, fs = lax.axis_index("dp"), lax.axis_index("fsdp")
    core, yhi, z = dp % 2, fs // 4, fs % 4
    first_core = core == 0
    scalars = lax.dynamic_index_in_dim(jnp.asarray(scalar_table()), dp * 8 + fs, 0, False)
    own_blocks = scalars[OWN : OWN + 2]

    gains = jnp.pad(jnp.stack([gain_attn, gain_ffn], axis=1), ((0, 0), (0, 126)))
    part = call(
        prep_kernel, [sds((ROWS, WIDTH), BF)], [scalars, w_query, w_key.T, w_value.T, gains], 0
    )[0][None]
    chunks = pick(scalars, layer_input, (part,))
    x_got = [send(chunks[r], RELAY[r]) for r in range(4)]
    two = join(scalars, part, send(part, STEPS[0]), (x_got[0], x_got[3]))
    held0, gu, down = call(
        prep_ffn_kernel,
        [sds((4, ROWS, WIDTH), BF), sds((1, ROWS, UP + OUT), BF), sds((1, 80, D), BF)],
        [scalars, two, send(two, STEPS[1]), w_gate, w_up, w_down, w_output],
        0,
        deps=x_got[1:3],
    )
    x = assemble(scalars, x_got, (held0,))
    held1 = send(held0, STEPS[2])
    gu_got, down_got = send(gu, STEPS[0]), send(down, D_STEPS[0])
    other0 = send(held0, CC)
    other1 = send(held1, CC)
    chunks = pick(scalars, cotangent, (held0,))
    g_got = [send(chunks[r], RELAY[r]) for r in range(4)]
    gu, down = grow(scalars, gu, gu_got, down, down_got, False, (held1, g_got[0]))
    gu_got, down_got = send(gu, STEPS[1]), send(down, D_STEPS[1])
    weights = [a.reshape(D // 2, WIDTH) for a in (held0, held1, other0, other1)]

    seg = send(lax.dynamic_index_in_dim(segments, z, 0, False), SEGMENTS)
    index = (own_blocks[:, None] * 256 + jnp.arange(256, dtype=jnp.int32)[None, :]).reshape(TOK)
    seg_own = jnp.concatenate(
        [lax.dynamic_slice_in_dim(seg, own_blocks[j] * 256, 256) for j in range(2)]
    )
    first = jnp.sum((seg[:, None] < seg_own[None, :]).astype(jnp.int32), axis=0)
    pos = (index - first).astype(F32)
    freq = THETA ** (-(jnp.arange(32, dtype=F32) * 2.0) / HDIM)
    angle = freq[:, None] * pos[None, :]
    cosine, sine = jnp.cos(angle), jnp.sin(angle)
    first, index = first[None, :], index[None, :]

    q, kv, ha, hb = call(
        pre_kernel,
        [sds((D, TOK), BF), sds((2 * KVD, TOK), BF), sds((D, TOK), BF), sds((D, TOK), BF)],
        [scalars, x, *weights, cosine, sine],
        2 * TOK * D * 1664,
        [pltpu.VMEM((D, TOK), F32)],
        deps=(gu,),
    )
    kv_other = send(kv, CC)
    gu0, down0, up0 = grow(
        scalars, gu, gu_got, down, down_got, True, (kv,)
    )
    gu1, down1 = send(gu0, STEPS[2]), send(down0, D_STEPS[2])
    up0_other, down0_other = send(up0, DUP_X), send(down0, DUP_X)
    o, lse = attention(scalars, q, kv, kv_other, first, index, (gu0,))
    up1, wo_held = call(
        part_kernel,
        [sds((4, ROWS, UP), BF), sds((8, ROWS, OUT), BF)],
        [scalars, gu0, gu1],
        0,
        deps=(o, up0_other, down0_other, down1, g_got[3]),
    )
    wo_held = wo_held.reshape(D, OUT)
    wo_other = send(wo_held, CC)
    up1_other, down1_other = send(up1, DUP_X), send(down1, DUP_X)

    x1, oa, ob, h2, h2_send = call(
        post_kernel,
        [sds((D, TOK), F32)] + [sds((D, TOK), BF)] * 4,
        [scalars, o, wo_held, wo_other, x, *weights],
        2 * TOK * D * 1024,
        [pltpu.VMEM((D, TOK), F32)],
        deps=g_got[1:3],
        specs=[SMEM] + [VMEM] * 4 + [GAIN_SPEC] * 4,
    )
    h2_other = send(h2_send, CC)
    g = assemble(scalars, g_got, (h2,))
    g_other = send(g, CC)
    up0, up1, up0_other, up1_other = (
        a.reshape(D // 2, UP) for a in (up0, up1, up0_other, up1_other)
    )
    h2, g = (h2, h2_other), (g, g_other)
    *before, gu_give, d_give = ffn(scalars, h2, g, (up0, up1, down0, down1))
    gu_got = send(gu_give.reshape(8, ROWS, UP), DUP_X)
    out_own, out_part, dh_own, dh_part, gu_keep, d_keep = ffn(
        scalars, h2, g, (up0_other, up1_other, down0_other, down1_other), before
    )
    d_got = send(touch(d_give, (dh_part,)), DUP_X)
    gu_keep = gu_keep.reshape(8, ROWS, UP)
    g = g[0]
    dh_got = send(dh_part, CC)
    out_got = send(out_part, CC)
    dx1, do, wo_keep, wo_give, gg2 = call(
        mid_kernel,
        [
            sds((D, TOK), F32),
            sds((D, TOK), BF),
            sds((D, 512), BF),
            sds((D, 512), BF),
            sds((D, 128), F32),
        ],
        [scalars, dh_own, dh_got, x1, g, *weights, oa, ob, wo_held, wo_other],
        4 * TOK * D * 1024,
        [pltpu.VMEM((D, TOK), F32)],
        room=10,
        specs=[SMEM] + [VMEM] * 4 + [GAIN_SPEC] * 4 + [VMEM] * 4,
    )
    wo_got = send(wo_give, CC)
    gu_keep, gu_give = add(scalars, [[(gu_keep, gu_got)]], (do,))
    gu_got = send(gu_give, STEPS[2])
    out, wo_keep, wo_give = call(
        out_kernel,
        [sds((4, D, 128), BF)] + [sds((4, ROWS, OUT), BF)] * 2,
        [scalars, x1, out_own, out_got]
        + [a.reshape(8, ROWS, OUT) for a in (wo_keep, wo_got)],
        0,
        deps=(gu_keep,),
    )
    wo_got = send(wo_give, STEPS[2])

    def from_chip(chunks):
        return [send(chunks[r], RELAY_BACK[r]) for r in range(4)]

    out_got = from_chip(out)
    dq, dko, dkp, dvo, dvp = attention_back(
        scalars, q, kv, kv_other, do, o, lse, first, index, (out,)
    )
    dkv = send(jnp.concatenate([dkp, dvp], axis=0), CC)
    gu_keep, gu_give, d_keep, d_give = add(
        scalars,
        [[(gu_keep, gu_got), (wo_keep, wo_got)], [(d_keep, d_got)]],
        (dq, out_got[0], out_got[2]),
    )
    gu_got, d_got = send(gu_give, STEPS[1]), send(d_give, D_BACK[2])
    qkv, at_keep, at_give = call(
        last_kernel,
        [sds((1664, TOK), BF), sds((D, WIDTH), BF), sds((D, WIDTH), BF)],
        [scalars, dq, dko, dvo, dkv, cosine, sine, ha, hb],
        2 * TOK * D * 1664,
        deps=(gu_keep,),
    )
    gu_keep, gu_give, d_keep, d_give = add(
        scalars, [[(gu_keep, gu_got)], [(d_keep, d_got)]], (at_keep, out_got[3])
    )
    gu_got, d_got = send(gu_give, STEPS[0]), send(d_give, D_BACK[1])
    at_keep, at_give = (a.reshape(8, ROWS, WIDTH) for a in (at_keep, at_give))
    at_got = send(touch(at_give, (gu_keep,)), CC)
    gin, gains = call(
        input_kernel,
        [sds((4, D, 128), BF), sds((D, 128), BF)],
        [scalars, qkv, x, dx1, *weights, gg2],
        2 * TOK * D * 1664,
        [pltpu.VMEM((D, TOK), F32)],
        room=10,
        deps=(gu_keep,),
    )
    at_keep, at_give, grad_gu, d_keep, d_give = call(
        sum_kernel,
        [sds((4, ROWS, WIDTH), BF)] * 2 + [sds((1, ROWS, UP + OUT), BF)] + [sds((1, 80, D), BF)] * 2,
        [scalars, at_keep, at_got, gains.reshape(8, ROWS, 128), gu_keep, gu_got, d_keep, d_got],
        0,
        deps=(out_got[1],),
    )
    at_got, d_got = send(at_give, STEPS[2]), send(d_give, D_BACK[0])
    gin_got = from_chip(gin)
    out_final = finish(scalars, out_got, BF, (at_keep,))
    at_keep, at_give, grad_d = add(
        scalars, [[(at_keep, at_got)], [(d_keep, d_got)]], (gin_got[0], gin_got[2], out_final)
    )
    at_got = send(at_give, STEPS[1])
    at_keep, at_give = add(scalars, [[(at_keep, at_got)]], (gin_got[1], gin_got[3]))
    at_got = send(at_give, STEPS[0])
    grad_gu, grad_d = grad_gu[0], touch(grad_d, (at_keep,))[0]

    def sum_over(value, groups):
        n = len(groups[0])
        parts = value.reshape(n, value.shape[0] // n, value.shape[1])
        got = lax.all_to_all(parts, "dp", 0, 0, axis_index_groups=groups)
        return jnp.sum(got.astype(F32), axis=0).astype(BF)

    at = lambda yl, x, c: (yl * 4 + x) * 2 + c
    x_pairs = (((0, 3), (1, 2)), ((0, 1), (2, 3)))
    gu_groups = [
        [at(yl, x, c) for yl in range(2) for x in pair] for c in range(2) for pair in x_pairs[c]
    ]
    all_groups = [list(range(c, 16, 2)) for c in range(2)]
    joined = jnp.concatenate(
        [
            jnp.pad(grad_gu[:, :UP], ((0, 8), (0, 0))).reshape(4, 32, UP),
            jnp.pad(grad_d, ((0, 16), (0, 320))).reshape(4, 24, UP),
        ],
        axis=1,
    )
    pieces = sum_over(joined.reshape(224, UP), gu_groups)

    (attn,) = add(scalars, [[(at_keep, at_got)]], (pieces,))
    attn = jnp.concatenate([attn[0], grad_gu[:, UP:]], axis=1)
    attn = jnp.pad(attn, ((0, 8), (0, 0))).reshape(8, 16, WIDTH + OUT)
    pieces = jnp.pad(pieces, ((0, 0), (0, WIDTH + OUT - UP)))
    both = jnp.concatenate([jnp.broadcast_to(pieces[None], (8, *pieces.shape)), attn], axis=1)
    both = lax.all_to_all(both, "dp", 0, 0, axis_index_groups=all_groups)
    attn = jnp.sum(both[:, 56:].astype(F32), axis=0).astype(BF)
    gin_final = finish(scalars, gin_got, F32, (attn,))
    mine = both[:, :56, :UP]
    other = send(mine, CC)
    gate, up, down = call(
        functools.partial(grads_kernel, gu_groups),
        [sds((ROWS, 2560), F32), sds((ROWS, 2560), F32), sds((320, D), F32)],
        [scalars, mine, other],
        0,
    )
    mine = lax.all_to_all(
        jnp.broadcast_to(attn[None], (8, *attn.shape)), "dp", 0, 0, axis_index_groups=all_groups
    )
    other = send(mine, CC)
    query, key, value, output, gains = call(
        attn_grads_kernel,
        [
            sds((ROWS, D), F32),
            sds((KVD, ROWS), F32),
            sds((KVD, ROWS), F32),
            sds((ROWS, D), F32),
            sds((ROWS, 128), F32),
        ],
        [scalars, mine, other],
        0,
    )
    out_final = jnp.swapaxes(out_final, 1, 2)
    gin_final = jnp.swapaxes(gin_final, 1, 2)

    return (
        out_final,
        gin_final,
        query,
        key.T,
        value.T,
        output,
        gate,
        up,
        down,
        gains[:, 0],
        gains[:, 1],
    )


def solution(mesh):
    rows = P("fsdp", None)
    in_specs = (
        (P("dp", "fsdp", None), P("dp", None))
        + (rows,) * 7
        + (P("fsdp"), P("fsdp"), P("dp", "fsdp", None))
    )
    out_specs = (P("dp", "fsdp", None),) * 2 + (rows,) * 7 + (P("fsdp"), P("fsdp"))
    return jax.shard_map(body, mesh=mesh, in_specs=in_specs, out_specs=out_specs, check_vma=False)
```

```python
import functools

import jax
import jax.numpy as jnp
import numpy as np
from jax import lax
from jax.experimental import pallas as pl
from jax.experimental.pallas import tpu as pltpu
from jax.sharding import PartitionSpec as P

D = 960
H = 15
KVH = 5
HDIM = 64
FF = 2560
KVD = 320
LEN = 1024
EPS = 1e-05
THETA = 100000.0
TOK = 512
ROWS = 120
NEG = -1e30
BF = jnp.bfloat16
F32 = jnp.float32
AXES = ("dp", "fsdp")


def coords(i):
    dp, fs = divmod(i, 8)
    ylo, rest = divmod(dp, 8)
    x, core = divmod(rest, 2)
    yhi, z = divmod(fs, 4)
    return ylo, x, core, yhi, z


def flat(ylo, x, core, yhi, z):
    return ((ylo * 4 + x) * 2 + core) * 8 + yhi * 4 + z


def perm(fn, keep=lambda *a: True):
    return [(i, flat(*fn(*coords(i)))) for i in range(128) if keep(*coords(i))]


Z1 = perm(lambda yl, x, c, yh, z: (yl, x, c, yh, z ^ 1))
Z2 = perm(lambda yl, x, c, yh, z: (yl, x, c, yh, 3 - z))
Y2 = perm(lambda yl, x, c, yh, z: (1 - yl, x, c, 1 - yh, z))
CC = perm(lambda yl, x, c, yh, z: (yl, x, 1 - c, yh, z))
DUP_X = perm(lambda yl, x, c, yh, z: (yl, 3 - x if c else x ^ 1, c, yh, z))


def dup_x(x, core):
    return x >> 1 if core else (x >> 1) ^ (x & 1)


DIMS = (("z1", "z2", "y2"), ("z2", "y2", "z1"))
FLIP = {
    "z1": lambda yl, x, c, yh, z: (yl, x, c, yh, z ^ 1),
    "z2": lambda yl, x, c, yh, z: (yl, x, c, yh, 3 - z),
    "y2": lambda yl, x, c, yh, z: (1 - yl, x, c, 1 - yh, z),
}
STEPS = [perm(lambda yl, x, c, yh, z, k=k: FLIP[DIMS[c][k]](yl, x, c, yh, z)) for k in range(3)]
D_STEPS = [Y2, Z1, Z2]
D_BACK = [Z2, Y2, Z1]
GRAY = (0, 1, 3, 2)

CORE_OF = (0, 0, 1, 1, 1, 1, 0, 0)
RANK_OF = (0, 1, 0, 1, 2, 3, 2, 3)


AT = (lambda z: z, lambda z: z ^ 1, lambda z: 3 - z, lambda z: (z + 2) % 4)
RELAY = [
    perm(lambda yl, x, c, yh, z, r=r: (1 - yl, x, CORE_OF[yh * 4 + z], c, AT[r](z)))
    for r in range(4)
]
RELAY_BACK = [[(b, a) for a, b in pairs] for pairs in RELAY]
SEGMENTS = perm(lambda yl, x, c, yh, z: (1 - yl, x, yh, c, z))


def send(x, pairs):
    return lax.ppermute(x, AXES, pairs)


def nn(a, b):
    return lax.dot_general(a, b, (((1,), (0,)), ((), ())), preferred_element_type=F32)


def nt(a, b):
    return lax.dot_general(a, b, (((1,), (1,)), ((), ())), preferred_element_type=F32)


def tn(a, b):
    return lax.dot_general(a, b, (((0,), (0,)), ((), ())), preferred_element_type=F32)


def cost(flops, nbytes, trans=0):
    return pl.CostEstimate(flops=int(flops), bytes_accessed=int(nbytes), transcendentals=int(trans))


VMEM = pl.BlockSpec(memory_space=pltpu.VMEM)
SMEM = pl.BlockSpec(memory_space=pltpu.SMEM)
ANY = pl.BlockSpec(memory_space=pl.ANY)


def call(kernel, outs, ins, flops, scratch=(), trans=0, deps=(), specs=None, room=5):
    nbytes = sum(a.size * a.dtype.itemsize for a in ins) + sum(
        a.size * a.dtype.itemsize for a in outs
    )
    limit = int(1.08 * nbytes / 2**20 + room) + 2
    n_in, n_dep = len(ins), len(deps)

    def run(*refs):
        kernel(*refs[:n_in], *refs[n_in + n_dep :])

    return pl.pallas_call(
        run,
        out_shape=outs,
        grid=(1,) if specs else (),
        in_specs=(specs or [SMEM] + [VMEM] * (n_in - 1))
        + [pl.BlockSpec(memory_space=pl.ANY)] * n_dep,
        out_specs=[VMEM] * len(outs),
        scratch_shapes=list(scratch),
        cost_estimate=cost(flops, nbytes, trans),
        compiler_params=pltpu.CompilerParams(vmem_limit_bytes=limit * 1024 * 1024),
    )(*ins, *deps)


def sds(shape, dtype):
    return jax.ShapeDtypeStruct(shape, dtype)


A, B, MINE, OTHER, D_OF, G_OF, SEQ, POS, ROUND, OWN, PAIR, CORE, HALF = (
    0, 8, 16, 24, 32, 40, 48, 52, 56, 60, 62, 64, 65
)


def scalar_table():
    table = np.zeros((128, 66), np.int32)
    for i in range(128):
        yl, x, c, yh, z = coords(i)
        apart = [(s // 4 * 4 + GRAY[s % 4]) ^ (yh * 4 + GRAY[z]) for s in range(8)]
        orders = (apart, [a // 2 + a % 2 * 4 for a in apart])
        slots = [a // 4 + a % 4 * 2 for a in apart]
        back = [a % 2 * 4 + a // 4 * 2 + a // 2 % 2 for a in apart]
        senders = [[h * 4 + AT[r](z) for h in range(2)] for r in range(4)]
        places = [RANK_OF[q] for pair in senders for q in pair if CORE_OF[q] == c]
        table[i] = (
            orders[0]
            + orders[1]
            + orders[c]
            + orders[1 - c]
            + [slots.index(k) for k in range(8)]
            + [back.index(k) for k in range(8)]
            + [AT[r](z) for r in range(4)]
            + places
            + [places.index(k) for k in range(4)]
            + ([1, 2, 0, 3] if c else [0, 3, 1, 2])
            + [c, dup_x(x, c)]
        )
    return table


def to_slots(scalars, base, scratch, value):
    for s in range(8):
        at = pl.multiple_of(scalars[base + s] * ROWS, 8)
        scratch[pl.ds(at, ROWS), : value.shape[1]] = value[s * ROWS : (s + 1) * ROWS]
    return scratch[:, : value.shape[1]]


def from_slots(scalars, base, scratch, value):
    scratch[:, : value.shape[1]] = value
    return jnp.concatenate(
        [
            scratch[pl.ds(pl.multiple_of(scalars[base + s] * ROWS, 8), ROWS), : value.shape[1]]
            for s in range(8)
        ],
        axis=0,
    )


def join_kernel(scalars, a, b, out):
    n = a.shape[0]
    out[:n] = a[...]
    out[n:] = b[...]


def join(scalars, a, b, deps=()):
    shape = (2 * a.shape[0], *a.shape[1:])
    return call(join_kernel, [sds(shape, a.dtype)], [scalars, a, b], 0, deps=deps)[0]


def add_kernel(shape, scalars, *refs):
    outs = list(refs[sum(sum(group) for group in shape) :])
    at = 0
    for group in shape:
        totals = []
        for count in group:
            total = refs[at][...].astype(F32)
            for k in range(1, count):
                total = total + refs[at + k][...].astype(F32)
            at += count
            totals.append(total.astype(BF))
        total = totals[0] if len(totals) == 1 else jnp.concatenate(totals, axis=-1)
        half = total.shape[0] // 2
        if half:
            outs.pop(0)[...] = total[:half]
            outs.pop(0)[...] = total[half:]
        else:
            outs.pop(0)[...] = total


def add(scalars, groups, deps=()):
    outs = []
    for group in groups:
        n = group[0][0].shape[0]
        shape = (*group[0][0].shape[1:-1], sum(terms[0].shape[-1] for terms in group))
        outs += [sds((n // 2, *shape), BF)] * 2 if n > 1 else [sds((n, *shape), BF)]
    return call(
        functools.partial(add_kernel, [[len(terms) for terms in group] for group in groups]),
        outs,
        [scalars, *[a for group in groups for terms in group for a in terms]],
        0,
        deps=deps,
    )


def touch_kernel(value, *refs):
    pass


def touch(value, deps):
    return pl.pallas_call(
        touch_kernel,
        out_shape=sds(value.shape, value.dtype),
        in_specs=[ANY] * (1 + len(deps)),
        out_specs=ANY,
        input_output_aliases={0: 0},
    )(value, *deps)


def pick_kernel(scalars, value, *outs):
    for r, ref in enumerate(outs):
        ref[...] = value[scalars[SEQ + r]]


def pick(scalars, value, deps=()):
    value = jnp.swapaxes(value, 1, 2)
    return call(pick_kernel, [sds((D, 128), BF)] * 4, [scalars, value], 0, deps=deps)


def assemble_kernel(scalars, r0, r1, r2, r3, out):
    for r, ref in enumerate((r0, r1, r2, r3)):
        out[:, pl.ds(pl.multiple_of(scalars[POS + r] * 128, 128), 128)] = ref[...]


def assemble(scalars, got, deps=()):
    return call(assemble_kernel, [sds((D, TOK), BF)], [scalars, *got], 0, deps=deps)[0]


def store_chunks(scalars, out, value):
    for k in range(4):
        out[scalars[ROUND + k]] = value[:, k * 128 : (k + 1) * 128]


def finish_kernel(scalars, r0, r1, r2, r3, out):
    for r, ref in enumerate((r0, r1, r2, r3)):
        out[scalars[SEQ + r]] = ref[...].astype(out.dtype)


def finish(scalars, got, dtype, deps=()):
    return call(finish_kernel, [sds((4, D, 128), dtype)], [scalars, *got], 0, deps=deps)[0]


def rope(value, cosine, sine):
    parts = []
    for h in range(value.shape[0] // HDIM):
        first = value[h * HDIM : h * HDIM + 32]
        second = value[h * HDIM + 32 : (h + 1) * HDIM]
        parts += [first * cosine - second * sine, second * cosine + first * sine]
    return jnp.concatenate(parts, axis=0)


def by_core(scalars, held, other):
    zero = scalars[CORE] == 0
    return jnp.where(zero, held, other), jnp.where(zero, other, held)


def rows_of(first, second):
    return jnp.concatenate([first[...], second[...]], axis=0)


WIDTH = 896
GAIN_SPEC = pl.BlockSpec((D // 2, 128), lambda i: (0, 6))
UP, OUT = 1280, 512


def prep_kernel(scalars, wq, wk, wv, gains, out):
    zero = lax.broadcasted_iota(jnp.int32, (1, 1), 0) + scalars[CORE] == 0
    out[...] = jnp.where(
        zero,
        jnp.concatenate([wq[:, :768], gains[...]], axis=1),
        jnp.concatenate([wq[:, 768:], wk[...].T, wv[...].T, jnp.zeros((ROWS, 64), BF)], axis=1),
    )


def columns_of(w, core, half):
    at = [320 * s + 160 * core + 80 * half for s in range(8)]
    return [w[:, a : a + 80] for a in at]


def prep_ffn_kernel(scalars, two, got, wg, wu, wd, wo, held, gu, down):
    join_kernel(scalars, two, got, held)
    one = lax.broadcasted_iota(jnp.int32, (1, 1), 0)
    zero, first = one + scalars[CORE] == 0, one + scalars[HALF] == 0
    gate, up = wg[...], wu[...]
    options = [
        [
            jnp.concatenate(columns_of(gate, c, h) + columns_of(up, c, h), axis=1)
            for h in range(2)
        ]
        for c in range(2)
    ]
    gu[0, :, :UP] = jnp.where(
        zero,
        jnp.where(first, options[0][0], options[0][1]),
        jnp.where(first, options[1][0], options[1][1]),
    )
    rest = jnp.concatenate([wo[:, OUT:], jnp.zeros((ROWS, 64), BF)], axis=1)
    gu[0, :, UP:] = jnp.where(zero, wo[:, :OUT], rest)
    at = pl.multiple_of(scalars[CORE] * 160 + scalars[HALF] * 80, 16)
    down[0] = wd[pl.ds(at, 80), :]


def grow_kernel(scalars, gu, gu_got, down, down_got, gu_out, down_out, *only):
    n = gu.shape[0]
    gu_out[:n] = gu[...]
    gu_out[n:] = gu_got[...]
    down_out[:n] = down[...]
    down_out[n:] = down_got[...]
    for ref in only:
        ref[:n] = gu[:, :, :UP]
        ref[n:] = gu_got[:, :, :UP]


def grow(scalars, gu, gu_got, down, down_got, last, deps):
    outs = [sds((2 * a.shape[0], *a.shape[1:]), BF) for a in (gu, down)]
    if last:
        outs.append(sds((2 * gu.shape[0], ROWS, UP), BF))
    return call(grow_kernel, outs, [scalars, gu, gu_got, down, down_got], 0, deps=deps)


def part_kernel(scalars, gu0, gu1, up1, wo):
    up1[...] = gu1[:, :, :UP]
    wo[:4] = gu0[:, :, UP:]
    wo[4:] = gu1[:, :, UP:]


def pre_kernel(scalars, x, h0, h1, o0, o1, cos, sin, q_out, kv_out, ha_out, hb_out, scr):
    wa, wb = by_core(scalars, rows_of(h0, h1), rows_of(o0, o1))
    xv = x[...].astype(F32)
    r1 = lax.rsqrt(jnp.mean(xv * xv, axis=0, keepdims=True) + EPS)
    ha = (to_slots(scalars, A, scr, xv * r1) * wa[:, 768:769].astype(F32)).astype(BF)
    hb = to_slots(scalars, B, scr, from_slots(scalars, A, scr, ha.astype(F32))).astype(BF)
    ha_out[...] = ha
    hb_out[...] = hb
    cosine, sine = cos[...], sin[...]
    q0 = rope(tn(wa[:, :768], ha), cosine, sine)
    q_out[0:768, :] = (q0.astype(BF).astype(F32) * 0.125).astype(BF)
    rest = tn(wb, hb)
    q1 = rope(rest[:192], cosine, sine)
    q_out[768:960, :] = (q1.astype(BF).astype(F32) * 0.125).astype(BF)
    kv_out[0:320, :] = rope(rest[192:512], cosine, sine).astype(BF)
    kv_out[320:640, :] = rest[512:832].astype(BF)


def place_keys(scalars, out, own, other):
    for j in range(2):
        lo = j * 256
        out[:, pl.ds(pl.multiple_of(scalars[OWN + j] * 256, 256), 256)] = own[:, lo : lo + 256]
        out[:, pl.ds(pl.multiple_of(scalars[PAIR + j] * 256, 256), 256)] = other[:, lo : lo + 256]


def allowed(first, index, lo, keys):
    key = lax.broadcasted_iota(jnp.int32, (keys, 256), 0)
    return (key >= first[:, lo : lo + 256]) & (key <= index[:, lo : lo + 256])


def attn_kernel(scalars, q, ko, kp, vo, vp, first, index, o_out, lse_out, kscr, vscr):
    place_keys(scalars, kscr, ko, kp)
    place_keys(scalars, vscr, vo, vp)
    for j, keys in enumerate((512, 1024)):
        lo = j * 256
        ok = allowed(first[...], index[...], lo, keys)
        for h in range(3):
            s = tn(kscr[:, :keys], q[h * HDIM : (h + 1) * HDIM, lo : lo + 256])
            s = jnp.where(ok, s, NEG)
            top = jnp.max(s, axis=0, keepdims=True)
            p = jnp.exp(s - top)
            total = jnp.sum(p, axis=0, keepdims=True)
            o = nn(vscr[:, :keys], p.astype(BF)) / total
            o_out[h * HDIM : (h + 1) * HDIM, lo : lo + 256] = o.astype(BF)
            lse_out[0, h : h + 1, lo : lo + 256] = top + jnp.log(total)


def group_spec(rows):
    return pl.BlockSpec((rows, TOK), lambda g, *_: (g, 0))


def value_spec():
    return pl.BlockSpec((HDIM, TOK), lambda g, *_: (KVH + g, 0))


def row_spec():
    return pl.BlockSpec((1, TOK), lambda g, *_: (0, 0))


def skip(kernel, first, count):
    def run(*refs):
        kernel(*refs[:first], *refs[first + count :])

    return run


def attention(scalars, q, kv_own, kv_other, first, index, deps):
    return pl.pallas_call(
        skip(attn_kernel, 8, len(deps)),
        out_shape=[sds((D, TOK), BF), sds((KVH, 8, TOK), F32)],
        grid=(KVH,),
        in_specs=[
            SMEM,
            group_spec(192),
            group_spec(HDIM),
            group_spec(HDIM),
            value_spec(),
            value_spec(),
            row_spec(),
            row_spec(),
        ]
        + [ANY] * len(deps),
        out_specs=[group_spec(192), pl.BlockSpec((1, 8, TOK), lambda g: (g, 0, 0))],
        scratch_shapes=[pltpu.VMEM((HDIM, LEN), BF), pltpu.VMEM((HDIM, LEN), BF)],
        cost_estimate=cost(12e9, 6e6, 6e6),
        compiler_params=pltpu.CompilerParams(vmem_limit_bytes=12 * 1024 * 1024),
    )(scalars, q, kv_own, kv_other, kv_own, kv_other, first, index, *deps)


def attn_back_kernel(
    scalars, q, ko, kp, vo, vp, do, o, lse, first, index, dq_out, dko, dkp, dvo, dvp, kscr, vscr, dk, dv
):
    place_keys(scalars, kscr, ko, kp)
    place_keys(scalars, vscr, vo, vp)
    for j, keys in ((1, 1024), (0, 512)):
        lo = j * 256
        ok = allowed(first[...], index[...], lo, keys)
        dkt, dvt = None, None
        for h in range(3):
            rows = slice(h * HDIM, (h + 1) * HDIM)
            qh, doh = q[rows, lo : lo + 256], do[rows, lo : lo + 256]
            delta = jnp.sum(
                doh.astype(F32) * o[rows, lo : lo + 256].astype(F32), axis=0, keepdims=True
            )
            s = tn(kscr[:, :keys], qh)
            p = jnp.exp(jnp.where(ok, s - lse[0, h : h + 1, lo : lo + 256], NEG))
            dp = tn(vscr[:, :keys], doh)
            ds = (p * (dp - delta)).astype(BF)
            dq_out[rows, lo : lo + 256] = (nn(kscr[:, :keys], ds) * 0.125).astype(BF)
            a, b = nt(qh, ds), nt(doh, p.astype(BF))
            dkt = a if dkt is None else dkt + a
            dvt = b if dvt is None else dvt + b
        if j == 1:
            dk[...] = dkt
            dv[...] = dvt
        else:
            dk[:, :512] += dkt
            dv[:, :512] += dvt
    for j in range(2):
        lo = j * 256
        own = pl.ds(pl.multiple_of(scalars[OWN + j] * 256, 256), 256)
        other = pl.ds(pl.multiple_of(scalars[PAIR + j] * 256, 256), 256)
        dko[:, lo : lo + 256] = dk[:, own].astype(BF)
        dkp[:, lo : lo + 256] = dk[:, other].astype(BF)
        dvo[:, lo : lo + 256] = dv[:, own].astype(BF)
        dvp[:, lo : lo + 256] = dv[:, other].astype(BF)


def attention_back(scalars, q, kv_own, kv_other, do, o, lse, first, index, deps):
    return pl.pallas_call(
        skip(attn_back_kernel, 11, len(deps)),
        out_shape=[sds((D, TOK), BF)] + [sds((KVD, TOK), BF)] * 4,
        grid=(KVH,),
        in_specs=[
            SMEM,
            group_spec(192),
            group_spec(HDIM),
            group_spec(HDIM),
            value_spec(),
            value_spec(),
            group_spec(192),
            group_spec(192),
            pl.BlockSpec((1, 8, TOK), lambda g: (g, 0, 0)),
            row_spec(),
            row_spec(),
        ]
        + [ANY] * len(deps),
        out_specs=[group_spec(192)] + [group_spec(HDIM)] * 4,
        scratch_shapes=[
            pltpu.VMEM((HDIM, LEN), BF),
            pltpu.VMEM((HDIM, LEN), BF),
            pltpu.VMEM((HDIM, LEN), F32),
            pltpu.VMEM((HDIM, LEN), F32),
        ],
        cost_estimate=cost(30e9, 10e6, 6e6),
        compiler_params=pltpu.CompilerParams(vmem_limit_bytes=16 * 1024 * 1024),
    )(scalars, q, kv_own, kv_other, kv_own, kv_other, do, o, lse, first, index, *deps)


def gain_of(scalars, scr, gains, column):
    gains = by_core(scalars, rows_of(*gains[:2]), rows_of(*gains[2:]))[0]
    return from_slots(scalars, A, scr, gains.astype(F32))[:, column : column + 1]


def post_kernel(
    scalars, o, ho, oo, x, g0, g1, g2, g3, x1_out, oa_out, ob_out, h2_out, h2_send, scr
):
    of = o[...].astype(F32)
    wo0, wo1 = by_core(scalars, ho[...], oo[...])
    oa = to_slots(scalars, A, scr, of).astype(BF)
    ob = to_slots(scalars, B, scr, of).astype(BF)
    oa_out[...] = oa
    ob_out[...] = ob
    x1 = x[...].astype(F32) + jnp.concatenate([tn(wo0, oa), tn(wo1, ob)[:448]], axis=0)
    x1_out[...] = x1
    r2 = lax.rsqrt(jnp.mean(x1 * x1, axis=0, keepdims=True) + EPS)
    h2 = x1 * r2 * gain_of(scalars, scr, (g0, g1, g2, g3), 1)
    h2_out[...] = to_slots(scalars, MINE, scr, h2).astype(BF)
    h2_send[...] = to_slots(scalars, OTHER, scr, h2).astype(BF)


HID = 640


def ffn_kernel(more, scalars, h2o, h2p, go, gp, w0, w1, d0, d1, *refs):
    before, refs = refs[: 4 * more], refs[4 * more :]
    out_o, out_p, dh_o, dh_p, grad_w, grad_d, wd, gd = refs

    def rows_at(table, k):
        return pl.ds(pl.multiple_of(scalars[table + k] * 80, 16), 80)

    for k in range(8):
        wd[rows_at(D_OF, k), :] = (d0, d1)[k // 4][k % 4]
    w, wdv = rows_of(w0, w1), wd[...]
    h2 = jnp.concatenate([h2o[...], h2p[...]], axis=1)
    g = jnp.concatenate([go[...], gp[...]], axis=1)
    both = tn(w, h2)
    gate, up = both[:HID], both[HID:]
    dhid = nn(wdv, g)
    sig = 1.0 / (1.0 + jnp.exp(-gate))
    silu = gate * sig
    hid = (silu * up).astype(BF)
    dgt = (dhid * up * (sig * (1.0 + gate * (1.0 - sig)))).astype(BF)
    dboth = jnp.concatenate([dgt, (dhid * silu).astype(BF)], axis=0)
    out, dh = tn(wdv, hid), nn(w, dboth)
    if more:
        out = out + jnp.concatenate([before[0][...], before[1][...]], axis=1).astype(F32)
        dh = dh + jnp.concatenate([before[2][...], before[3][...]], axis=1).astype(F32)
    for value, own, other in ((out, out_o, out_p), (dh, dh_o, dh_p)):
        own[...] = value[:, :TOK].astype(own.dtype)
        other[...] = value[:, TOK:].astype(other.dtype)
    grad_w[...] = nt(h2, dboth).astype(BF)
    gd[...] = nt(hid, g).astype(BF)
    for k in range(8):
        grad_d[k] = gd[rows_at(G_OF, k), :]


def ffn(scalars, h2, g, weights, before=(), deps=()):
    return call(
        functools.partial(ffn_kernel, bool(before)),
        [sds((D, TOK), BF)] * 4
        + [sds((D, UP), BF), sds((8, 80, D), BF)],
        [scalars, *h2, *g, *weights, *before],
        2 * 9 * 1024 * D * HID,
        [pltpu.VMEM((HID, D), BF), pltpu.VMEM((HID, D), BF)],
        deps=deps,
        room=15,
    )


def norm_back(dh, source, inv, gain):
    scaled = dh * gain
    total = jnp.sum(scaled * source, axis=0, keepdims=True)
    grad_gain = jnp.sum(dh * source * inv, axis=1, keepdims=True)
    return inv * scaled - source * (inv * inv * inv * total * (1.0 / D)), grad_gain


def mid_kernel(
    scalars, dho, dhr, x1, g, g0, g1, g2, g3, oa, ob, ho, oo,
    dx_out, do_out, keep, give, gg_out, scr,
):
    wo0, wo1 = by_core(scalars, ho[...], oo[...])
    x1v = x1[...]
    r2 = lax.rsqrt(jnp.mean(x1v * x1v, axis=0, keepdims=True) + EPS)
    dh = from_slots(scalars, MINE, scr, dho[...].astype(F32))
    dh = dh + from_slots(scalars, OTHER, scr, dhr[...].astype(F32))
    back, grad_gain = norm_back(dh, x1v, r2, gain_of(scalars, scr, (g0, g1, g2, g3), 1))
    gg_out[...] = jnp.broadcast_to(grad_gain, (D, 128))
    dx = g[...].astype(F32) + back
    dx_out[...] = dx
    low = jnp.concatenate([dx.astype(BF), jnp.zeros((64, TOK), BF)], axis=0)
    gw0 = nt(oa[...], low[:512]).astype(BF)
    gw1 = nt(ob[...], low[512:]).astype(BF)
    keep[...], give[...] = by_core(scalars, gw0, gw1)
    do = from_slots(scalars, A, scr, nn(wo0, low[:512]))
    do_out[...] = (do + from_slots(scalars, B, scr, nn(wo1, low[512:]))).astype(BF)


def out_kernel(scalars, x1, own, got, wo, wo_got, out, wo_keep, wo_give):
    store_chunks(scalars, out, (x1[...] + own[...].astype(F32) + got[...].astype(F32)).astype(BF))
    total = (wo[...].astype(F32) + wo_got[...].astype(F32)).astype(BF)
    wo_keep[...], wo_give[...] = total[:4], total[4:]


def gain1_of(scalars, scr, wa):
    return from_slots(scalars, A, scr, wa[:, 768:896].astype(F32))[:, 0:1]


def last_kernel(scalars, dq, dko, dvo, dkv, cos, sin, ha, hb, qkv, keep, give):
    cosine, sine = cos[...], -sin[...]
    dqp = rope(dq[...].astype(F32), cosine, sine).astype(BF)
    dkp = rope(dko[...].astype(F32) + dkv[:KVD].astype(F32), cosine, sine).astype(BF)
    dvb = (dvo[...].astype(F32) + dkv[KVD:].astype(F32)).astype(BF)
    rest = jnp.concatenate([dqp[768:], dkp, dvb, jnp.zeros((64, TOK), BF)], axis=0)
    qkv[:768] = dqp[:768]
    qkv[768:] = rest
    gwb = nt(hb[...], rest).astype(BF)
    gwa = jnp.concatenate([nt(ha[...], dqp[:768]), jnp.zeros((D, 128), F32)], axis=1).astype(BF)
    keep[...], give[...] = by_core(scalars, gwa, gwb)


def input_kernel(scalars, qkv, x, dx1, h0, h1, o0, o1, gain2, chunks, gains, scr):
    wa, wb = by_core(scalars, rows_of(h0, h1), rows_of(o0, o1))
    dh = from_slots(scalars, A, scr, nn(wa[:, :768], qkv[:768]))
    dh = dh + from_slots(scalars, B, scr, nn(wb, qkv[768:]))
    xv = x[...].astype(F32)
    r1 = lax.rsqrt(jnp.mean(xv * xv, axis=0, keepdims=True) + EPS)
    back, gain1 = norm_back(dh, xv, r1, gain1_of(scalars, scr, wa))
    store_chunks(scalars, chunks, (dx1[...] + back).astype(BF))
    lane = lax.broadcasted_iota(jnp.int32, (D, 128), 1) - scalars[CORE] * 64
    value = jnp.where(lane == 0, gain1, jnp.where(lane == 1, gain2[...], 0.0))
    gains[...] = to_slots(scalars, MINE, scr, value).astype(BF)


def sum_kernel(scalars, keep, got, gains, gu, gu_got, d, d_got, *outs):
    total = keep[...].astype(F32) + got[...].astype(F32)
    last = total[:, :, 768:] + gains[...].astype(F32)
    outs[0][:, :, :768] = total[:4, :, :768].astype(BF)
    outs[0][:, :, 768:] = last[:4].astype(BF)
    outs[1][:, :, :768] = total[4:, :, :768].astype(BF)
    outs[1][:, :, 768:] = last[4:].astype(BF)
    outs[2][...] = (gu[...].astype(F32) + gu_got[...].astype(F32)).astype(BF)
    value = (d[...].astype(F32) + d_got[...].astype(F32)).astype(BF)
    outs[3][...], outs[4][...] = value[:1], value[1:]


def grads_kernel(groups, scalars, mine, other, gate, up, down):
    pieces = by_core(scalars, mine[...], other[...])
    parts = []
    for c in range(2):
        for half in range(2):
            group = groups[2 * c + 1 - half]
            rows = [pieces[c][d // 2, :32] for d in group]
            parts.append(jnp.concatenate(rows, axis=0)[:ROWS])
            rows = [pieces[c][d // 2, 32:, :D].astype(F32) for d in group]
            at = 160 * c + 80 * half
            down[at : at + 80, :] = jnp.concatenate(rows, axis=0)[:80]
    for lo, ref in ((0, gate), (HID, up)):
        blocks = [p[:, lo + 80 * s : lo + 80 * (s + 1)] for s in range(8) for p in parts]
        ref[...] = jnp.concatenate(blocks, axis=1).astype(F32)


def attn_grads_kernel(scalars, mine, other, query, key, value, output, gains):
    a, b = by_core(scalars, mine[...].astype(F32), other[...].astype(F32))
    a = a.reshape(128, a.shape[2])[:ROWS]
    b = b.reshape(128, b.shape[2])[:ROWS]
    query[:, :768] = a[:, :768]
    query[:, 768:] = b[:, :192]
    key[...] = b[:, 192:512].T
    value[...] = b[:, 512:832].T
    output[:, :OUT] = a[:, WIDTH:]
    output[:, OUT:] = b[:, WIDTH:1344]
    gains[...] = a[:, 768:896] + jnp.concatenate([b[:, 832:896], b[:, 832:896]], axis=1)


def body(
    layer_input,
    segments,
    w_query,
    w_key,
    w_value,
    w_output,
    w_gate,
    w_up,
    w_down,
    gain_attn,
    gain_ffn,
    cotangent,
):
    dp, fs = lax.axis_index("dp"), lax.axis_index("fsdp")
    core, yhi, z = dp % 2, fs // 4, fs % 4
    first_core = core == 0
    scalars = lax.dynamic_index_in_dim(jnp.asarray(scalar_table()), dp * 8 + fs, 0, False)
    own_blocks = scalars[OWN : OWN + 2]

    gains = jnp.pad(jnp.stack([gain_attn, gain_ffn], axis=1), ((0, 0), (0, 126)))
    part = call(
        prep_kernel, [sds((ROWS, WIDTH), BF)], [scalars, w_query, w_key.T, w_value.T, gains], 0
    )[0][None]
    chunks = pick(scalars, layer_input, (part,))
    x_got = [send(chunks[r], RELAY[r]) for r in range(4)]
    two = join(scalars, part, send(part, STEPS[0]), (x_got[0], x_got[3]))
    held0, gu, down = call(
        prep_ffn_kernel,
        [sds((4, ROWS, WIDTH), BF), sds((1, ROWS, UP + OUT), BF), sds((1, 80, D), BF)],
        [scalars, two, send(two, STEPS[1]), w_gate, w_up, w_down, w_output],
        0,
        deps=x_got[1:3],
    )
    x = assemble(scalars, x_got, (held0,))
    held1 = send(held0, STEPS[2])
    gu_got, down_got = send(gu, STEPS[0]), send(down, D_STEPS[0])
    other0 = send(held0, CC)
    other1 = send(held1, CC)
    chunks = pick(scalars, cotangent, (held0,))
    g_got = [send(chunks[r], RELAY[r]) for r in range(4)]
    gu, down = grow(scalars, gu, gu_got, down, down_got, False, (held1, g_got[0]))
    gu_got, down_got = send(gu, STEPS[1]), send(down, D_STEPS[1])
    weights = [a.reshape(D // 2, WIDTH) for a in (held0, held1, other0, other1)]

    seg = send(lax.dynamic_index_in_dim(segments, z, 0, False), SEGMENTS)
    index = (own_blocks[:, None] * 256 + jnp.arange(256, dtype=jnp.int32)[None, :]).reshape(TOK)
    seg_own = jnp.concatenate(
        [lax.dynamic_slice_in_dim(seg, own_blocks[j] * 256, 256) for j in range(2)]
    )
    first = jnp.sum((seg[:, None] < seg_own[None, :]).astype(jnp.int32), axis=0)
    pos = (index - first).astype(F32)
    freq = THETA ** (-(jnp.arange(32, dtype=F32) * 2.0) / HDIM)
    angle = freq[:, None] * pos[None, :]
    cosine, sine = jnp.cos(angle), jnp.sin(angle)
    first, index = first[None, :], index[None, :]

    q, kv, ha, hb = call(
        pre_kernel,
        [sds((D, TOK), BF), sds((2 * KVD, TOK), BF), sds((D, TOK), BF), sds((D, TOK), BF)],
        [scalars, x, *weights, cosine, sine],
        2 * TOK * D * 1664,
        [pltpu.VMEM((D, TOK), F32)],
        deps=(gu,),
    )
    kv_other = send(kv, CC)
    gu0, down0, up0 = grow(
        scalars, gu, gu_got, down, down_got, True, (kv,)
    )
    gu1, down1 = send(gu0, STEPS[2]), send(down0, D_STEPS[2])
    up0_other, down0_other = send(up0, DUP_X), send(down0, DUP_X)
    o, lse = attention(scalars, q, kv, kv_other, first, index, (gu0,))
    up1, wo_held = call(
        part_kernel,
        [sds((4, ROWS, UP), BF), sds((8, ROWS, OUT), BF)],
        [scalars, gu0, gu1],
        0,
        deps=(o, up0_other, down0_other, down1, g_got[3]),
    )
    wo_held = wo_held.reshape(D, OUT)
    wo_other = send(wo_held, CC)
    up1_other, down1_other = send(up1, DUP_X), send(down1, DUP_X)

    x1, oa, ob, h2, h2_send = call(
        post_kernel,
        [sds((D, TOK), F32)] + [sds((D, TOK), BF)] * 4,
        [scalars, o, wo_held, wo_other, x, *weights],
        2 * TOK * D * 1024,
        [pltpu.VMEM((D, TOK), F32)],
        deps=g_got[1:3],
        specs=[SMEM] + [VMEM] * 4 + [GAIN_SPEC] * 4,
    )
    h2_other = send(h2_send, CC)
    g = assemble(scalars, g_got, (h2,))
    g_other = send(g, CC)
    up0, up1, up0_other, up1_other = (
        a.reshape(D // 2, UP) for a in (up0, up1, up0_other, up1_other)
    )
    h2, g = (h2, h2_other), (g, g_other)
    *before, gu_give, d_give = ffn(scalars, h2, g, (up0, up1, down0, down1))
    gu_got = send(gu_give.reshape(8, ROWS, UP), DUP_X)
    out_own, out_part, dh_own, dh_part, gu_keep, d_keep = ffn(
        scalars, h2, g, (up0_other, up1_other, down0_other, down1_other), before
    )
    d_got = send(touch(d_give, (dh_part,)), DUP_X)
    gu_keep = gu_keep.reshape(8, ROWS, UP)
    g = g[0]
    dh_got = send(dh_part, CC)
    out_got = send(out_part, CC)
    dx1, do, wo_keep, wo_give, gg2 = call(
        mid_kernel,
        [
            sds((D, TOK), F32),
            sds((D, TOK), BF),
            sds((D, 512), BF),
            sds((D, 512), BF),
            sds((D, 128), F32),
        ],
        [scalars, dh_own, dh_got, x1, g, *weights, oa, ob, wo_held, wo_other],
        4 * TOK * D * 1024,
        [pltpu.VMEM((D, TOK), F32)],
        room=9,
        specs=[SMEM] + [VMEM] * 4 + [GAIN_SPEC] * 4 + [VMEM] * 4,
    )
    wo_got = send(wo_give, CC)
    gu_keep, gu_give = add(scalars, [[(gu_keep, gu_got)]], (do,))
    gu_got = send(gu_give, STEPS[2])
    out, wo_keep, wo_give = call(
        out_kernel,
        [sds((4, D, 128), BF)] + [sds((4, ROWS, OUT), BF)] * 2,
        [scalars, x1, out_own, out_got]
        + [a.reshape(8, ROWS, OUT) for a in (wo_keep, wo_got)],
        0,
        deps=(gu_keep,),
    )
    wo_got = send(wo_give, STEPS[2])

    def from_chip(chunks):
        return [send(chunks[r], RELAY_BACK[r]) for r in range(4)]

    out_got = from_chip(out)
    dq, dko, dkp, dvo, dvp = attention_back(
        scalars, q, kv, kv_other, do, o, lse, first, index, (out,)
    )
    dkv = send(jnp.concatenate([dkp, dvp], axis=0), CC)
    gu_keep, gu_give, d_keep, d_give = add(
        scalars,
        [[(gu_keep, gu_got), (wo_keep, wo_got)], [(d_keep, d_got)]],
        (dq, out_got[0], out_got[2]),
    )
    gu_got, d_got = send(gu_give, STEPS[1]), send(d_give, D_BACK[2])
    qkv, at_keep, at_give = call(
        last_kernel,
        [sds((1664, TOK), BF), sds((D, WIDTH), BF), sds((D, WIDTH), BF)],
        [scalars, dq, dko, dvo, dkv, cosine, sine, ha, hb],
        2 * TOK * D * 1664,
        deps=(gu_keep,),
    )
    gu_keep, gu_give, d_keep, d_give = add(
        scalars, [[(gu_keep, gu_got)], [(d_keep, d_got)]], (at_keep, out_got[3])
    )
    gu_got, d_got = send(gu_give, STEPS[0]), send(d_give, D_BACK[1])
    at_keep, at_give = (a.reshape(8, ROWS, WIDTH) for a in (at_keep, at_give))
    at_got = send(touch(at_give, (gu_keep,)), CC)
    gin, gains = call(
        input_kernel,
        [sds((4, D, 128), BF), sds((D, 128), BF)],
        [scalars, qkv, x, dx1, *weights, gg2],
        2 * TOK * D * 1664,
        [pltpu.VMEM((D, TOK), F32)],
        room=9,
        deps=(gu_keep,),
    )
    at_keep, at_give, grad_gu, d_keep, d_give = call(
        sum_kernel,
        [sds((4, ROWS, WIDTH), BF)] * 2 + [sds((1, ROWS, UP + OUT), BF)] + [sds((1, 80, D), BF)] * 2,
        [scalars, at_keep, at_got, gains.reshape(8, ROWS, 128), gu_keep, gu_got, d_keep, d_got],
        0,
        deps=(out_got[1],),
    )
    at_got, d_got = send(at_give, STEPS[2]), send(d_give, D_BACK[0])
    gin_got = from_chip(gin)
    out_final = finish(scalars, out_got, BF, (at_keep,))
    at_keep, at_give, grad_d = add(
        scalars, [[(at_keep, at_got)], [(d_keep, d_got)]], (gin_got[0], gin_got[2], out_final)
    )
    at_got = send(at_give, STEPS[1])
    at_keep, at_give = add(scalars, [[(at_keep, at_got)]], (gin_got[1], gin_got[3]))
    at_got = send(at_give, STEPS[0])
    grad_gu, grad_d = grad_gu[0], touch(grad_d, (at_keep,))[0]

    def sum_over(value, groups):
        n = len(groups[0])
        parts = value.reshape(n, value.shape[0] // n, value.shape[1])
        got = lax.all_to_all(parts, "dp", 0, 0, axis_index_groups=groups)
        return jnp.sum(got.astype(F32), axis=0).astype(BF)

    at = lambda yl, x, c: (yl * 4 + x) * 2 + c
    x_pairs = (((0, 3), (1, 2)), ((0, 1), (2, 3)))
    gu_groups = [
        [at(yl, x, c) for yl in range(2) for x in pair] for c in range(2) for pair in x_pairs[c]
    ]
    all_groups = [list(range(c, 16, 2)) for c in range(2)]
    joined = jnp.concatenate(
        [
            jnp.pad(grad_gu[:, :UP], ((0, 8), (0, 0))).reshape(4, 32, UP),
            jnp.pad(grad_d, ((0, 16), (0, 320))).reshape(4, 24, UP),
        ],
        axis=1,
    )
    pieces = sum_over(joined.reshape(224, UP), gu_groups)

    (attn,) = add(scalars, [[(at_keep, at_got)]], (pieces,))
    attn = jnp.concatenate([attn[0], grad_gu[:, UP:]], axis=1)
    attn = jnp.pad(attn, ((0, 8), (0, 0))).reshape(8, 16, WIDTH + OUT)
    pieces = jnp.pad(pieces, ((0, 0), (0, WIDTH + OUT - UP)))
    both = jnp.concatenate([jnp.broadcast_to(pieces[None], (8, *pieces.shape)), attn], axis=1)
    both = lax.all_to_all(both, "dp", 0, 0, axis_index_groups=all_groups)
    attn = jnp.sum(both[:, 56:].astype(F32), axis=0).astype(BF)
    gin_final = finish(scalars, gin_got, F32, (attn,))
    mine = both[:, :56, :UP]
    other = send(mine, CC)
    gate, up, down = call(
        functools.partial(grads_kernel, gu_groups),
        [sds((ROWS, 2560), F32), sds((ROWS, 2560), F32), sds((320, D), F32)],
        [scalars, mine, other],
        0,
    )
    mine = lax.all_to_all(
        jnp.broadcast_to(attn[None], (8, *attn.shape)), "dp", 0, 0, axis_index_groups=all_groups
    )
    other = send(mine, CC)
    query, key, value, output, gains = call(
        attn_grads_kernel,
        [
            sds((ROWS, D), F32),
            sds((KVD, ROWS), F32),
            sds((KVD, ROWS), F32),
            sds((ROWS, D), F32),
            sds((ROWS, 128), F32),
        ],
        [scalars, mine, other],
        0,
    )
    out_final = jnp.swapaxes(out_final, 1, 2)
    gin_final = jnp.swapaxes(gin_final, 1, 2)

    return (
        out_final,
        gin_final,
        query,
        key.T,
        value.T,
        output,
        gate,
        up,
        down,
        gains[:, 0],
        gains[:, 1],
    )


def solution(mesh):
    rows = P("fsdp", None)
    in_specs = (
        (P("dp", "fsdp", None), P("dp", None))
        + (rows,) * 7
        + (P("fsdp"), P("fsdp"), P("dp", "fsdp", None))
    )
    out_specs = (P("dp", "fsdp", None),) * 2 + (rows,) * 7 + (P("fsdp"), P("fsdp"))
    return jax.shard_map(body, mesh=mesh, in_specs=in_specs, out_specs=out_specs, check_vma=False)
```

```python
import functools

import jax
import jax.numpy as jnp
import numpy as np
from jax import lax
from jax.experimental import pallas as pl
from jax.experimental.pallas import tpu as pltpu
from jax.sharding import PartitionSpec as P

D = 960
H = 15
KVH = 5
HDIM = 64
FF = 2560
KVD = 320
LEN = 1024
EPS = 1e-05
THETA = 100000.0
TOK = 512
ROWS = 120
NEG = -1e30
BF = jnp.bfloat16
F32 = jnp.float32
AXES = ("dp", "fsdp")


def coords(i):
    dp, fs = divmod(i, 8)
    ylo, rest = divmod(dp, 8)
    x, core = divmod(rest, 2)
    yhi, z = divmod(fs, 4)
    return ylo, x, core, yhi, z


def flat(ylo, x, core, yhi, z):
    return ((ylo * 4 + x) * 2 + core) * 8 + yhi * 4 + z


def perm(fn, keep=lambda *a: True):
    return [(i, flat(*fn(*coords(i)))) for i in range(128) if keep(*coords(i))]


Z1 = perm(lambda yl, x, c, yh, z: (yl, x, c, yh, z ^ 1))
Z2 = perm(lambda yl, x, c, yh, z: (yl, x, c, yh, 3 - z))
Y2 = perm(lambda yl, x, c, yh, z: (1 - yl, x, c, 1 - yh, z))
CC = perm(lambda yl, x, c, yh, z: (yl, x, 1 - c, yh, z))
DUP_X = perm(lambda yl, x, c, yh, z: (yl, 3 - x if c else x ^ 1, c, yh, z))


def dup_x(x, core):
    return x >> 1 if core else (x >> 1) ^ (x & 1)


DIMS = (("z1", "z2", "y2"), ("z2", "y2", "z1"))
FLIP = {
    "z1": lambda yl, x, c, yh, z: (yl, x, c, yh, z ^ 1),
    "z2": lambda yl, x, c, yh, z: (yl, x, c, yh, 3 - z),
    "y2": lambda yl, x, c, yh, z: (1 - yl, x, c, 1 - yh, z),
}
STEPS = [perm(lambda yl, x, c, yh, z, k=k: FLIP[DIMS[c][k]](yl, x, c, yh, z)) for k in range(3)]
D_STEPS = [Y2, Z1, Z2]
D_BACK = [Z2, Y2, Z1]
GRAY = (0, 1, 3, 2)

CORE_OF = (0, 0, 1, 1, 1, 1, 0, 0)
RANK_OF = (0, 1, 0, 1, 2, 3, 2, 3)


AT = (lambda z: z, lambda z: z ^ 1, lambda z: 3 - z, lambda z: (z + 2) % 4)
RELAY = [
    perm(lambda yl, x, c, yh, z, r=r: (1 - yl, x, CORE_OF[yh * 4 + z], c, AT[r](z)))
    for r in range(4)
]
RELAY_BACK = [[(b, a) for a, b in pairs] for pairs in RELAY]
SEGMENTS = perm(lambda yl, x, c, yh, z: (1 - yl, x, yh, c, z))


def send(x, pairs):
    return lax.ppermute(x, AXES, pairs)


def nn(a, b):
    return lax.dot_general(a, b, (((1,), (0,)), ((), ())), preferred_element_type=F32)


def nt(a, b):
    return lax.dot_general(a, b, (((1,), (1,)), ((), ())), preferred_element_type=F32)


def tn(a, b):
    return lax.dot_general(a, b, (((0,), (0,)), ((), ())), preferred_element_type=F32)


def cost(flops, nbytes, trans=0):
    return pl.CostEstimate(flops=int(flops), bytes_accessed=int(nbytes), transcendentals=int(trans))


VMEM = pl.BlockSpec(memory_space=pltpu.VMEM)
SMEM = pl.BlockSpec(memory_space=pltpu.SMEM)
ANY = pl.BlockSpec(memory_space=pl.ANY)


def call(kernel, outs, ins, flops, scratch=(), trans=0, deps=(), specs=None, room=5):
    nbytes = sum(a.size * a.dtype.itemsize for a in ins) + sum(
        a.size * a.dtype.itemsize for a in outs
    )
    limit = int(1.08 * nbytes / 2**20 + room) + 2
    n_in, n_dep = len(ins), len(deps)

    def run(*refs):
        kernel(*refs[:n_in], *refs[n_in + n_dep :])

    return pl.pallas_call(
        run,
        out_shape=outs,
        grid=(1,) if specs else (),
        in_specs=(specs or [SMEM] + [VMEM] * (n_in - 1))
        + [pl.BlockSpec(memory_space=pl.ANY)] * n_dep,
        out_specs=[VMEM] * len(outs),
        scratch_shapes=list(scratch),
        cost_estimate=cost(flops, nbytes, trans),
        compiler_params=pltpu.CompilerParams(vmem_limit_bytes=limit * 1024 * 1024),
    )(*ins, *deps)


def sds(shape, dtype):
    return jax.ShapeDtypeStruct(shape, dtype)


A, B, MINE, OTHER, D_OF, G_OF, SEQ, POS, ROUND, OWN, PAIR, CORE, HALF = (
    0, 8, 16, 24, 32, 40, 48, 52, 56, 60, 62, 64, 65
)


def scalar_table():
    table = np.zeros((128, 66), np.int32)
    for i in range(128):
        yl, x, c, yh, z = coords(i)
        apart = [(s // 4 * 4 + GRAY[s % 4]) ^ (yh * 4 + GRAY[z]) for s in range(8)]
        orders = (apart, [a // 2 + a % 2 * 4 for a in apart])
        slots = [a // 4 + a % 4 * 2 for a in apart]
        back = [a % 2 * 4 + a // 4 * 2 + a // 2 % 2 for a in apart]
        senders = [[h * 4 + AT[r](z) for h in range(2)] for r in range(4)]
        places = [RANK_OF[q] for pair in senders for q in pair if CORE_OF[q] == c]
        table[i] = (
            orders[0]
            + orders[1]
            + orders[c]
            + orders[1 - c]
            + [slots.index(k) for k in range(8)]
            + [back.index(k) for k in range(8)]
            + [AT[r](z) for r in range(4)]
            + places
            + [places.index(k) for k in range(4)]
            + ([1, 2, 0, 3] if c else [0, 3, 1, 2])
            + [c, dup_x(x, c)]
        )
    return table


def to_slots(scalars, base, scratch, value):
    for s in range(8):
        at = pl.multiple_of(scalars[base + s] * ROWS, 8)
        scratch[pl.ds(at, ROWS), : value.shape[1]] = value[s * ROWS : (s + 1) * ROWS]
    return scratch[:, : value.shape[1]]


def from_slots(scalars, base, scratch, value):
    scratch[:, : value.shape[1]] = value
    return jnp.concatenate(
        [
            scratch[pl.ds(pl.multiple_of(scalars[base + s] * ROWS, 8), ROWS), : value.shape[1]]
            for s in range(8)
        ],
        axis=0,
    )


def join_kernel(scalars, a, b, out):
    n = a.shape[0]
    out[:n] = a[...]
    out[n:] = b[...]


def join(scalars, a, b, deps=()):
    shape = (2 * a.shape[0], *a.shape[1:])
    return call(join_kernel, [sds(shape, a.dtype)], [scalars, a, b], 0, deps=deps)[0]


def add_kernel(shape, scalars, *refs):
    outs = list(refs[sum(sum(group) for group in shape) :])
    at = 0
    for group in shape:
        totals = []
        for count in group:
            total = refs[at][...].astype(F32)
            for k in range(1, count):
                total = total + refs[at + k][...].astype(F32)
            at += count
            totals.append(total.astype(BF))
        total = totals[0] if len(totals) == 1 else jnp.concatenate(totals, axis=-1)
        half = total.shape[0] // 2
        if half:
            outs.pop(0)[...] = total[:half]
            outs.pop(0)[...] = total[half:]
        else:
            outs.pop(0)[...] = total


def add(scalars, groups, deps=()):
    outs = []
    for group in groups:
        n = group[0][0].shape[0]
        shape = (*group[0][0].shape[1:-1], sum(terms[0].shape[-1] for terms in group))
        outs += [sds((n // 2, *shape), BF)] * 2 if n > 1 else [sds((n, *shape), BF)]
    return call(
        functools.partial(add_kernel, [[len(terms) for terms in group] for group in groups]),
        outs,
        [scalars, *[a for group in groups for terms in group for a in terms]],
        0,
        deps=deps,
    )


def touch_kernel(value, *refs):
    pass


def touch(value, deps):
    return pl.pallas_call(
        touch_kernel,
        out_shape=sds(value.shape, value.dtype),
        in_specs=[ANY] * (1 + len(deps)),
        out_specs=ANY,
        input_output_aliases={0: 0},
    )(value, *deps)


def pick_kernel(scalars, value, *outs):
    for r, ref in enumerate(outs):
        ref[...] = value[scalars[SEQ + r]]


def pick(scalars, value, deps=()):
    value = jnp.swapaxes(value, 1, 2)
    return call(pick_kernel, [sds((D, 128), BF)] * 4, [scalars, value], 0, deps=deps)


def assemble_kernel(scalars, r0, r1, r2, r3, out):
    for r, ref in enumerate((r0, r1, r2, r3)):
        out[:, pl.ds(pl.multiple_of(scalars[POS + r] * 128, 128), 128)] = ref[...]


def assemble(scalars, got, deps=()):
    return call(assemble_kernel, [sds((D, TOK), BF)], [scalars, *got], 0, deps=deps)[0]


def store_chunks(scalars, out, value):
    for k in range(4):
        out[scalars[ROUND + k]] = value[:, k * 128 : (k + 1) * 128]


def finish_kernel(scalars, r0, r1, r2, r3, out):
    for r, ref in enumerate((r0, r1, r2, r3)):
        out[scalars[SEQ + r]] = ref[...].astype(out.dtype)


def finish(scalars, got, dtype, deps=()):
    return call(finish_kernel, [sds((4, D, 128), dtype)], [scalars, *got], 0, deps=deps)[0]


def rope(value, cosine, sine):
    parts = []
    for h in range(value.shape[0] // HDIM):
        first = value[h * HDIM : h * HDIM + 32]
        second = value[h * HDIM + 32 : (h + 1) * HDIM]
        parts += [first * cosine - second * sine, second * cosine + first * sine]
    return jnp.concatenate(parts, axis=0)


def by_core(scalars, held, other):
    zero = scalars[CORE] == 0
    return jnp.where(zero, held, other), jnp.where(zero, other, held)


def rows_of(first, second):
    return jnp.concatenate([first[...], second[...]], axis=0)


WIDTH = 896
GAIN_SPEC = pl.BlockSpec((D // 2, 128), lambda i: (0, 6))
UP, OUT = 1280, 512


def prep_kernel(scalars, wq, wk, wv, gains, out):
    zero = lax.broadcasted_iota(jnp.int32, (1, 1), 0) + scalars[CORE] == 0
    out[...] = jnp.where(
        zero,
        jnp.concatenate([wq[:, :768], gains[...]], axis=1),
        jnp.concatenate([wq[:, 768:], wk[...].T, wv[...].T, jnp.zeros((ROWS, 64), BF)], axis=1),
    )


def columns_of(w, core, half):
    at = [320 * s + 160 * core + 80 * half for s in range(8)]
    return [w[:, a : a + 80] for a in at]


def prep_ffn_kernel(scalars, two, got, wg, wu, wd, wo, held, gu, down):
    join_kernel(scalars, two, got, held)
    one = lax.broadcasted_iota(jnp.int32, (1, 1), 0)
    zero, first = one + scalars[CORE] == 0, one + scalars[HALF] == 0
    gate, up = wg[...], wu[...]
    options = [
        [
            jnp.concatenate(columns_of(gate, c, h) + columns_of(up, c, h), axis=1)
            for h in range(2)
        ]
        for c in range(2)
    ]
    gu[0, :, :UP] = jnp.where(
        zero,
        jnp.where(first, options[0][0], options[0][1]),
        jnp.where(first, options[1][0], options[1][1]),
    )
    rest = jnp.concatenate([wo[:, OUT:], jnp.zeros((ROWS, 64), BF)], axis=1)
    gu[0, :, UP:] = jnp.where(zero, wo[:, :OUT], rest)
    at = pl.multiple_of(scalars[CORE] * 160 + scalars[HALF] * 80, 16)
    down[0] = wd[pl.ds(at, 80), :]


def grow_kernel(scalars, gu, gu_got, down, down_got, gu_out, down_out, *only):
    n = gu.shape[0]
    gu_out[:n] = gu[...]
    gu_out[n:] = gu_got[...]
    down_out[:n] = down[...]
    down_out[n:] = down_got[...]
    for ref in only:
        ref[:n] = gu[:, :, :UP]
        ref[n:] = gu_got[:, :, :UP]


def grow(scalars, gu, gu_got, down, down_got, last, deps):
    outs = [sds((2 * a.shape[0], *a.shape[1:]), BF) for a in (gu, down)]
    if last:
        outs.append(sds((2 * gu.shape[0], ROWS, UP), BF))
    return call(grow_kernel, outs, [scalars, gu, gu_got, down, down_got], 0, deps=deps)


def part_kernel(scalars, gu0, gu1, up1, wo):
    up1[...] = gu1[:, :, :UP]
    wo[:4] = gu0[:, :, UP:]
    wo[4:] = gu1[:, :, UP:]


def pre_kernel(scalars, x, h0, h1, o0, o1, cos, sin, q_out, kv_out, ha_out, hb_out, scr):
    wa, wb = by_core(scalars, rows_of(h0, h1), rows_of(o0, o1))
    xv = x[...].astype(F32)
    r1 = lax.rsqrt(jnp.mean(xv * xv, axis=0, keepdims=True) + EPS)
    ha = (to_slots(scalars, A, scr, xv * r1) * wa[:, 768:769].astype(F32)).astype(BF)
    hb = to_slots(scalars, B, scr, from_slots(scalars, A, scr, ha.astype(F32))).astype(BF)
    ha_out[...] = ha
    hb_out[...] = hb
    cosine, sine = cos[...], sin[...]
    q0 = rope(tn(wa[:, :768], ha), cosine, sine)
    q_out[0:768, :] = (q0.astype(BF).astype(F32) * 0.125).astype(BF)
    rest = tn(wb, hb)
    q1 = rope(rest[:192], cosine, sine)
    q_out[768:960, :] = (q1.astype(BF).astype(F32) * 0.125).astype(BF)
    kv_out[0:320, :] = rope(rest[192:512], cosine, sine).astype(BF)
    kv_out[320:640, :] = rest[512:832].astype(BF)


def place_keys(scalars, out, own, other):
    for j in range(2):
        lo = j * 256
        out[:, pl.ds(pl.multiple_of(scalars[OWN + j] * 256, 256), 256)] = own[:, lo : lo + 256]
        out[:, pl.ds(pl.multiple_of(scalars[PAIR + j] * 256, 256), 256)] = other[:, lo : lo + 256]


def allowed(first, index, lo, keys):
    key = lax.broadcasted_iota(jnp.int32, (keys, 256), 0)
    return (key >= first[:, lo : lo + 256]) & (key <= index[:, lo : lo + 256])


def attn_kernel(scalars, q, ko, kp, vo, vp, first, index, o_out, lse_out, kscr, vscr):
    place_keys(scalars, kscr, ko, kp)
    place_keys(scalars, vscr, vo, vp)
    for j, keys in enumerate((512, 1024)):
        lo = j * 256
        ok = allowed(first[...], index[...], lo, keys)
        for h in range(3):
            s = tn(kscr[:, :keys], q[h * HDIM : (h + 1) * HDIM, lo : lo + 256])
            s = jnp.where(ok, s, NEG)
            top = jnp.max(s, axis=0, keepdims=True)
            p = jnp.exp(s - top)
            total = jnp.sum(p, axis=0, keepdims=True)
            o = nn(vscr[:, :keys], p.astype(BF)) / total
            o_out[h * HDIM : (h + 1) * HDIM, lo : lo + 256] = o.astype(BF)
            lse_out[0, h : h + 1, lo : lo + 256] = top + jnp.log(total)


def group_spec(rows):
    return pl.BlockSpec((rows, TOK), lambda g, *_: (g, 0))


def value_spec():
    return pl.BlockSpec((HDIM, TOK), lambda g, *_: (KVH + g, 0))


def row_spec():
    return pl.BlockSpec((1, TOK), lambda g, *_: (0, 0))


def skip(kernel, first, count):
    def run(*refs):
        kernel(*refs[:first], *refs[first + count :])

    return run


def attention(scalars, q, kv_own, kv_other, first, index, deps):
    return pl.pallas_call(
        skip(attn_kernel, 8, len(deps)),
        out_shape=[sds((D, TOK), BF), sds((KVH, 8, TOK), F32)],
        grid=(KVH,),
        in_specs=[
            SMEM,
            group_spec(192),
            group_spec(HDIM),
            group_spec(HDIM),
            value_spec(),
            value_spec(),
            row_spec(),
            row_spec(),
        ]
        + [ANY] * len(deps),
        out_specs=[group_spec(192), pl.BlockSpec((1, 8, TOK), lambda g: (g, 0, 0))],
        scratch_shapes=[pltpu.VMEM((HDIM, LEN), BF), pltpu.VMEM((HDIM, LEN), BF)],
        cost_estimate=cost(12e9, 6e6, 6e6),
        compiler_params=pltpu.CompilerParams(vmem_limit_bytes=8 * 1024 * 1024),
    )(scalars, q, kv_own, kv_other, kv_own, kv_other, first, index, *deps)


def attn_back_kernel(
    scalars, q, ko, kp, vo, vp, do, o, lse, first, index, dq_out, dko, dkp, dvo, dvp, kscr, vscr, dk, dv
):
    place_keys(scalars, kscr, ko, kp)
    place_keys(scalars, vscr, vo, vp)
    for j, keys in ((1, 1024), (0, 512)):
        lo = j * 256
        ok = allowed(first[...], index[...], lo, keys)
        dkt, dvt = None, None
        for h in range(3):
            rows = slice(h * HDIM, (h + 1) * HDIM)
            qh, doh = q[rows, lo : lo + 256], do[rows, lo : lo + 256]
            delta = jnp.sum(
                doh.astype(F32) * o[rows, lo : lo + 256].astype(F32), axis=0, keepdims=True
            )
            s = tn(kscr[:, :keys], qh)
            p = jnp.exp(jnp.where(ok, s - lse[0, h : h + 1, lo : lo + 256], NEG))
            dp = tn(vscr[:, :keys], doh)
            ds = (p * (dp - delta)).astype(BF)
            dq_out[rows, lo : lo + 256] = (nn(kscr[:, :keys], ds) * 0.125).astype(BF)
            a, b = nt(qh, ds), nt(doh, p.astype(BF))
            dkt = a if dkt is None else dkt + a
            dvt = b if dvt is None else dvt + b
        if j == 1:
            dk[...] = dkt
            dv[...] = dvt
        else:
            dk[:, :512] += dkt
            dv[:, :512] += dvt
    for j in range(2):
        lo = j * 256
        own = pl.ds(pl.multiple_of(scalars[OWN + j] * 256, 256), 256)
        other = pl.ds(pl.multiple_of(scalars[PAIR + j] * 256, 256), 256)
        dko[:, lo : lo + 256] = dk[:, own].astype(BF)
        dkp[:, lo : lo + 256] = dk[:, other].astype(BF)
        dvo[:, lo : lo + 256] = dv[:, own].astype(BF)
        dvp[:, lo : lo + 256] = dv[:, other].astype(BF)


def attention_back(scalars, q, kv_own, kv_other, do, o, lse, first, index, deps):
    return pl.pallas_call(
        skip(attn_back_kernel, 11, len(deps)),
        out_shape=[sds((D, TOK), BF)] + [sds((KVD, TOK), BF)] * 4,
        grid=(KVH,),
        in_specs=[
            SMEM,
            group_spec(192),
            group_spec(HDIM),
            group_spec(HDIM),
            value_spec(),
            value_spec(),
            group_spec(192),
            group_spec(192),
            pl.BlockSpec((1, 8, TOK), lambda g: (g, 0, 0)),
            row_spec(),
            row_spec(),
        ]
        + [ANY] * len(deps),
        out_specs=[group_spec(192)] + [group_spec(HDIM)] * 4,
        scratch_shapes=[
            pltpu.VMEM((HDIM, LEN), BF),
            pltpu.VMEM((HDIM, LEN), BF),
            pltpu.VMEM((HDIM, LEN), F32),
            pltpu.VMEM((HDIM, LEN), F32),
        ],
        cost_estimate=cost(30e9, 10e6, 6e6),
        compiler_params=pltpu.CompilerParams(vmem_limit_bytes=10 * 1024 * 1024),
    )(scalars, q, kv_own, kv_other, kv_own, kv_other, do, o, lse, first, index, *deps)


def gain_of(scalars, scr, gains, column):
    gains = by_core(scalars, rows_of(*gains[:2]), rows_of(*gains[2:]))[0]
    return from_slots(scalars, A, scr, gains.astype(F32))[:, column : column + 1]


def post_kernel(
    scalars, o, ho, oo, x, g0, g1, g2, g3, x1_out, oa_out, ob_out, h2_out, h2_send, scr
):
    of = o[...].astype(F32)
    wo0, wo1 = by_core(scalars, ho[...], oo[...])
    oa = to_slots(scalars, A, scr, of).astype(BF)
    ob = to_slots(scalars, B, scr, of).astype(BF)
    oa_out[...] = oa
    ob_out[...] = ob
    x1 = x[...].astype(F32) + jnp.concatenate([tn(wo0, oa), tn(wo1, ob)[:448]], axis=0)
    x1_out[...] = x1
    r2 = lax.rsqrt(jnp.mean(x1 * x1, axis=0, keepdims=True) + EPS)
    h2 = x1 * r2 * gain_of(scalars, scr, (g0, g1, g2, g3), 1)
    h2_out[...] = to_slots(scalars, MINE, scr, h2).astype(BF)
    h2_send[...] = to_slots(scalars, OTHER, scr, h2).astype(BF)


HID = 640


def ffn_kernel(more, scalars, h2o, h2p, go, gp, w0, w1, d0, d1, *refs):
    before, refs = refs[: 4 * more], refs[4 * more :]
    out_o, out_p, dh_o, dh_p, grad_w, grad_d, wd, gd = refs

    def rows_at(table, k):
        return pl.ds(pl.multiple_of(scalars[table + k] * 80, 16), 80)

    for k in range(8):
        wd[rows_at(D_OF, k), :] = (d0, d1)[k // 4][k % 4]
    w, wdv = rows_of(w0, w1), wd[...]
    h2 = jnp.concatenate([h2o[...], h2p[...]], axis=1)
    g = jnp.concatenate([go[...], gp[...]], axis=1)
    both = tn(w, h2)
    gate, up = both[:HID], both[HID:]
    dhid = nn(wdv, g)
    sig = 1.0 / (1.0 + jnp.exp(-gate))
    silu = gate * sig
    hid = (silu * up).astype(BF)
    dgt = (dhid * up * (sig * (1.0 + gate * (1.0 - sig)))).astype(BF)
    dboth = jnp.concatenate([dgt, (dhid * silu).astype(BF)], axis=0)
    out, dh = tn(wdv, hid), nn(w, dboth)
    if more:
        out = out + jnp.concatenate([before[0][...], before[1][...]], axis=1).astype(F32)
        dh = dh + jnp.concatenate([before[2][...], before[3][...]], axis=1).astype(F32)
    for value, own, other in ((out, out_o, out_p), (dh, dh_o, dh_p)):
        own[...] = value[:, :TOK].astype(own.dtype)
        other[...] = value[:, TOK:].astype(other.dtype)
    grad_w[...] = nt(h2, dboth).astype(BF)
    gd[...] = nt(hid, g).astype(BF)
    for k in range(8):
        grad_d[k] = gd[rows_at(G_OF, k), :]


def ffn(scalars, h2, g, weights, before=(), deps=()):
    return call(
        functools.partial(ffn_kernel, bool(before)),
        [sds((D, TOK), BF)] * 4
        + [sds((D, UP), BF), sds((8, 80, D), BF)],
        [scalars, *h2, *g, *weights, *before],
        2 * 9 * 1024 * D * HID,
        [pltpu.VMEM((HID, D), BF), pltpu.VMEM((HID, D), BF)],
        deps=deps,
        room=14,
    )


def norm_back(dh, source, inv, gain):
    scaled = dh * gain
    total = jnp.sum(scaled * source, axis=0, keepdims=True)
    grad_gain = jnp.sum(dh * source * inv, axis=1, keepdims=True)
    return inv * scaled - source * (inv * inv * inv * total * (1.0 / D)), grad_gain


def mid_kernel(
    scalars, dho, dhr, x1, g, g0, g1, g2, g3, oa, ob, ho, oo,
    dx_out, do_out, keep, give, gg_out, scr,
):
    wo0, wo1 = by_core(scalars, ho[...], oo[...])
    x1v = x1[...]
    r2 = lax.rsqrt(jnp.mean(x1v * x1v, axis=0, keepdims=True) + EPS)
    dh = from_slots(scalars, MINE, scr, dho[...].astype(F32))
    dh = dh + from_slots(scalars, OTHER, scr, dhr[...].astype(F32))
    back, grad_gain = norm_back(dh, x1v, r2, gain_of(scalars, scr, (g0, g1, g2, g3), 1))
    gg_out[...] = jnp.broadcast_to(grad_gain, (D, 128))
    dx = g[...].astype(F32) + back
    dx_out[...] = dx
    low = jnp.concatenate([dx.astype(BF), jnp.zeros((64, TOK), BF)], axis=0)
    gw0 = nt(oa[...], low[:512]).astype(BF)
    gw1 = nt(ob[...], low[512:]).astype(BF)
    keep[...], give[...] = by_core(scalars, gw0, gw1)
    do = from_slots(scalars, A, scr, nn(wo0, low[:512]))
    do_out[...] = (do + from_slots(scalars, B, scr, nn(wo1, low[512:]))).astype(BF)


def out_kernel(scalars, x1, own, got, wo, wo_got, out, wo_keep, wo_give):
    store_chunks(scalars, out, (x1[...] + own[...].astype(F32) + got[...].astype(F32)).astype(BF))
    total = (wo[...].astype(F32) + wo_got[...].astype(F32)).astype(BF)
    wo_keep[...], wo_give[...] = total[:4], total[4:]


def gain1_of(scalars, scr, wa):
    return from_slots(scalars, A, scr, wa[:, 768:896].astype(F32))[:, 0:1]


def last_kernel(scalars, dq, dko, dvo, dkv, cos, sin, ha, hb, qkv, keep, give):
    cosine, sine = cos[...], -sin[...]
    dqp = rope(dq[...].astype(F32), cosine, sine).astype(BF)
    dkp = rope(dko[...].astype(F32) + dkv[:KVD].astype(F32), cosine, sine).astype(BF)
    dvb = (dvo[...].astype(F32) + dkv[KVD:].astype(F32)).astype(BF)
    rest = jnp.concatenate([dqp[768:], dkp, dvb, jnp.zeros((64, TOK), BF)], axis=0)
    qkv[:768] = dqp[:768]
    qkv[768:] = rest
    gwb = nt(hb[...], rest).astype(BF)
    gwa = jnp.concatenate([nt(ha[...], dqp[:768]), jnp.zeros((D, 128), F32)], axis=1).astype(BF)
    keep[...], give[...] = by_core(scalars, gwa, gwb)


def input_kernel(scalars, qkv, x, dx1, h0, h1, o0, o1, gain2, chunks, gains, scr):
    wa, wb = by_core(scalars, rows_of(h0, h1), rows_of(o0, o1))
    dh = from_slots(scalars, A, scr, nn(wa[:, :768], qkv[:768]))
    dh = dh + from_slots(scalars, B, scr, nn(wb, qkv[768:]))
    xv = x[...].astype(F32)
    r1 = lax.rsqrt(jnp.mean(xv * xv, axis=0, keepdims=True) + EPS)
    back, gain1 = norm_back(dh, xv, r1, gain1_of(scalars, scr, wa))
    store_chunks(scalars, chunks, (dx1[...] + back).astype(BF))
    lane = lax.broadcasted_iota(jnp.int32, (D, 128), 1) - scalars[CORE] * 64
    value = jnp.where(lane == 0, gain1, jnp.where(lane == 1, gain2[...], 0.0))
    gains[...] = to_slots(scalars, MINE, scr, value).astype(BF)


def sum_kernel(scalars, keep, got, gains, gu, gu_got, d, d_got, *outs):
    total = keep[...].astype(F32) + got[...].astype(F32)
    last = total[:, :, 768:] + gains[...].astype(F32)
    outs[0][:, :, :768] = total[:4, :, :768].astype(BF)
    outs[0][:, :, 768:] = last[:4].astype(BF)
    outs[1][:, :, :768] = total[4:, :, :768].astype(BF)
    outs[1][:, :, 768:] = last[4:].astype(BF)
    outs[2][...] = (gu[...].astype(F32) + gu_got[...].astype(F32)).astype(BF)
    value = (d[...].astype(F32) + d_got[...].astype(F32)).astype(BF)
    outs[3][...], outs[4][...] = value[:1], value[1:]


def grads_kernel(groups, scalars, mine, other, gate, up, down):
    pieces = by_core(scalars, mine[...], other[...])
    parts = []
    for c in range(2):
        for half in range(2):
            group = groups[2 * c + 1 - half]
            rows = [pieces[c][d // 2, :32] for d in group]
            parts.append(jnp.concatenate(rows, axis=0)[:ROWS])
            rows = [pieces[c][d // 2, 32:, :D].astype(F32) for d in group]
            at = 160 * c + 80 * half
            down[at : at + 80, :] = jnp.concatenate(rows, axis=0)[:80]
    for lo, ref in ((0, gate), (HID, up)):
        blocks = [p[:, lo + 80 * s : lo + 80 * (s + 1)] for s in range(8) for p in parts]
        ref[...] = jnp.concatenate(blocks, axis=1).astype(F32)


def attn_grads_kernel(scalars, mine, other, query, key, value, output, gains):
    a, b = by_core(scalars, mine[...].astype(F32), other[...].astype(F32))
    a = a.reshape(128, a.shape[2])[:ROWS]
    b = b.reshape(128, b.shape[2])[:ROWS]
    query[:, :768] = a[:, :768]
    query[:, 768:] = b[:, :192]
    key[...] = b[:, 192:512].T
    value[...] = b[:, 512:832].T
    output[:, :OUT] = a[:, WIDTH:]
    output[:, OUT:] = b[:, WIDTH:1344]
    gains[...] = a[:, 768:896] + jnp.concatenate([b[:, 832:896], b[:, 832:896]], axis=1)


def body(
    layer_input,
    segments,
    w_query,
    w_key,
    w_value,
    w_output,
    w_gate,
    w_up,
    w_down,
    gain_attn,
    gain_ffn,
    cotangent,
):
    dp, fs = lax.axis_index("dp"), lax.axis_index("fsdp")
    core, yhi, z = dp % 2, fs // 4, fs % 4
    first_core = core == 0
    scalars = lax.dynamic_index_in_dim(jnp.asarray(scalar_table()), dp * 8 + fs, 0, False)
    own_blocks = scalars[OWN : OWN + 2]

    gains = jnp.pad(jnp.stack([gain_attn, gain_ffn], axis=1), ((0, 0), (0, 126)))
    part = call(
        prep_kernel, [sds((ROWS, WIDTH), BF)], [scalars, w_query, w_key.T, w_value.T, gains], 0
    )[0][None]
    chunks = pick(scalars, layer_input, (part,))
    x_got = [send(chunks[r], RELAY[r]) for r in range(4)]
    two = join(scalars, part, send(part, STEPS[0]), (x_got[0], x_got[3]))
    held0, gu, down = call(
        prep_ffn_kernel,
        [sds((4, ROWS, WIDTH), BF), sds((1, ROWS, UP + OUT), BF), sds((1, 80, D), BF)],
        [scalars, two, send(two, STEPS[1]), w_gate, w_up, w_down, w_output],
        0,
        deps=x_got[1:3],
    )
    x = assemble(scalars, x_got, (held0,))
    held1 = send(held0, STEPS[2])
    gu_got, down_got = send(gu, STEPS[0]), send(down, D_STEPS[0])
    other0 = send(held0, CC)
    other1 = send(held1, CC)
    chunks = pick(scalars, cotangent, (held0,))
    g_got = [send(chunks[r], RELAY[r]) for r in range(4)]
    gu, down = grow(scalars, gu, gu_got, down, down_got, False, (held1, g_got[0]))
    gu_got, down_got = send(gu, STEPS[1]), send(down, D_STEPS[1])
    weights = [a.reshape(D // 2, WIDTH) for a in (held0, held1, other0, other1)]

    seg = send(lax.dynamic_index_in_dim(segments, z, 0, False), SEGMENTS)
    index = (own_blocks[:, None] * 256 + jnp.arange(256, dtype=jnp.int32)[None, :]).reshape(TOK)
    seg_own = jnp.concatenate(
        [lax.dynamic_slice_in_dim(seg, own_blocks[j] * 256, 256) for j in range(2)]
    )
    first = jnp.sum((seg[:, None] < seg_own[None, :]).astype(jnp.int32), axis=0)
    pos = (index - first).astype(F32)
    freq = THETA ** (-(jnp.arange(32, dtype=F32) * 2.0) / HDIM)
    angle = freq[:, None] * pos[None, :]
    cosine, sine = jnp.cos(angle), jnp.sin(angle)
    first, index = first[None, :], index[None, :]

    q, kv, ha, hb = call(
        pre_kernel,
        [sds((D, TOK), BF), sds((2 * KVD, TOK), BF), sds((D, TOK), BF), sds((D, TOK), BF)],
        [scalars, x, *weights, cosine, sine],
        2 * TOK * D * 1664,
        [pltpu.VMEM((D, TOK), F32)],
        deps=(gu,),
    )
    kv_other = send(kv, CC)
    gu0, down0, up0 = grow(
        scalars, gu, gu_got, down, down_got, True, (kv,)
    )
    gu1, down1 = send(gu0, STEPS[2]), send(down0, D_STEPS[2])
    up0_other, down0_other = send(up0, DUP_X), send(down0, DUP_X)
    o, lse = attention(scalars, q, kv, kv_other, first, index, (gu0,))
    up1, wo_held = call(
        part_kernel,
        [sds((4, ROWS, UP), BF), sds((8, ROWS, OUT), BF)],
        [scalars, gu0, gu1],
        0,
        deps=(o, up0_other, down0_other, down1, g_got[3]),
    )
    wo_held = wo_held.reshape(D, OUT)
    wo_other = send(wo_held, CC)
    up1_other, down1_other = send(up1, DUP_X), send(down1, DUP_X)

    x1, oa, ob, h2, h2_send = call(
        post_kernel,
        [sds((D, TOK), F32)] + [sds((D, TOK), BF)] * 4,
        [scalars, o, wo_held, wo_other, x, *weights],
        2 * TOK * D * 1024,
        [pltpu.VMEM((D, TOK), F32)],
        deps=g_got[1:3],
        specs=[SMEM] + [VMEM] * 4 + [GAIN_SPEC] * 4,
    )
    h2_other = send(h2_send, CC)
    g = assemble(scalars, g_got, (h2,))
    g_other = send(g, CC)
    up0, up1, up0_other, up1_other = (
        a.reshape(D // 2, UP) for a in (up0, up1, up0_other, up1_other)
    )
    h2, g = (h2, h2_other), (g, g_other)
    *before, gu_give, d_give = ffn(scalars, h2, g, (up0, up1, down0, down1))
    gu_got = send(gu_give.reshape(8, ROWS, UP), DUP_X)
    out_own, out_part, dh_own, dh_part, gu_keep, d_keep = ffn(
        scalars, h2, g, (up0_other, up1_other, down0_other, down1_other), before
    )
    d_got = send(touch(d_give, (dh_part,)), DUP_X)
    gu_keep = gu_keep.reshape(8, ROWS, UP)
    g = g[0]
    dh_got = send(dh_part, CC)
    out_got = send(out_part, CC)
    dx1, do, wo_keep, wo_give, gg2 = call(
        mid_kernel,
        [
            sds((D, TOK), F32),
            sds((D, TOK), BF),
            sds((D, 512), BF),
            sds((D, 512), BF),
            sds((D, 128), F32),
        ],
        [scalars, dh_own, dh_got, x1, g, *weights, oa, ob, wo_held, wo_other],
        4 * TOK * D * 1024,
        [pltpu.VMEM((D, TOK), F32)],
        room=9,
        specs=[SMEM] + [VMEM] * 4 + [GAIN_SPEC] * 4 + [VMEM] * 4,
    )
    wo_got = send(wo_give, CC)
    gu_keep, gu_give = add(scalars, [[(gu_keep, gu_got)]], (do,))
    gu_got = send(gu_give, STEPS[2])
    out, wo_keep, wo_give = call(
        out_kernel,
        [sds((4, D, 128), BF)] + [sds((4, ROWS, OUT), BF)] * 2,
        [scalars, x1, out_own, out_got]
        + [a.reshape(8, ROWS, OUT) for a in (wo_keep, wo_got)],
        0,
        deps=(gu_keep,),
    )
    wo_got = send(wo_give, STEPS[2])

    def from_chip(chunks):
        return [send(chunks[r], RELAY_BACK[r]) for r in range(4)]

    out_got = from_chip(out)
    dq, dko, dkp, dvo, dvp = attention_back(
        scalars, q, kv, kv_other, do, o, lse, first, index, (out,)
    )
    dkv = send(jnp.concatenate([dkp, dvp], axis=0), CC)
    gu_keep, gu_give, d_keep, d_give = add(
        scalars,
        [[(gu_keep, gu_got), (wo_keep, wo_got)], [(d_keep, d_got)]],
        (dq, out_got[0], out_got[2]),
    )
    gu_got, d_got = send(gu_give, STEPS[1]), send(d_give, D_BACK[2])
    qkv, at_keep, at_give = call(
        last_kernel,
        [sds((1664, TOK), BF), sds((D, WIDTH), BF), sds((D, WIDTH), BF)],
        [scalars, dq, dko, dvo, dkv, cosine, sine, ha, hb],
        2 * TOK * D * 1664,
        deps=(gu_keep,),
    )
    gu_keep, gu_give, d_keep, d_give = add(
        scalars, [[(gu_keep, gu_got)], [(d_keep, d_got)]], (at_keep, out_got[3])
    )
    gu_got, d_got = send(gu_give, STEPS[0]), send(d_give, D_BACK[1])
    at_keep, at_give = (a.reshape(8, ROWS, WIDTH) for a in (at_keep, at_give))
    at_got = send(touch(at_give, (gu_keep,)), CC)
    gin, gains = call(
        input_kernel,
        [sds((4, D, 128), BF), sds((D, 128), BF)],
        [scalars, qkv, x, dx1, *weights, gg2],
        2 * TOK * D * 1664,
        [pltpu.VMEM((D, TOK), F32)],
        room=9,
        deps=(gu_keep,),
    )
    at_keep, at_give, grad_gu, d_keep, d_give = call(
        sum_kernel,
        [sds((4, ROWS, WIDTH), BF)] * 2 + [sds((1, ROWS, UP + OUT), BF)] + [sds((1, 80, D), BF)] * 2,
        [scalars, at_keep, at_got, gains.reshape(8, ROWS, 128), gu_keep, gu_got, d_keep, d_got],
        0,
        deps=(out_got[1],),
    )
    at_got, d_got = send(at_give, STEPS[2]), send(d_give, D_BACK[0])
    gin_got = from_chip(gin)
    out_final = finish(scalars, out_got, BF, (at_keep,))
    at_keep, at_give, grad_d = add(
        scalars, [[(at_keep, at_got)], [(d_keep, d_got)]], (gin_got[0], gin_got[2], out_final)
    )
    at_got = send(at_give, STEPS[1])
    at_keep, at_give = add(scalars, [[(at_keep, at_got)]], (gin_got[1], gin_got[3]))
    at_got = send(at_give, STEPS[0])
    grad_gu, grad_d = grad_gu[0], touch(grad_d, (at_keep,))[0]

    def sum_over(value, groups):
        n = len(groups[0])
        parts = value.reshape(n, value.shape[0] // n, value.shape[1])
        got = lax.all_to_all(parts, "dp", 0, 0, axis_index_groups=groups)
        return jnp.sum(got.astype(F32), axis=0).astype(BF)

    at = lambda yl, x, c: (yl * 4 + x) * 2 + c
    x_pairs = (((0, 3), (1, 2)), ((0, 1), (2, 3)))
    gu_groups = [
        [at(yl, x, c) for yl in range(2) for x in pair] for c in range(2) for pair in x_pairs[c]
    ]
    all_groups = [list(range(c, 16, 2)) for c in range(2)]
    joined = jnp.concatenate(
        [
            jnp.pad(grad_gu[:, :UP], ((0, 8), (0, 0))).reshape(4, 32, UP),
            jnp.pad(grad_d, ((0, 16), (0, 320))).reshape(4, 24, UP),
        ],
        axis=1,
    )
    pieces = sum_over(joined.reshape(224, UP), gu_groups)

    (attn,) = add(scalars, [[(at_keep, at_got)]], (pieces,))
    attn = jnp.concatenate([attn[0], grad_gu[:, UP:]], axis=1)
    attn = jnp.pad(attn, ((0, 8), (0, 0))).reshape(8, 16, WIDTH + OUT)
    pieces = jnp.pad(pieces, ((0, 0), (0, WIDTH + OUT - UP)))
    both = jnp.concatenate([jnp.broadcast_to(pieces[None], (8, *pieces.shape)), attn], axis=1)
    both = lax.all_to_all(both, "dp", 0, 0, axis_index_groups=all_groups)
    attn = jnp.sum(both[:, 56:].astype(F32), axis=0).astype(BF)
    gin_final = finish(scalars, gin_got, F32, (attn,))
    mine = both[:, :56, :UP]
    other = send(mine, CC)
    gate, up, down = call(
        functools.partial(grads_kernel, gu_groups),
        [sds((ROWS, 2560), F32), sds((ROWS, 2560), F32), sds((320, D), F32)],
        [scalars, mine, other],
        0,
    )
    mine = lax.all_to_all(
        jnp.broadcast_to(attn[None], (8, *attn.shape)), "dp", 0, 0, axis_index_groups=all_groups
    )
    other = send(mine, CC)
    query, key, value, output, gains = call(
        attn_grads_kernel,
        [
            sds((ROWS, D), F32),
            sds((KVD, ROWS), F32),
            sds((KVD, ROWS), F32),
            sds((ROWS, D), F32),
            sds((ROWS, 128), F32),
        ],
        [scalars, mine, other],
        0,
    )
    out_final = jnp.swapaxes(out_final, 1, 2)
    gin_final = jnp.swapaxes(gin_final, 1, 2)

    return (
        out_final,
        gin_final,
        query,
        key.T,
        value.T,
        output,
        gate,
        up,
        down,
        gains[:, 0],
        gains[:, 1],
    )


def solution(mesh):
    rows = P("fsdp", None)
    in_specs = (
        (P("dp", "fsdp", None), P("dp", None))
        + (rows,) * 7
        + (P("fsdp"), P("fsdp"), P("dp", "fsdp", None))
    )
    out_specs = (P("dp", "fsdp", None),) * 2 + (rows,) * 7 + (P("fsdp"), P("fsdp"))
    return jax.shard_map(body, mesh=mesh, in_specs=in_specs, out_specs=out_specs, check_vma=False)
```
